512 devices in a mesh: region: 16 (over y, core), group: 32 (over z, x).
Axes of the slice: x: 4, y: 8, z: 8, core: 2. Of those that a mesh axis runs over, the one named last changes fastest.
Arguments:
- geom: float32 [4, 262144], P(None, ('region', 'group')), as said below
- density: float32 [262144], P(('region', 'group')), may hold values from 0.5 to 4
- velocity: float32 [3, 262144], P(None, ('region', 'group')), may hold values from -3 to 3
- pressure: float32 [262144], P(('region', 'group')), may hold values from 0.5 to 4
- block_live: int32 [1024], P(('region', 'group')), may hold values from 0 to 256, as said below
- pair_list: int32 [7168, 2], P(('region', 'group')), may hold values from -1 to 1023, as said below
Outputs:
- gradients: float32 [15, 262144], P(None, ('region', 'group'))
- rate: float32 [5, 262144], P(None, ('region', 'group'))
The draws below stay inside these ranges and needn't reach their ends.
Inputs may be any that keep to these rules, and one draw needn't show every extreme that they name: `geom`: rows are x, y, z and H. Particles sit one to a site of a cubic lattice of unit spacing, each moved by at most 0.3 along each axis; block g covers a box of 4 x 8 x 8 sites; H lies between 1.6 and 2.4. `block_live`: A block's particle slots below its count are live, the others are padding. `pair_list`: block g lives on device g // 2 (devices in region-major order) in its slot g % 2. Each device's 14 rows hold pairs (a, b) of block ids with a on that device and b equal to a or a block of the same or a neighbouring region; the row (a, b) is present exactly when the row (b, a) is present on b's device; every nonempty block has the row (a, a); no pair appears twice; rows (-1, -1) are padding and follow all other rows of a device.
All inputs are finite; a program needn't handle non-finite values.
Results may differ from the reference program's by a relative error of at most 0.0003.
Values sent between devices are 32-bit elements; how exact they have to be, the bound alone decides.
A program may use at most 64 MiB of HBM per device.

```python
import math
import jax
import jax.numpy as jnp
from jax import lax

BLOCK_X = 4
BLOCK_Y = 8
BLOCK_Z = 8
BLOCK = 256
PAIR_DEV = 14
REGIONS = 16
REGION_BLOCKS = 64
GRID_Y = 8
GRID_Z = 8
NBLK = 1024
NPART = 262144
NPAIR = 7168


def permute_region(region_key):
    return jax.random.permutation(region_key, REGION_BLOCKS)


def block_cells(key):
    region_keys = jax.random.split(jax.random.fold_in(key, 11), REGIONS)
    return jax.vmap(permute_region)(region_keys).astype(jnp.int32)


def block_counts(key):
    key = jax.random.fold_in(key, 23)
    first_key, second_key, third_key = jax.random.split(key, 3)
    center = jax.random.randint(first_key, (), 0, REGIONS)
    region_of = jnp.arange(NBLK) // REGION_BLOCKS
    inside = jnp.abs(region_of - center) <= REGIONS // 8
    empty_flag = jax.random.randint(second_key, (NBLK,), 0, 2) == 0
    partial_count = jax.random.randint(third_key, (NBLK,), BLOCK // 8, BLOCK + 1)
    return jnp.where(inside, BLOCK, jnp.where(empty_flag, 0, partial_count)).astype(jnp.int32)


def draw_geom(key, part):
    block_cell = block_cells(key)
    key = jax.random.fold_in(key, 3)
    jitter_key, radius_key = jax.random.split(key)
    particle = jnp.arange(NPART)
    block_index = particle // BLOCK
    block_slot = particle % BLOCK
    region = block_index // REGION_BLOCKS
    cell_index = block_cell[region, block_index % REGION_BLOCKS]
    cell_y = cell_index // GRID_Z
    cell_z = cell_index % GRID_Z
    site_x = block_slot // (BLOCK_Y * BLOCK_Z)
    site_y = block_slot // BLOCK_Z % BLOCK_Y
    site_z = block_slot % BLOCK_Z
    lattice = jnp.stack([region * BLOCK_X + site_x, cell_y * BLOCK_Y + site_y, cell_z * BLOCK_Z + site_z]).astype(jnp.float32)
    jitter = jax.random.uniform(jitter_key, (3, NPART), jnp.float32, -0.3, 0.3)
    radius = jnp.exp(jax.random.uniform(radius_key, (NPART,), jnp.float32, math.log(1.6), math.log(2.4)))
    return jnp.concatenate([lattice + jitter, radius[None]], axis=0)


def draw_block_live(key, part):
    counts_drawn = block_counts(key)
    return counts_drawn


def draw_pair_list(key, part):
    block_cell = block_cells(key)
    counts_drawn = block_counts(key)
    region_index = jnp.arange(REGIONS)
    placed = jnp.zeros((REGIONS, REGION_BLOCKS), jnp.int32).at[region_index[:, None], block_cell].set((jnp.arange(REGION_BLOCKS)[None, :] + region_index[:, None] * REGION_BLOCKS).astype(jnp.int32))
    block_index = jnp.arange(NBLK)
    region = block_index // REGION_BLOCKS
    cell_index = block_cell[region, block_index % REGION_BLOCKS]
    cell_y = cell_index // GRID_Z
    cell_z = cell_index % GRID_Z
    region_moves = [0, -1, 1, 0, 0, 0, 0]
    y_moves = [0, 0, 0, -1, 1, 0, 0]
    z_moves = [0, 0, 0, 0, 0, -1, 1]
    partners = []
    validity = []
    for direction in range(7):
        other_region = region + region_moves[direction]
        other_y = cell_y + y_moves[direction]
        other_z = cell_z + z_moves[direction]
        exists = (other_region >= 0) & (other_region < REGIONS) & (other_y >= 0) & (other_y < GRID_Y) & (other_z >= 0) & (other_z < GRID_Z)
        clipped_region = jnp.clip(other_region, 0, REGIONS - 1)
        clipped_cell = jnp.clip(other_y, 0, GRID_Y - 1) * GRID_Z + jnp.clip(other_z, 0, GRID_Z - 1)
        partner = placed[clipped_region, clipped_cell]
        valid = exists & (counts_drawn[block_index] > 0) & (counts_drawn[partner] > 0)
        partners.append(partner)
        validity.append(valid)
    partner_rows = jnp.stack(partners, axis=1).reshape(-1, PAIR_DEV)
    valid_rows = jnp.stack(validity, axis=1).reshape(-1, PAIR_DEV)
    owner_rows = jnp.repeat(block_index[:, None], 7, axis=1).reshape(-1, PAIR_DEV).astype(jnp.int32)
    ordering = jnp.argsort(jnp.where(valid_rows, 0, 1).astype(jnp.int32), axis=1, stable=True)
    partner_rows = jnp.take_along_axis(partner_rows, ordering, axis=1)
    owner_rows = jnp.take_along_axis(owner_rows, ordering, axis=1)
    valid_rows = jnp.take_along_axis(valid_rows, ordering, axis=1)
    listed = jnp.stack([jnp.where(valid_rows, owner_rows, -1), jnp.where(valid_rows, partner_rows, -1)], axis=-1)
    return listed.reshape(NPAIR, 2).astype(jnp.int32)


def level_of(own_key, shape, shards, low, high):
    def one(position, shards_of):
        heights = jax.random.uniform(jax.random.fold_in(jax.random.fold_in(own_key, 6), position), (shards_of,), jnp.float32, low / len(shards), high / len(shards))
        return jnp.repeat(jnp.exp(heights), shape[position] // shards_of).reshape((-1,) + (1,) * (len(shape) - position - 1))

    gain = one(*shards[0])
    for cut in shards[1:]:
        gain = gain * one(*cut)
    return gain


def scatter_about(rng, shape, spread, bound, cuts=(), kind=jnp.bfloat16):
    entries = jax.random.normal(rng, shape, jnp.float32) * spread
    if len(cuts) > 0:
        entries = level_of(rng, shape, cuts, -0.22, 0.18) * entries
    return jnp.clip(entries, min=-bound, max=bound).astype(kind)


def setup_inputs(seed: int = 0) -> dict:
    key_of = jax.random.split(jax.random.key(seed), 7)
    return {
        "geom": draw_geom(jax.random.fold_in(key_of[6], 71), 0),
        "density": jnp.clip(jnp.exp(math.log(4.0) - 2.0794415 * jax.random.uniform(key_of[1], (NPART,), jnp.float32) ** level_of(key_of[1], (NPART,), ((0, 512),), -0.2, 0.2)), 0.5, 4.0),
        "velocity": scatter_about(key_of[2], (3, NPART), 0.5, 3.0, ((1, 512),), jnp.float32),
        "pressure": jnp.clip(jnp.exp(math.log(4.0) - 2.0794415 * jax.random.uniform(key_of[3], (NPART,), jnp.float32) ** level_of(key_of[3], (NPART,), ((0, 512),), -0.2, 0.2)), 0.5, 4.0),
        "block_live": draw_block_live(jax.random.fold_in(key_of[6], 71), 0),
        "pair_list": draw_pair_list(jax.random.fold_in(key_of[6], 71), 0),
    }


adiabatic = 5.0 / 3.0
ridge_scale = 0.05

def kernel_weight(scaled_distance):
    remain = jnp.maximum(1.0 - scaled_distance, 0.0)
    square = remain * remain
    return square * square * (1.0 + 4.0 * scaled_distance)

def moment_tile(block_a, block_b):
    offset = block_b[0:3, None, :] - block_a[0:3, :, None]
    distance = jnp.sqrt(lax.optimization_barrier(jnp.sum(offset * offset, axis=0)))
    change = block_b[4:9, None, :] - block_a[4:9, :, None]
    seconds = jnp.stack([offset[0] * offset[0], offset[1] * offset[1], offset[2] * offset[2], offset[0] * offset[1], offset[0] * offset[2], offset[1] * offset[2]])
    firsts = (change[:, None] * offset[None]).reshape((15,) + distance.shape)
    term_rows = jnp.concatenate([jnp.ones((1,) + distance.shape, distance.dtype), seconds, firsts], axis=0)
    weight_a = kernel_weight(distance / block_a[3][:, None]) * block_b[9][None, :]
    return lax.optimization_barrier(jnp.sum(term_rows * weight_a[None], axis=2))

def finish_moments(totals, radius, alive_mask):
    omega_sum = totals[0] + (1.0 - alive_mask)
    scaled = totals[1:] / omega_sum[None]
    diagonal_shift = ridge_scale * radius * radius
    matrix = [scaled[0] + diagonal_shift, scaled[1] + diagonal_shift, scaled[2] + diagonal_shift, scaled[3], scaled[4], scaled[5]]
    cofactor = [matrix[1] * matrix[2] - matrix[5] * matrix[5], matrix[0] * matrix[2] - matrix[4] * matrix[4], matrix[0] * matrix[1] - matrix[3] * matrix[3], matrix[4] * matrix[5] - matrix[3] * matrix[2], matrix[3] * matrix[5] - matrix[4] * matrix[1], matrix[3] * matrix[4] - matrix[0] * matrix[5]]
    determinant = matrix[0] * cofactor[0] + matrix[3] * cofactor[3] + matrix[4] * cofactor[4]
    inverse = jnp.stack(cofactor) / determinant[None]
    moment = scaled[6:21].reshape(5, 3, -1)
    gradient_rows = jnp.stack([inverse[0] * moment[:, 0] + inverse[3] * moment[:, 1] + inverse[4] * moment[:, 2], inverse[3] * moment[:, 0] + inverse[1] * moment[:, 1] + inverse[5] * moment[:, 2], inverse[4] * moment[:, 0] + inverse[5] * moment[:, 1] + inverse[2] * moment[:, 2]], axis=1).reshape(15, -1)
    return jnp.concatenate([inverse, gradient_rows, omega_sum[None]], axis=0)

def riemann_side(state, normal):
    density_value = jnp.exp(state[0])
    pressure_value = jnp.exp(state[4])
    motion = state[1:4]
    normal_speed = lax.optimization_barrier(jnp.sum(motion * normal, axis=0))
    sound_speed = jnp.sqrt(adiabatic * pressure_value / density_value)
    energy = pressure_value / (adiabatic - 1.0) + 0.5 * density_value * lax.optimization_barrier(jnp.sum(motion * motion, axis=0))
    conserved = jnp.concatenate([density_value[None], density_value[None] * motion, energy[None]], axis=0)
    face_flux = jnp.concatenate([(density_value * normal_speed)[None], (density_value * normal_speed)[None] * motion + pressure_value[None] * normal, ((energy + pressure_value) * normal_speed)[None]], axis=0)
    return (density_value, pressure_value, motion, normal_speed, sound_speed, energy, conserved, face_flux)

def star_flux(side_values, wave_speed, middle, normal):
    density_value, pressure_value, motion, normal_speed, sound_speed, energy, conserved, face_flux = side_values
    mass_rate = density_value * (wave_speed - normal_speed)
    factor = mass_rate / (wave_speed - middle)
    star_state = jnp.concatenate([factor[None], factor[None] * (motion + (middle - normal_speed)[None] * normal), (factor * (energy / density_value + (middle - normal_speed) * (middle + pressure_value / mass_rate)))[None]], axis=0)
    return face_flux + wave_speed[None] * (star_state - conserved)

def riemann(left_state, right_state, normal):
    left_side = riemann_side(left_state, normal)
    right_side = riemann_side(right_state, normal)
    speed_left = jnp.minimum(left_side[3] - left_side[4], right_side[3] - right_side[4])
    speed_right = jnp.maximum(left_side[3] + left_side[4], right_side[3] + right_side[4])
    mass_left = left_side[0] * (speed_left - left_side[3])
    mass_right = right_side[0] * (speed_right - right_side[3])
    middle = (right_side[1] - left_side[1] + mass_left * left_side[3] - mass_right * right_side[3]) / (mass_left - mass_right)
    star_left = star_flux(left_side, speed_left, middle, normal)
    star_right = star_flux(right_side, speed_right, middle, normal)
    return jnp.where(speed_left[None] >= 0.0, left_side[7], jnp.where(middle[None] >= 0.0, star_left, jnp.where(speed_right[None] > 0.0, star_right, right_side[7])))

def apply_matrix(inverse, offset):
    return jnp.stack([inverse[0] * offset[0] + inverse[3] * offset[1] + inverse[4] * offset[2], inverse[3] * offset[0] + inverse[1] * offset[1] + inverse[5] * offset[2], inverse[4] * offset[0] + inverse[5] * offset[1] + inverse[2] * offset[2]])

def flux_tile(block_a, extra_a, block_b, extra_b, self_flag):
    offset = block_b[0:3, None, :] - block_a[0:3, :, None]
    diagonal = jnp.eye(offset.shape[1], dtype=offset.dtype) * self_flag
    distance = jnp.sqrt(lax.optimization_barrier(jnp.sum(offset * offset, axis=0)) + diagonal)
    normal = offset / distance[None]
    weight_a = kernel_weight(distance / block_a[3][:, None]) / (extra_a[21] * extra_a[21])[:, None]
    weight_b = kernel_weight(distance / block_b[3][None, :]) / (extra_b[21] * extra_b[21])[None, :]
    face_vector = weight_a[None] * apply_matrix(extra_a[0:6, :, None], offset) + weight_b[None] * apply_matrix(extra_b[0:6, None, :], offset)
    face_area = jnp.sqrt(lax.optimization_barrier(jnp.sum(face_vector * face_vector, axis=0)))
    grad_a = extra_a[6:21].reshape(5, 3, -1)
    grad_b = extra_b[6:21].reshape(5, 3, -1)
    slope_a = grad_a[:, 0, :, None] * offset[0][None] + grad_a[:, 1, :, None] * offset[1][None] + grad_a[:, 2, :, None] * offset[2][None]
    slope_b = grad_b[:, 0, None, :] * offset[0][None] + grad_b[:, 1, None, :] * offset[1][None] + grad_b[:, 2, None, :] * offset[2][None]
    left_state = block_a[4:9, :, None] + 0.5 * jnp.tanh(slope_a)
    right_state = block_b[4:9, None, :] - 0.5 * jnp.tanh(slope_b)
    face_flux = riemann(left_state, right_state, normal)
    pair_weight = face_area * block_a[9][:, None] * block_b[9][None, :] * (1.0 - diagonal)
    carried = face_flux * pair_weight[None]
    return -lax.optimization_barrier(jnp.sum(carried, axis=2))

def reference(geom, density, velocity, pressure, block_live, pair_list):
    blocks = block_live.shape[0]
    block_slot = jnp.arange(geom.shape[1]) % BLOCK
    alive_mask = (block_slot < jnp.repeat(block_live, BLOCK)).astype(jnp.float32)
    first_rows = jnp.concatenate([geom, jnp.log(density)[None], velocity, jnp.log(pressure)[None], alive_mask[None]], axis=0)
    block_tiles = first_rows.reshape(10, blocks, BLOCK).transpose(1, 0, 2)

    def moment_row(totals, pair_row):
        head_block = jnp.maximum(pair_row[0], 0)
        tail_block = jnp.maximum(pair_row[1], 0)

        def compute(totals_in):
            return totals_in.at[head_block].add(moment_tile(block_tiles[head_block], block_tiles[tail_block]))

        def keeping(totals_in):
            return totals_in
        return (lax.cond(pair_row[0] >= 0, compute, keeping, totals), None)
    totals = lax.scan(moment_row, jnp.zeros((blocks, 22, BLOCK), jnp.float32), pair_list)[0]
    flat_totals = totals.transpose(1, 0, 2).reshape(22, -1)
    extra_rows = finish_moments(flat_totals, geom[3], alive_mask)
    gradients = extra_rows[6:21] * alive_mask[None]
    extras = extra_rows.reshape(22, blocks, BLOCK).transpose(1, 0, 2)

    def flux_row(totals_now, pair_row):
        head_block = jnp.maximum(pair_row[0], 0)
        tail_block = jnp.maximum(pair_row[1], 0)
        self_flag = (head_block == tail_block).astype(jnp.float32)

        def compute(totals_in):
            return totals_in.at[head_block].add(flux_tile(block_tiles[head_block], extras[head_block], block_tiles[tail_block], extras[tail_block], self_flag))

        def keeping(totals_in):
            return totals_in
        return (lax.cond(pair_row[0] >= 0, compute, keeping, totals_now), None)
    rate_sums = lax.scan(flux_row, jnp.zeros((blocks, 5, BLOCK), jnp.float32), pair_list)[0]
    rate_rows = rate_sums.transpose(1, 0, 2).reshape(5, -1)
    return (gradients, rate_rows)
```

```python
import functools

import jax
import jax.numpy as jnp
from jax import lax
from jax.experimental import pallas as pl
from jax.experimental.pallas import tpu as pltpu
from jax.sharding import PartitionSpec as P

BLOCK = 256
LIST = 14
LAYERS = 3
F32 = jnp.float32
BF16 = jnp.bfloat16
ridge_scale = 0.05
gamma = 5.0 / 3.0
HEAD, TAIL, CODE = 64, 78, 92
SELF = 13


def iota(shape, dim):
    return lax.broadcasted_iota(jnp.int32, shape, dim)


def split3(value):
    high = value.astype(BF16)
    rest = value - high.astype(F32)
    middle = rest.astype(BF16)
    low = (rest - middle.astype(F32)).astype(BF16)
    return high, middle, low


def prepare(geom, density, velocity, pressure, live, pair, chunk, place):
    lanes = iota((1, 128), 1)
    total = jnp.zeros((40, 128), F32)
    line = jnp.zeros((1, 128), F32)
    heads = pair[:, 0:1].astype(F32)
    tails = pair[:, 1:2].astype(F32)
    row_lane = iota((LIST, 128), 1) - iota((LIST, 128), 0)
    listed = jnp.where(row_lane == HEAD, heads, 0.0) + jnp.where(row_lane == TAIL, tails, 0.0)
    line = line + jnp.sum(listed, axis=0, keepdims=True)
    for s in range(2):
        at = slice(s * BLOCK, (s + 1) * BLOCK)
        corner = geom[:, at]
        columns = jnp.concatenate([corner, corner], axis=0).T
        cells = []
        for k, count in ((0, 64), (1, 32), (2, 32)):
            smaller = columns[:, k : k + 1] < corner[k : k + 1, :]
            rank = jnp.sum(jnp.where(smaller, 1.0, 0.0), axis=0, keepdims=True)
            cells.append(jnp.floor(rank * (1.0 / count)).astype(jnp.int32))
            low = jnp.min(corner[k : k + 1, :], axis=1, keepdims=True)
            line = line + jnp.where(lanes == CODE + 3 * s + k, low, 0.0)
        lane = cells[0] * 8 + cells[2]
        alive = iota((1, BLOCK), 1) < live[s]
        rows = [corner[0:1], corner[1:2], corner[2:3], jnp.log(density[:, at])]
        rows += [velocity[k : k + 1, at] for k in range(3)]
        rows += [jnp.log(pressure[:, at]), jnp.where(alive, corner[3:4], 0.0)]
        here = iota((8, BLOCK), 0) == cells[1]
        spread = [jnp.where(here, row, 0.0) for row in rows] + [jnp.zeros((8, BLOCK), F32)]
        for par in range(2):
            target = jnp.where(iota((128, BLOCK), 0) == lane + (par * 64 + s * 32), 1.0, 0.0)
            target = target.astype(BF16)
            for part in split3(jnp.concatenate(spread[par::2], axis=0)):
                total = total + lax.dot_general(
                    part, target, (((1,), (1,)), ((), ())), preferred_element_type=F32
                )
        place[0:1, at] = cells[1].astype(F32)
        place[1:2, at] = (cells[0] * 16 + cells[2] + 8 * s).astype(F32)
        place[2:3, at] = jnp.where(alive, 1.0, 0.0)
    chunk[...] = total + jnp.where(iota((40, 128), 0) == 32, line, 0.0)


def prepare_call(geom, density, velocity, pressure, live, pair):
    vmem = pl.BlockSpec(memory_space=pltpu.VMEM)
    smem = pl.BlockSpec(memory_space=pltpu.SMEM)
    return pl.pallas_call(
        prepare,
        out_shape=(jax.ShapeDtypeStruct((40, 128), F32), jax.ShapeDtypeStruct((8, 512), F32)),
        in_specs=[vmem, vmem, vmem, vmem, smem, vmem],
        out_specs=(vmem, vmem),
        name="site_order",
    )(geom, density[None], velocity, pressure[None], live, pair)


def make_lines(rows, own, region):
    lanes = iota(rows.shape, 1)
    kind = (lanes - CODE) % 3
    scale = jnp.where(kind == 0, 0.25, 0.125)
    weight = jnp.where(kind == 0, 1024.0, jnp.where(kind == 1, 32.0, 1.0))
    origin = jnp.where(lanes[0:1] >= CODE + 3, jnp.roll(own, 3, axis=1), own)
    steps = jnp.floor((rows - origin) * scale + 0.5) * weight
    steps = steps + jnp.roll(steps, -1, axis=1) + jnp.roll(steps, -2, axis=1)
    whole = jnp.where(lanes < CODE, rows, steps).astype(jnp.int32)
    return whole


def locate(block, region):
    owner = block // 2
    layer = owner // 32 - region + 1
    return layer, (owner % 32) * LAYERS + layer, block % 2


def direction(step):
    u = step + 1057
    a, b, c = u >> 10, (u >> 5) & 31, u & 31
    valid = (u >= 0) & (a <= 2) & (b <= 2) & (c <= 2)
    return valid, a * 9 + b * 3 + c


def fill_tables(lines, region, own, source, used, faces, face_used):
    def clear(k, _):
        source[k] = -1
        return _

    lax.fori_loop(0, 27 * 16, clear, 0, unroll=16)

    def clear_dir(k, _):
        used[k] = 0
        face_used[k] = 0
        faces[k] = -1
        faces[27 + k] = -1
        return _

    lax.fori_loop(0, 27, clear_dir, 0, unroll=9)

    def slot(p, _):
        head = lines[own, HEAD + p]
        tail = lines[own, TAIL + p]

        @pl.when(head >= 0)
        def _row():
            _, at, s = locate(tail, region)
            place = lines[at, CODE + 3 * s]
            home = lines[own, CODE + 3 * (head % 2)]
            valid, way = direction(place - home)

            @pl.when(valid)
            def _face():
                faces[(head % 2) * 27 + way] = p
                face_used[way] = 1

            def entry(k, _):
                @pl.when(lines[at, HEAD + k] == tail)
                def _listed():
                    layer, there, t = locate(lines[at, TAIL + k], region)
                    near = (layer >= 0) & (layer < LAYERS)
                    there = jnp.where(near, there, 0)
                    fits, towards = direction(lines[there, CODE + 3 * t] - place)

                    @pl.when(fits & near)
                    def _set():
                        source[towards * 16 + p] = there * 2 + t
                        used[towards] = 1

                return _

            lax.fori_loop(0, LIST, entry, 0)

        return _

    lax.fori_loop(0, LIST, slot, 0)


def gather_sites(chunks, source, used, near):
    group = iota((8, 128), 1) // 8

    def one_way(way, _):
        @pl.when(used[way] > 0)
        def _present():
            froms = [source[way * 16 + p] for p in range(LIST)]
            wanted = [jnp.where(f >= 0, p, -1) for p, f in enumerate(froms)]
            froms = [jnp.maximum(f, 0) for f in froms]

            def one_tile(t, _):
                sums = [jnp.zeros((8, 128), F32) for _k in range(8)]
                for p in range(LIST):
                    tile = chunks[froms[p] // 2, pl.ds(pl.multiple_of(t * 8, 8), 8), :]
                    tile = pltpu.roll(tile, (froms[p] % 2) * 96 + p * 8, 1)
                    mask = group == wanted[p]
                    for k in range(8):
                        moved = pltpu.roll(tile, (128 - 64 * (k // 4) - 8 * (k % 4)) % 128, 1)
                        sums[k] = jnp.where(mask, moved, sums[k])
                for k in range(8):
                    near[way, 2 * t + k // 4, k % 4] = sums[k]
                return _

            lax.fori_loop(0, 5, one_tile, 0)
            for x in range(4):
                radius = near[way, 8, x]
                near[way, 9, x] = radius
                near[way, 8, x] = jnp.where(radius > 0.0, 1.0, 0.0)

        @pl.when(used[way] == 0)
        def _absent():
            near[way] = jnp.zeros((10, 4, 8, 128), F32)

        return _

    lax.fori_loop(0, 27, one_way, 0)


def shifted(base, below, above, z, dz):
    if dz == 0:
        return base
    inside = pltpu.roll(base, (-dz) % 128, 1)
    if dz > 0:
        return jnp.where(z + dz < 8, inside, pltpu.roll(above, 8 - dz, 1))
    return jnp.where(z + dz >= 0, inside, pltpu.roll(below, 128 - 8 - dz, 1))


def shift_sites(near, halo):
    z = iota((8, 128), 1) % 8

    def one_row(row, _):
        for xe in range(8):
            sx, x = (0, xe + 2) if xe < 2 else (1, xe - 2) if xe < 6 else (2, xe - 6)
            for sy in range(3):
                base, below, above = [near[sx * 9 + sy * 3 + sz, row, x] for sz in (1, 0, 2)]
                for dz in range(-2, 3):
                    halo[dz + 2, row, xe, 8 * sy : 8 * sy + 8, :] = shifted(
                        base, below, above, z, dz
                    )
        return _

    lax.fori_loop(0, 9, one_row, 0)


def moments(near, halo, fields):
    def one_plane(x, _):
        xi, yi, zi = [near[SELF, k, x] for k in range(3)]
        qi = [near[SELF, 3 + k, x] for k in range(5)]
        alive, radius = near[SELF, 8, x], near[SELF, 9, x]
        radius = jnp.where(radius > 0.0, radius, 1.0)
        inverse_radius = 1.0 / radius

        def step(n, sums):
            dz = n // 5
            xe = n % 5 + x
            sums = list(sums)
            for dy in range(-2, 3):
                near_j = [halo[dz, k, xe, 8 + dy : 16 + dy, :] for k in range(9)]
                ox, oy, oz = near_j[0] - xi, near_j[1] - yi, near_j[2] - zi
                square = ox * ox + oy * oy + oz * oz
                scaled = square * lax.rsqrt(jnp.maximum(square, 1e-12)) * inverse_radius
                remain = jnp.maximum(1.0 - scaled, 0.0)
                remain = remain * remain
                w = remain * remain * (1.0 + 4.0 * scaled) * near_j[8]
                wx, wy, wz = w * ox, w * oy, w * oz
                terms = [w, wx * ox, wy * oy, wz * oz, wx * oy, wx * oz, wy * oz]
                for k in range(5):
                    change = near_j[3 + k] - qi[k]
                    terms += [wx * change, wy * change, wz * change]
                sums = [a + b for a, b in zip(sums, terms)]
            return tuple(sums)

        zero = jnp.zeros((8, 128), F32)
        sums = lax.fori_loop(0, 25, step, (zero,) * 22)
        omega = sums[0] + (1.0 - alive)
        per = 1.0 / omega
        shift = ridge_scale * radius * radius
        m = [sums[1 + k] * per for k in range(6)]
        m[0], m[1], m[2] = m[0] + shift, m[1] + shift, m[2] + shift
        c = [
            m[1] * m[2] - m[5] * m[5],
            m[0] * m[2] - m[4] * m[4],
            m[0] * m[1] - m[3] * m[3],
            m[4] * m[5] - m[3] * m[2],
            m[3] * m[5] - m[4] * m[1],
            m[3] * m[4] - m[0] * m[5],
        ]
        over = 1.0 / (m[0] * c[0] + m[3] * c[3] + m[4] * c[4])
        b = [v * over for v in c]
        rows = [xi, yi, zi] + qi + [near[SELF, 9, x]]
        square = per * per
        rows += [v * square for v in b]
        for k in range(5):
            f = [sums[7 + 3 * k + a] * per for a in range(3)]
            rows.append(b[0] * f[0] + b[3] * f[1] + b[4] * f[2])
            rows.append(b[3] * f[0] + b[1] * f[1] + b[5] * f[2])
            rows.append(b[4] * f[0] + b[5] * f[1] + b[2] * f[2])
        for k in range(10):
            pair = jnp.concatenate(rows[3 * k : 3 * k + 3], axis=0)
            for n, part in enumerate(split3(pair)):
                fields[x, n, 24 * k : 24 * k + 24, :] = part.astype(F32)
        return _

    lax.fori_loop(0, 4, one_plane, 0)


def gather_fields(fields, faces, face_used, around):
    lanes = iota((1, 128), 1)
    z = lanes % 8
    sources = iota((128, 128), 0)

    def one_way(n, _):
        sz = n // 3
        sy = n % 3
        any_used = face_used[sy * 3 + sz] + face_used[9 + sy * 3 + sz] + face_used[18 + sy * 3 + sz]

        @pl.when(any_used > 0)
        def _present():
            total = jnp.zeros((240, 128), F32)
            for x in range(4):
                wanted = jnp.full((1, 128), -1, jnp.int32)
                for sx, xe in ((1, x + 2), (2, x + 6) if x < 2 else (0, x - 2)):
                    for s in range(2):
                        p = faces[s * 27 + sx * 9 + sy * 3 + sz]
                        lane = jnp.where(p >= 0, p * 8 + z, -1)
                        wanted = jnp.where(lanes // 8 == xe * 2 + s, lane, wanted)
                hot = jnp.where(sources == wanted, 1.0, 0.0).astype(BF16)
                for k in range(3):
                    total = total + jnp.dot(
                        fields[x, k].astype(BF16), hot, preferred_element_type=F32
                    )
            around[n] = total

        @pl.when(any_used == 0)
        def _absent():
            around[n] = jnp.zeros((240, 128), F32)

        return _

    lax.fori_loop(0, 9, one_way, 0)


def shift_fields(around, wide):
    lanes = iota((8, 128), 1)
    z = lanes % 8
    left = lanes < 64

    def one_row(row, _):
        at = pl.ds(pl.multiple_of(row * 8, 8), 8)
        for sy in range(3):
            base, below, above = [around[sz * 3 + sy, at, :] for sz in (1, 0, 2)]
            for dz in range(-2, 3):
                far = shifted(base, below, above, z, dz)
                rows = slice(8 * sy, 8 * sy + 8)
                wide[dz + 2, 0, row, rows, :] = far
                for k, step in ((1, 16), (2, 32)):
                    both = jnp.where(left, pltpu.roll(far, 128 - step, 1), pltpu.roll(far, step, 1))
                    wide[dz + 2, k, row, rows, :] = both
        return _

    lax.fori_loop(0, 30, one_row, 0)


def weight(scaled):
    remain = jnp.maximum(1.0 - scaled, 0.0)
    remain = remain * remain
    return remain * remain * (1.0 + 4.0 * scaled)


def side(state, n):
    density, pressure = jnp.exp(state[0]), jnp.exp(state[4])
    v = state[1:4]
    speed = v[0] * n[0] + v[1] * n[1] + v[2] * n[2]
    sound = jnp.exp(0.5 * (state[4] - state[0])) * (gamma**0.5)
    return density, pressure, v[0], v[1], v[2], speed, sound


def face(near, far):
    o = [far(k) - near(k) for k in range(3)]
    square = jnp.maximum(o[0] * o[0] + o[1] * o[1] + o[2] * o[2], 1e-12)
    inverse = lax.rsqrt(square)
    distance = square * inverse
    n = [v * inverse for v in o]
    hi, hj = near(8), far(8)
    live = jnp.minimum(hi, hj) > 0.0
    wi = weight(distance * (1.0 / jnp.where(hi > 0.0, hi, 1.0)))
    wj = weight(distance * (1.0 / jnp.where(hj > 0.0, hj, 1.0)))
    c = [wi * near(9 + k) + wj * far(9 + k) for k in range(6)]
    a = [
        c[0] * o[0] + c[3] * o[1] + c[4] * o[2],
        c[3] * o[0] + c[1] * o[1] + c[5] * o[2],
        c[4] * o[0] + c[5] * o[1] + c[2] * o[2],
    ]
    area = a[0] * a[0] + a[1] * a[1] + a[2] * a[2]
    area = jnp.where(live, jnp.sqrt(area), 0.0)
    left, right = [], []
    for k in range(5):
        gi = near(15 + 3 * k) * o[0] + near(16 + 3 * k) * o[1] + near(17 + 3 * k) * o[2]
        gj = far(15 + 3 * k) * o[0] + far(16 + 3 * k) * o[1] + far(17 + 3 * k) * o[2]
        left.append(near(3 + k) + 0.5 * jnp.tanh(gi))
        right.append(far(3 + k) - 0.5 * jnp.tanh(gj))
    sl, sr = side(left, n), side(right, n)
    slow = jnp.minimum(sl[5] - sl[6], sr[5] - sr[6])
    fast = jnp.maximum(sl[5] + sl[6], sr[5] + sr[6])
    ml, mr = sl[0] * (slow - sl[5]), sr[0] * (fast - sr[5])
    middle = (sr[1] - sl[1] + ml * sl[5] - mr * sr[5]) / (ml - mr)
    from_left = (slow >= 0.0) | (middle >= 0.0)
    density, pressure, v0, v1, v2, speed, _ = [
        jnp.where(from_left, p, q) for p, q in zip(sl, sr)
    ]
    mass, wave = jnp.where(from_left, ml, mr), jnp.where(from_left, slow, fast)
    star = jnp.where(from_left, -slow, fast) > 0.0
    kinetic = 0.5 * (v0 * v0 + v1 * v1 + v2 * v2)
    energy = pressure * (1.0 / (gamma - 1.0)) + density * kinetic
    push = jnp.where(star, wave * mass / (wave - middle), 0.0)
    rest = speed - jnp.where(star, wave, 0.0)
    lift = middle - speed
    flow = density * rest + push
    press = pressure + push * lift
    heat = energy * rest + pressure * speed
    heat = heat + push * (energy / density + lift * (middle + pressure / mass))
    terms = [flow, v0 * flow + press * n[0], v1 * flow + press * n[1], v2 * flow + press * n[2]]
    return [jnp.where(live, t * area, 0.0) for t in terms + [heat]]


def fluxes(wide):
    half = iota((8, 128), 1) < 64

    def near(row):
        return wide[2, 2, row, 8:16, :]

    def add(sums, far):
        return tuple(a + b for a, b in zip(sums, face(near, far)))

    def step(dz, sums):
        for k in range(2):
            for dy in range(-2, 3):
                sums = add(sums, lambda row: wide[dz, k, row, 8 + dy : 16 + dy, :])
        for d in (-2, 1):
            sums = add(
                sums,
                lambda row: jnp.where(
                    half, wide[dz, 2, row, 8 + d : 16 + d, :], wide[dz, 2, row, 9 + d : 17 + d, :]
                ),
            )
        return sums

    sums = lax.fori_loop(0, 5, step, (jnp.zeros((8, 128), F32),) * 5)
    for d in (0, 1):
        sums = add(
            sums, lambda row: jnp.where(half, wide[d, 2, row, 8:16, :], wide[4 - d, 2, row, 8:16, :])
        )
    return [-(v + pltpu.roll(v, 64, 1)) for v in sums]


def sweep(
    lines, chunks, place, gradients, rate, source, used, faces, face_used, near, halo, fields,
    around, wide,
):
    region, own = lines[0, 126], lines[0, 127]
    fill_tables(lines, region, own, source, used, faces, face_used)
    gather_sites(chunks, source, used, near)
    shift_sites(near, halo)
    moments(near, halo, fields)
    gather_fields(fields, faces, face_used, around)
    shift_fields(around, wide)
    rates = fluxes(wide)
    rows = [wide[2, 2, 15 + k, 8:16, :] for k in range(15)] + rates
    found = jnp.concatenate(rows, axis=0)
    lane = place[1:2, :].astype(jnp.int32)
    hot = jnp.where(iota((128, 512), 0) == lane, 1.0, 0.0).astype(BF16)
    total = jnp.zeros((160, 512), F32)
    for part in split3(found):
        total = total + jnp.dot(part, hot, preferred_element_type=F32)
    here = (iota((8, 512), 0) == place[0:1, :].astype(jnp.int32)) & (place[2:3, :] > 0.0)
    for k in range(20):
        row = jnp.sum(jnp.where(here, total[8 * k : 8 * k + 8], 0.0), axis=0, keepdims=True)
        if k < 15:
            gradients[k : k + 1, :] = row
        else:
            rate[k - 15 : k - 14, :] = row


def sweep_call(lines, chunks, place):
    vmem = pl.BlockSpec(memory_space=pltpu.VMEM)
    smem = pl.BlockSpec(memory_space=pltpu.SMEM)
    return pl.pallas_call(
        sweep,
        out_shape=(jax.ShapeDtypeStruct((15, 512), F32), jax.ShapeDtypeStruct((5, 512), F32)),
        in_specs=[smem, vmem, vmem],
        out_specs=(vmem, vmem),
        scratch_shapes=[
            pltpu.SMEM((27 * 16,), jnp.int32),
            pltpu.SMEM((27,), jnp.int32),
            pltpu.SMEM((54,), jnp.int32),
            pltpu.SMEM((27,), jnp.int32),
            pltpu.VMEM((27, 10, 4, 8, 128), F32),
            pltpu.VMEM((5, 9, 8, 24, 128), F32),
            pltpu.VMEM((4, 3, 240, 128), F32),
            pltpu.VMEM((9, 240, 128), F32),
            pltpu.VMEM((5, 3, 30, 24, 128), F32),
        ],
        compiler_params=pltpu.CompilerParams(vmem_limit_bytes=48 * 1024 * 1024),
        name="sweep",
    )(lines, chunks, place)


def beside(chunk):
    count = lax.axis_size("region")
    up = [(i, i + 1) for i in range(count - 1)]
    down = [(i + 1, i) for i in range(count - 1)]
    below, above = lax.ppermute(chunk, "region", up), lax.ppermute(chunk, "region", down)
    return jnp.stack([below, chunk, above])


def body(geom, density, velocity, pressure, block_live, pair_list):
    chunk, place = prepare_call(geom, density, velocity, pressure, block_live, pair_list)
    chunks = lax.all_gather(beside(chunk), "group", axis=0, tiled=True)
    region = lax.axis_index("region")
    own = lax.axis_index("group") * LAYERS + 1
    lines = make_lines(chunks[:, 32, :], chunk[32:33, :], region)
    tag = jnp.where(iota((1, 128), 1) == 126, region, own)
    lines = jnp.where(iota(lines.shape, 1) >= 126, tag, lines)
    return sweep_call(lines, chunks, place)


def solution(mesh):
    both = ("region", "group")
    return jax.shard_map(
        body,
        mesh=mesh,
        in_specs=(P(None, both), P(both), P(None, both), P(both), P(both), P(both, None)),
        out_specs=(P(None, both), P(None, both)),
        check_vma=False,
    )
```

```python
import functools

import jax
import jax.numpy as jnp
from jax import lax
from jax.experimental import pallas as pl
from jax.experimental.pallas import tpu as pltpu
from jax.sharding import PartitionSpec as P

BLOCK = 256
LIST = 14
LAYERS = 3
F32 = jnp.float32
BF16 = jnp.bfloat16
ridge_scale = 0.05
gamma = 5.0 / 3.0
HEAD, TAIL, CORNER = 64, 78, 92
MESH = pl.DeviceIdType.MESH
SELF = 13


def iota(shape, dim):
    return lax.broadcasted_iota(jnp.int32, shape, dim)


def split3(value):
    high = value.astype(BF16)
    rest = value - high.astype(F32)
    middle = rest.astype(BF16)
    low = (rest - middle.astype(F32)).astype(BF16)
    return high, middle, low


def prepare(geom, density, velocity, pressure, live, pair, line, place):
    lanes = iota((1, 128), 1)
    total = jnp.zeros((40, 128), F32)
    line[...] = jnp.zeros((8, 128), F32)
    line[0:1, HEAD : HEAD + LIST] = pair[0:1, :].astype(F32)
    line[0:1, TAIL : TAIL + LIST] = pair[1:2, :].astype(F32)
    listed = line[0:1, :]
    for s in range(2):
        at = slice(s * BLOCK, (s + 1) * BLOCK)
        corner = geom[:, at]
        columns = jnp.concatenate([corner, corner], axis=0).T
        cells = []
        for k, count in ((0, 64), (1, 32), (2, 32)):
            smaller = columns[:, k : k + 1] < corner[k : k + 1, :]
            rank = jnp.sum(jnp.where(smaller, 1.0, 0.0), axis=0, keepdims=True)
            cells.append(jnp.floor(rank * (1.0 / count)).astype(jnp.int32))
            low = jnp.min(corner[k : k + 1, :], axis=1, keepdims=True)
            listed = listed + jnp.where(lanes == CORNER + 3 * s + k, low, 0.0)
        lane = cells[0] * 8 + cells[2]
        alive = iota((1, BLOCK), 1) < live[s]
        rows = [corner[0:1], corner[1:2], corner[2:3], jnp.log(density[:, at])]
        rows += [velocity[k : k + 1, at] for k in range(3)]
        rows += [jnp.log(pressure[:, at]), jnp.where(alive, corner[3:4], 0.0)]
        here = iota((8, BLOCK), 0) == cells[1]
        spread = [jnp.where(here, row, 0.0) for row in rows] + [jnp.zeros((8, BLOCK), F32)]
        for par in range(2):
            target = jnp.where(iota((128, BLOCK), 0) == lane + (par * 64 + s * 32), 1.0, 0.0)
            target = target.astype(BF16)
            for part in split3(jnp.concatenate(spread[par::2], axis=0)):
                total = total + lax.dot_general(
                    part, target, (((1,), (1,)), ((), ())), preferred_element_type=F32
                )
        place[0:1, at] = cells[1].astype(F32)
        place[1:2, at] = (cells[0] * 16 + cells[2] + 8 * s).astype(F32)
        place[2:3, at] = jnp.where(alive, 1.0, 0.0)
    return total + jnp.where(iota((40, 128), 0) == 32, listed, 0.0)


def read_lists(chunks, lists, region, group):
    lanes = iota((32, 128), 1)
    kind = (lanes - CORNER) % 3
    scale = jnp.where(kind == 0, 0.25, 0.125)
    weight = jnp.where(kind == 0, 1024.0, jnp.where(kind == 1, 32.0, 1.0))
    own = chunks[32 + group, 32:33, :]
    own = jnp.where(lanes[0:1] >= CORNER + 3, pltpu.roll(own, 3, 1), own)
    whole = jnp.where(lanes == 96, region, group)
    for layer in range(LAYERS):
        rows = chunks[32 * layer : 32 * layer + 32, 32, :]
        steps = jnp.floor((rows - own) * scale + 0.5) * weight
        steps = steps + pltpu.roll(steps, 127, 1) + pltpu.roll(steps, 126, 1)
        rows = pltpu.roll(jnp.where(lanes < CORNER, rows, steps), 64 + 32 * layer, 1)
        whole = jnp.where(lanes // 32 == layer, rows.astype(jnp.int32), whole)
    lists[...] = whole


def exchange(
    geom, density, velocity, pressure, live, pair, chunks, place, lists, line,
    x_send, x_recv, z_send, z_recv, r_send, r_recv,
):
    region, group = lax.axis_index("region"), lax.axis_index("group")
    z, x = group // 4, group % 4

    def column(step):
        return (region, z * 4 + (x + step) % 4)

    def plane(step):
        return (region, (z + 8 + step) % 8 * 4 + x)

    def slab(step):
        return ((region + 16 + step) % 16, group)

    partners = [column(k) for k in (1, 2, 3)] + [plane(1), plane(-1), slab(1), slab(-1)]
    barrier = pltpu.get_barrier_semaphore()
    for partner in partners:
        pl.semaphore_signal(barrier, inc=1, device_id=partner, device_id_type=MESH)
    chunks[32 + group] = prepare(geom, density, velocity, pressure, live, pair, line, place)
    pl.semaphore_wait(barrier, len(partners))

    def copy(start, count, to, device, send, recv):
        return pltpu.make_async_remote_copy(
            src_ref=chunks.at[pl.ds(start, count)],
            dst_ref=chunks.at[pl.ds(to, count)],
            send_sem=send,
            recv_sem=recv,
            device_id=device,
            device_id_type=MESH,
        )

    def along_x(k):
        return copy(32 + group, 1, 32 + group, column(k), x_send.at[k - 1], x_recv.at[k - 1])

    def bundle(step):
        return 32 + (z + 16 + step) % 8 * 4

    def along_z(step, t):
        start = bundle(-step * t)
        if t == 3:
            start = start + (0 if step > 0 else 2)
        side = 0 if step > 0 else 1
        count = 2 if t == 3 else 4
        return copy(start, count, start, plane(step), z_send.at[side, t], z_recv.at[side, t])

    def arrived_z(step, t):
        start = bundle(-step * (t + 1))
        if t == 3:
            start = start + (0 if step > 0 else 2)
        side = 0 if step > 0 else 1
        count = 2 if t == 3 else 4
        return copy(start, count, start, plane(step), z_send.at[side, t], z_recv.at[side, t])

    def along_r(step, k):
        side = 0 if step > 0 else 1
        to = bundle(k) + (-32 if step > 0 else 32)
        return copy(bundle(k), 4, to, slab(step), r_send.at[side, k], r_recv.at[side, k])

    def arrived_r(step, k):
        side = 0 if step > 0 else 1
        to = bundle(k) + (-32 if step > 0 else 32)
        return copy(to, 4, to, slab(step), r_send.at[side, k], r_recv.at[side, k])

    def give(k):
        for step in (1, -1):
            along_r(step, k % 8).start()

    for k in (2, 1, 3):
        along_x(k).start()
    for k in (1, 2, 3):
        begin = 32 + z * 4 + (x + 4 - k) % 4
        copy(begin, 1, begin, column(k), x_send.at[k - 1], x_recv.at[k - 1]).wait_recv()
    along_z(1, 0).start()
    along_z(-1, 0).start()
    give(0)
    for t in range(3):
        for step in (1, -1):
            arrived_z(step, t).wait_recv()
            along_z(step, t + 1).start()
            give(-step * (t + 1))
    arrived_z(1, 3).wait_recv()
    arrived_z(-1, 3).wait_recv()
    give(4)
    for k in range(8):
        arrived_r(1, k).wait_recv()
        arrived_r(-1, k).wait_recv()
    read_lists(chunks, lists, region, group)
    for k in (1, 2, 3):
        along_x(k).wait_send()
    for t in range(4):
        along_z(1, t).wait_send()
        along_z(-1, t).wait_send()
    for k in range(8):
        along_r(1, k).wait_send()
        along_r(-1, k).wait_send()


def exchange_call(geom, density, velocity, pressure, live, pair):
    vmem = pl.BlockSpec(memory_space=pltpu.VMEM)
    smem = pl.BlockSpec(memory_space=pltpu.SMEM)
    dma = pltpu.SemaphoreType.DMA
    return pl.pallas_call(
        exchange,
        out_shape=(
            jax.ShapeDtypeStruct((96, 40, 128), F32),
            jax.ShapeDtypeStruct((8, 512), F32),
            jax.ShapeDtypeStruct((32, 128), jnp.int32),
        ),
        in_specs=[vmem, vmem, vmem, vmem, smem, vmem],
        out_specs=(vmem, vmem, vmem),
        scratch_shapes=[
            pltpu.VMEM((8, 128), F32),
            dma((3,)),
            dma((3,)),
            dma((2, 4)),
            dma((2, 4)),
            dma((2, 8)),
            dma((2, 8)),
        ],
        compiler_params=pltpu.CompilerParams(
            collective_id=0, has_side_effects=True, vmem_limit_bytes=16 * 1024 * 1024
        ),
        name="gather_sites",
    )(geom, density[None], velocity, pressure[None], live, pair.T)


def locate(block, region):
    owner = block // 2
    return owner // 32 - region + 1, owner % 32, block % 2


def direction(step):
    u = step + 1057
    a, b, c = u >> 10, (u >> 5) & 31, u & 31
    valid = (u >= 0) & (a <= 2) & (b <= 2) & (c <= 2)
    return valid, a * 9 + b * 3 + c


def fill_tables(lists, region, group, source, used, faces, face_used):
    def clear(k, _):
        source[k] = -1
        return _

    lax.fori_loop(0, 27 * 16, clear, 0, unroll=16)

    def clear_dir(k, _):
        used[k] = 0
        face_used[k] = 0
        faces[k] = -1
        faces[27 + k] = -1
        return _

    lax.fori_loop(0, 27, clear_dir, 0, unroll=9)

    def code(g, layer, s):
        return lists[g, layer * 32 + 28 + 3 * s]

    def slot(p, _):
        head = lists[group, 32 + p]
        tail = lists[group, 32 + LIST + p]

        @pl.when(head >= 0)
        def _row():
            layer, g, s = locate(tail, region)
            place = code(g, layer, s)
            valid, way = direction(place - code(group, 1, head % 2))

            @pl.when(valid)
            def _face():
                faces[(head % 2) * 27 + way] = p
                face_used[way] = 1

            def entry(k, _):
                @pl.when(lists[g, layer * 32 + k] == tail)
                def _listed():
                    wide, there, t = locate(lists[g, layer * 32 + LIST + k], region)
                    near = (wide >= 0) & (wide < LAYERS)
                    wide = jnp.where(near, wide, 1)
                    fits, towards = direction(code(there, wide, t) - place)

                    @pl.when(fits & near)
                    def _set():
                        source[towards * 16 + p] = (wide * 32 + there) * 2 + t
                        used[towards] = 1

                return _

            lax.fori_loop(0, LIST, entry, 0)

        return _

    lax.fori_loop(0, LIST, slot, 0)


def collect_sites(chunks, source, used, near):
    group = iota((8, 128), 1) // 8

    def one_way(way, _):
        @pl.when(used[way] > 0)
        def _present():
            froms = [source[way * 16 + p] for p in range(LIST)]
            wanted = [jnp.where(f >= 0, p, -1) for p, f in enumerate(froms)]
            froms = [jnp.maximum(f, 0) for f in froms]

            def one_tile(t, _):
                sums = [jnp.zeros((8, 128), F32) for _k in range(8)]
                for p in range(LIST):
                    tile = chunks[froms[p] // 2, pl.ds(pl.multiple_of(t * 8, 8), 8), :]
                    tile = pltpu.roll(tile, (froms[p] % 2) * 96 + p * 8, 1)
                    mask = group == wanted[p]
                    for k in range(8):
                        moved = pltpu.roll(tile, (128 - 64 * (k // 4) - 8 * (k % 4)) % 128, 1)
                        sums[k] = jnp.where(mask, moved, sums[k])
                for k in range(8):
                    near[way, 2 * t + k // 4, k % 4] = sums[k]
                return _

            lax.fori_loop(0, 5, one_tile, 0)
            for x in range(4):
                radius = near[way, 8, x]
                near[way, 9, x] = radius
                near[way, 8, x] = jnp.where(radius > 0.0, 1.0, 0.0)

        @pl.when(used[way] == 0)
        def _absent():
            near[way] = jnp.zeros((10, 4, 8, 128), F32)

        return _

    lax.fori_loop(0, 27, one_way, 0)


def shifted(base, below, above, z, dz):
    if dz == 0:
        return base
    inside = pltpu.roll(base, (-dz) % 128, 1)
    if dz > 0:
        return jnp.where(z + dz < 8, inside, pltpu.roll(above, 8 - dz, 1))
    return jnp.where(z + dz >= 0, inside, pltpu.roll(below, 128 - 8 - dz, 1))


def shift_sites(near, halo):
    z = iota((8, 128), 1) % 8

    def one_row(row, _):
        for xe in range(8):
            sx, x = (0, xe + 2) if xe < 2 else (1, xe - 2) if xe < 6 else (2, xe - 6)
            for sy in range(3):
                base, below, above = [near[sx * 9 + sy * 3 + sz, row, x] for sz in (1, 0, 2)]
                for dz in range(-2, 3):
                    halo[dz + 2, row, xe, 8 * sy : 8 * sy + 8, :] = shifted(
                        base, below, above, z, dz
                    )
        return _

    lax.fori_loop(0, 9, one_row, 0)


def moments(near, halo, fields):
    def one_plane(x, _):
        xi, yi, zi = [near[SELF, k, x] for k in range(3)]
        qi = [near[SELF, 3 + k, x] for k in range(5)]
        alive, radius = near[SELF, 8, x], near[SELF, 9, x]
        radius = jnp.where(radius > 0.0, radius, 1.0)
        inverse_radius = 1.0 / radius

        def step(n, sums):
            dz = n // 5
            xe = n % 5 + x
            sums = list(sums)
            for dy in range(-2, 3):
                near_j = [halo[dz, k, xe, 8 + dy : 16 + dy, :] for k in range(9)]
                ox, oy, oz = near_j[0] - xi, near_j[1] - yi, near_j[2] - zi
                square = ox * ox + oy * oy + oz * oz
                scaled = square * lax.rsqrt(jnp.maximum(square, 1e-12)) * inverse_radius
                remain = jnp.maximum(1.0 - scaled, 0.0)
                remain = remain * remain
                w = remain * remain * (1.0 + 4.0 * scaled) * near_j[8]
                wx, wy, wz = w * ox, w * oy, w * oz
                terms = [w, wx * ox, wy * oy, wz * oz, wx * oy, wx * oz, wy * oz]
                for k in range(5):
                    change = near_j[3 + k] - qi[k]
                    terms += [wx * change, wy * change, wz * change]
                sums = [a + b for a, b in zip(sums, terms)]
            return tuple(sums)

        zero = jnp.zeros((8, 128), F32)
        sums = lax.fori_loop(0, 25, step, (zero,) * 22)
        omega = sums[0] + (1.0 - alive)
        per = 1.0 / omega
        shift = ridge_scale * radius * radius
        m = [sums[1 + k] * per for k in range(6)]
        m[0], m[1], m[2] = m[0] + shift, m[1] + shift, m[2] + shift
        c = [
            m[1] * m[2] - m[5] * m[5],
            m[0] * m[2] - m[4] * m[4],
            m[0] * m[1] - m[3] * m[3],
            m[4] * m[5] - m[3] * m[2],
            m[3] * m[5] - m[4] * m[1],
            m[3] * m[4] - m[0] * m[5],
        ]
        over = 1.0 / (m[0] * c[0] + m[3] * c[3] + m[4] * c[4])
        b = [v * over for v in c]
        rows = [xi, yi, zi] + qi + [near[SELF, 9, x]]
        square = per * per
        rows += [v * square for v in b]
        for k in range(5):
            f = [sums[7 + 3 * k + a] * per for a in range(3)]
            rows.append(b[0] * f[0] + b[3] * f[1] + b[4] * f[2])
            rows.append(b[3] * f[0] + b[1] * f[1] + b[5] * f[2])
            rows.append(b[4] * f[0] + b[5] * f[1] + b[2] * f[2])
        for k in range(10):
            pair = jnp.concatenate(rows[3 * k : 3 * k + 3], axis=0)
            for n, part in enumerate(split3(pair)):
                fields[x, n, 24 * k : 24 * k + 24, :] = part.astype(F32)
        return _

    lax.fori_loop(0, 4, one_plane, 0)


def gather_fields(fields, faces, face_used, around):
    lanes = iota((1, 128), 1)
    z = lanes % 8
    sources = iota((128, 128), 0)

    def one_way(n, _):
        sz = n // 3
        sy = n % 3
        any_used = face_used[sy * 3 + sz] + face_used[9 + sy * 3 + sz] + face_used[18 + sy * 3 + sz]

        @pl.when(any_used > 0)
        def _present():
            total = jnp.zeros((240, 128), F32)
            for x in range(4):
                wanted = jnp.full((1, 128), -1, jnp.int32)
                for sx, xe in ((1, x + 2), (2, x + 6) if x < 2 else (0, x - 2)):
                    for s in range(2):
                        p = faces[s * 27 + sx * 9 + sy * 3 + sz]
                        lane = jnp.where(p >= 0, p * 8 + z, -1)
                        wanted = jnp.where(lanes // 8 == xe * 2 + s, lane, wanted)
                hot = jnp.where(sources == wanted, 1.0, 0.0).astype(BF16)
                for k in range(3):
                    total = total + jnp.dot(
                        fields[x, k].astype(BF16), hot, preferred_element_type=F32
                    )
            around[n] = total

        @pl.when(any_used == 0)
        def _absent():
            around[n] = jnp.zeros((240, 128), F32)

        return _

    lax.fori_loop(0, 9, one_way, 0)


def shift_fields(around, wide):
    lanes = iota((8, 128), 1)
    z = lanes % 8
    left = lanes < 64

    def one_row(row, _):
        at = pl.ds(pl.multiple_of(row * 8, 8), 8)
        for sy in range(3):
            base, below, above = [around[sz * 3 + sy, at, :] for sz in (1, 0, 2)]
            for dz in range(-2, 3):
                far = shifted(base, below, above, z, dz)
                rows = slice(8 * sy, 8 * sy + 8)
                wide[dz + 2, 0, row, rows, :] = far
                for k, step in ((1, 16), (2, 32)):
                    both = jnp.where(left, pltpu.roll(far, 128 - step, 1), pltpu.roll(far, step, 1))
                    wide[dz + 2, k, row, rows, :] = both
        return _

    lax.fori_loop(0, 30, one_row, 0)


def weight(scaled):
    remain = jnp.maximum(1.0 - scaled, 0.0)
    remain = remain * remain
    return remain * remain * (1.0 + 4.0 * scaled)


def side(state, n):
    density, pressure = jnp.exp(state[0]), jnp.exp(state[4])
    v = state[1:4]
    speed = v[0] * n[0] + v[1] * n[1] + v[2] * n[2]
    sound = jnp.exp(0.5 * (state[4] - state[0])) * (gamma**0.5)
    return density, pressure, v[0], v[1], v[2], speed, sound


def face(near, far):
    o = [far(k) - near(k) for k in range(3)]
    square = jnp.maximum(o[0] * o[0] + o[1] * o[1] + o[2] * o[2], 1e-12)
    inverse = lax.rsqrt(square)
    distance = square * inverse
    n = [v * inverse for v in o]
    hi, hj = near(8), far(8)
    live = jnp.minimum(hi, hj) > 0.0
    wi = weight(distance * (1.0 / jnp.where(hi > 0.0, hi, 1.0)))
    wj = weight(distance * (1.0 / jnp.where(hj > 0.0, hj, 1.0)))
    c = [wi * near(9 + k) + wj * far(9 + k) for k in range(6)]
    a = [
        c[0] * o[0] + c[3] * o[1] + c[4] * o[2],
        c[3] * o[0] + c[1] * o[1] + c[5] * o[2],
        c[4] * o[0] + c[5] * o[1] + c[2] * o[2],
    ]
    area = a[0] * a[0] + a[1] * a[1] + a[2] * a[2]
    area = jnp.where(live, jnp.sqrt(area), 0.0)
    left, right = [], []
    for k in range(5):
        gi = near(15 + 3 * k) * o[0] + near(16 + 3 * k) * o[1] + near(17 + 3 * k) * o[2]
        gj = far(15 + 3 * k) * o[0] + far(16 + 3 * k) * o[1] + far(17 + 3 * k) * o[2]
        left.append(near(3 + k) + 0.5 * jnp.tanh(gi))
        right.append(far(3 + k) - 0.5 * jnp.tanh(gj))
    sl, sr = side(left, n), side(right, n)
    slow = jnp.minimum(sl[5] - sl[6], sr[5] - sr[6])
    fast = jnp.maximum(sl[5] + sl[6], sr[5] + sr[6])
    ml, mr = sl[0] * (slow - sl[5]), sr[0] * (fast - sr[5])
    middle = (sr[1] - sl[1] + ml * sl[5] - mr * sr[5]) / (ml - mr)
    from_left = (slow >= 0.0) | (middle >= 0.0)
    density, pressure, v0, v1, v2, speed, _ = [
        jnp.where(from_left, p, q) for p, q in zip(sl, sr)
    ]
    mass, wave = jnp.where(from_left, ml, mr), jnp.where(from_left, slow, fast)
    star = jnp.where(from_left, -slow, fast) > 0.0
    kinetic = 0.5 * (v0 * v0 + v1 * v1 + v2 * v2)
    energy = pressure * (1.0 / (gamma - 1.0)) + density * kinetic
    push = jnp.where(star, wave * mass / (wave - middle), 0.0)
    rest = speed - jnp.where(star, wave, 0.0)
    lift = middle - speed
    flow = density * rest + push
    press = pressure + push * lift
    heat = energy * rest + pressure * speed
    heat = heat + push * (energy / density + lift * (middle + pressure / mass))
    terms = [flow, v0 * flow + press * n[0], v1 * flow + press * n[1], v2 * flow + press * n[2]]
    return [jnp.where(live, t * area, 0.0) for t in terms + [heat]]


def fluxes(wide):
    half = iota((8, 128), 1) < 64

    def near(row):
        return wide[2, 2, row, 8:16, :]

    def add(sums, far):
        return tuple(a + b for a, b in zip(sums, face(near, far)))

    def step(dz, sums):
        for k in range(2):
            for dy in range(-2, 3):
                sums = add(sums, lambda row: wide[dz, k, row, 8 + dy : 16 + dy, :])
        for d in (-2, 1):
            sums = add(
                sums,
                lambda row: jnp.where(
                    half, wide[dz, 2, row, 8 + d : 16 + d, :], wide[dz, 2, row, 9 + d : 17 + d, :]
                ),
            )
        return sums

    sums = lax.fori_loop(0, 5, step, (jnp.zeros((8, 128), F32),) * 5)
    for d in (0, 1):
        sums = add(
            sums, lambda row: jnp.where(half, wide[d, 2, row, 8:16, :], wide[4 - d, 2, row, 8:16, :])
        )
    return [-(v + pltpu.roll(v, 64, 1)) for v in sums]


def sweep(
    lists, chunks, place, gradients, rate, source, used, faces, face_used, near, halo, fields,
    around, wide,
):
    region, group = lists[0, 96], lists[0, 97]
    fill_tables(lists, region, group, source, used, faces, face_used)
    collect_sites(chunks, source, used, near)
    shift_sites(near, halo)
    moments(near, halo, fields)
    gather_fields(fields, faces, face_used, around)
    shift_fields(around, wide)
    rates = fluxes(wide)
    rows = [wide[2, 2, 15 + k, 8:16, :] for k in range(15)] + rates
    found = jnp.concatenate(rows, axis=0)
    lane = place[1:2, :].astype(jnp.int32)
    hot = jnp.where(iota((128, 512), 0) == lane, 1.0, 0.0).astype(BF16)
    total = jnp.zeros((160, 512), F32)
    for part in split3(found):
        total = total + jnp.dot(part, hot, preferred_element_type=F32)
    here = (iota((8, 512), 0) == place[0:1, :].astype(jnp.int32)) & (place[2:3, :] > 0.0)
    for k in range(20):
        row = jnp.sum(jnp.where(here, total[8 * k : 8 * k + 8], 0.0), axis=0, keepdims=True)
        if k < 15:
            gradients[k : k + 1, :] = row
        else:
            rate[k - 15 : k - 14, :] = row


def sweep_call(lists, chunks, place):
    vmem = pl.BlockSpec(memory_space=pltpu.VMEM)
    smem = pl.BlockSpec(memory_space=pltpu.SMEM)
    return pl.pallas_call(
        sweep,
        out_shape=(jax.ShapeDtypeStruct((15, 512), F32), jax.ShapeDtypeStruct((5, 512), F32)),
        in_specs=[smem, vmem, vmem],
        out_specs=(vmem, vmem),
        scratch_shapes=[
            pltpu.SMEM((27 * 16,), jnp.int32),
            pltpu.SMEM((27,), jnp.int32),
            pltpu.SMEM((54,), jnp.int32),
            pltpu.SMEM((27,), jnp.int32),
            pltpu.VMEM((27, 10, 4, 8, 128), F32),
            pltpu.VMEM((5, 9, 8, 24, 128), F32),
            pltpu.VMEM((4, 3, 240, 128), F32),
            pltpu.VMEM((9, 240, 128), F32),
            pltpu.VMEM((5, 3, 30, 24, 128), F32),
        ],
        compiler_params=pltpu.CompilerParams(vmem_limit_bytes=48 * 1024 * 1024),
        name="sweep",
    )(lists, chunks, place)


def body(geom, density, velocity, pressure, block_live, pair_list):
    chunks, place, lists = exchange_call(geom, density, velocity, pressure, block_live, pair_list)
    return sweep_call(lists, chunks, place)


def solution(mesh):
    both = ("region", "group")
    return jax.shard_map(
        body,
        mesh=mesh,
        in_specs=(P(None, both), P(both), P(None, both), P(both), P(both), P(both, None)),
        out_specs=(P(None, both), P(None, both)),
        check_vma=False,
    )
```

```python
import functools

import jax
import jax.numpy as jnp
from jax import lax
from jax.experimental import pallas as pl
from jax.experimental.pallas import tpu as pltpu
from jax.sharding import PartitionSpec as P

BLOCK = 256
LIST = 14
LAYERS = 3
F32 = jnp.float32
BF16 = jnp.bfloat16
ridge_scale = 0.05
gamma = 5.0 / 3.0
HEAD, TAIL, CORNER = 64, 78, 92
MESH = pl.DeviceIdType.MESH
SELF = 13


def iota(shape, dim):
    return lax.broadcasted_iota(jnp.int32, shape, dim)


def split3(value):
    high = value.astype(BF16)
    rest = value - high.astype(F32)
    middle = rest.astype(BF16)
    low = (rest - middle.astype(F32)).astype(BF16)
    return high, middle, low


def prepare(geom, density, velocity, pressure, live, pair, line, place):
    lanes = iota((1, 128), 1)
    total = jnp.zeros((40, 128), F32)
    line[...] = jnp.zeros((8, 128), F32)
    line[0:1, HEAD : HEAD + LIST] = pair[0:1, :].astype(F32)
    line[0:1, TAIL : TAIL + LIST] = pair[1:2, :].astype(F32)
    listed = line[0:1, :]
    for s in range(2):
        at = slice(s * BLOCK, (s + 1) * BLOCK)
        corner = geom[:, at]
        columns = jnp.concatenate([corner, corner], axis=0).T
        cells = []
        for k, count in ((0, 64), (1, 32), (2, 32)):
            smaller = columns[:, k : k + 1] < corner[k : k + 1, :]
            rank = jnp.sum(jnp.where(smaller, 1.0, 0.0), axis=0, keepdims=True)
            cells.append(jnp.floor(rank * (1.0 / count)).astype(jnp.int32))
            low = jnp.min(corner[k : k + 1, :], axis=1, keepdims=True)
            listed = listed + jnp.where(lanes == CORNER + 3 * s + k, low, 0.0)
        lane = cells[0] * 8 + cells[2]
        alive = iota((1, BLOCK), 1) < live[s]
        rows = [corner[0:1], corner[1:2], corner[2:3], jnp.log(density[:, at])]
        rows += [velocity[k : k + 1, at] for k in range(3)]
        rows += [jnp.log(pressure[:, at]), jnp.where(alive, corner[3:4], 0.0)]
        here = iota((8, BLOCK), 0) == cells[1]
        spread = [jnp.where(here, row, 0.0) for row in rows] + [jnp.zeros((8, BLOCK), F32)]
        for par in range(2):
            target = jnp.where(iota((128, BLOCK), 0) == lane + (par * 64 + s * 32), 1.0, 0.0)
            target = target.astype(BF16)
            for part in split3(jnp.concatenate(spread[par::2], axis=0)):
                total = total + lax.dot_general(
                    part, target, (((1,), (1,)), ((), ())), preferred_element_type=F32
                )
        place[0:1, at] = cells[1].astype(F32)
        place[1:2, at] = (cells[0] * 16 + cells[2] + 8 * s).astype(F32)
        place[2:3, at] = jnp.where(alive, 1.0, 0.0)
    return total + jnp.where(iota((40, 128), 0) == 32, listed, 0.0)


def read_lists(chunks, lists, region, group):
    lanes = iota((24, 128), 1)
    kind = (lanes - CORNER) % 3
    scale = jnp.where(kind == 0, 0.25, 0.125)
    weight = jnp.where(kind == 0, 1024.0, jnp.where(kind == 1, 32.0, 1.0))
    own = chunks[32 + group, 32:33, :]
    own = jnp.where(lanes[0:1] >= CORNER + 3, pltpu.roll(own, 3, 1), own)
    first = ((region - 1) * 64).astype(F32)
    whole = jnp.zeros((24, 128), jnp.int32)
    for m in range(4):
        rows = chunks[pl.ds(m, 24, stride=4), 32, :]
        steps = jnp.floor((rows - own) * scale + 0.5) * weight
        steps = steps + pltpu.roll(steps, 127, 1) + pltpu.roll(steps, 126, 1)
        ids = jnp.where(rows < 0.0, -1.0, rows - first)
        rows = jnp.where(lanes < CORNER, ids, steps).astype(jnp.int32)
        rows = jnp.where(lanes == CORNER + 1, region, jnp.where(lanes == CORNER + 2, group, rows))
        whole = jnp.where(lanes // 32 == m, pltpu.roll(rows, (64 + 32 * m) % 128, 1), whole)
    lists[...] = whole


def exchange(
    geom, density, velocity, pressure, live, pair, chunks, place, lists, line,
    x_send, x_recv, z_send, z_recv, r_send, r_recv,
):
    region, group = lax.axis_index("region"), lax.axis_index("group")
    z, x = group // 4, group % 4

    def column(step):
        return (region, z * 4 + (x + step) % 4)

    def plane(step):
        return (region, (z + 8 + step) % 8 * 4 + x)

    def slab(step):
        return ((region + 16 + step) % 16, group)

    partners = [column(k) for k in (1, 2, 3)] + [plane(1), plane(-1), slab(1), slab(-1)]
    barrier = pltpu.get_barrier_semaphore()
    for partner in partners:
        pl.semaphore_signal(barrier, inc=1, device_id=partner, device_id_type=MESH)
    chunks[32 + group] = prepare(geom, density, velocity, pressure, live, pair, line, place)
    pl.semaphore_wait(barrier, len(partners))

    def copy(start, count, to, device, send, recv):
        return pltpu.make_async_remote_copy(
            src_ref=chunks.at[pl.ds(start, count)],
            dst_ref=chunks.at[pl.ds(to, count)],
            send_sem=send,
            recv_sem=recv,
            device_id=device,
            device_id_type=MESH,
        )

    def along_x(k):
        return copy(32 + group, 1, 32 + group, column(k), x_send.at[k - 1], x_recv.at[k - 1])

    def bundle(step):
        return 32 + (z + 16 + step) % 8 * 4

    def along_z(step, t):
        start = bundle(-step * t)
        if t == 3:
            start = start + (0 if step > 0 else 2)
        side = 0 if step > 0 else 1
        count = 2 if t == 3 else 4
        return copy(start, count, start, plane(step), z_send.at[side, t], z_recv.at[side, t])

    def arrived_z(step, t):
        start = bundle(-step * (t + 1))
        if t == 3:
            start = start + (0 if step > 0 else 2)
        side = 0 if step > 0 else 1
        count = 2 if t == 3 else 4
        return copy(start, count, start, plane(step), z_send.at[side, t], z_recv.at[side, t])

    def along_r(step, k):
        side = 0 if step > 0 else 1
        to = bundle(k) + (-32 if step > 0 else 32)
        return copy(bundle(k), 4, to, slab(step), r_send.at[side, k], r_recv.at[side, k])

    def arrived_r(step, k):
        side = 0 if step > 0 else 1
        to = bundle(k) + (-32 if step > 0 else 32)
        return copy(to, 4, to, slab(step), r_send.at[side, k], r_recv.at[side, k])

    def give(k):
        for step in (1, -1):
            along_r(step, k % 8).start()

    for k in (2, 1, 3):
        along_x(k).start()
    for k in (1, 2, 3):
        begin = 32 + z * 4 + (x + 4 - k) % 4
        copy(begin, 1, begin, column(k), x_send.at[k - 1], x_recv.at[k - 1]).wait_recv()
    along_z(1, 0).start()
    along_z(-1, 0).start()
    give(0)
    for t in range(3):
        for step in (1, -1):
            arrived_z(step, t).wait_recv()
            along_z(step, t + 1).start()
            give(-step * (t + 1))
    arrived_z(1, 3).wait_recv()
    arrived_z(-1, 3).wait_recv()
    give(4)
    for k in range(8):
        arrived_r(1, k).wait_recv()
        arrived_r(-1, k).wait_recv()
    read_lists(chunks, lists, region, group)
    for k in (1, 2, 3):
        along_x(k).wait_send()
    for t in range(4):
        along_z(1, t).wait_send()
        along_z(-1, t).wait_send()
    for k in range(8):
        along_r(1, k).wait_send()
        along_r(-1, k).wait_send()


def exchange_call(geom, density, velocity, pressure, live, pair):
    vmem = pl.BlockSpec(memory_space=pltpu.VMEM)
    smem = pl.BlockSpec(memory_space=pltpu.SMEM)
    dma = pltpu.SemaphoreType.DMA
    return pl.pallas_call(
        exchange,
        out_shape=(
            jax.ShapeDtypeStruct((96, 40, 128), F32),
            jax.ShapeDtypeStruct((8, 512), F32),
            jax.ShapeDtypeStruct((24, 128), jnp.int32),
        ),
        in_specs=[vmem, vmem, vmem, vmem, smem, vmem],
        out_specs=(vmem, vmem, vmem),
        scratch_shapes=[
            pltpu.VMEM((8, 128), F32),
            dma((3,)),
            dma((3,)),
            dma((2, 4)),
            dma((2, 4)),
            dma((2, 8)),
            dma((2, 8)),
        ],
        compiler_params=pltpu.CompilerParams(
            collective_id=0, has_side_effects=True, vmem_limit_bytes=16 * 1024 * 1024
        ),
        name="gather_sites",
    )(geom, density[None], velocity, pressure[None], live, pair.T)


def direction(step, wanted):
    u = step + 1057
    a, b, c = u >> 10, (u >> 5) & 31, u & 31
    fits = wanted & (u >= 0) & (jnp.maximum(jnp.maximum(a, b), c) <= 2)
    return jnp.where(fits, a * 9 + b * 3 + c, 27)


def fill_tables(lists, source, used, faces, face_used):
    def clear(k, _):
        source[k] = -1
        return _

    lax.fori_loop(0, 27 * 16, clear, 0, unroll=16)

    def clear_way(k, _):
        used[k] = 0
        face_used[k] = 0
        faces[k] = -1
        faces[28 + k] = -1
        return _

    lax.fori_loop(0, 28, clear_way, 0, unroll=14)
    own = (32 + lists[30]) * 32

    def code(block):
        return lists[(block >> 1) * 32 + 28 + 3 * (block & 1)]

    def slot(p, _):
        head = lists[own + p]
        listed = head >= 0
        tail = jnp.where(listed, lists[own + LIST + p], 64)
        place = code(tail)
        way = direction(place - lists[own + 28 + 3 * (head & 1)], listed)
        faces[(head & 1) * 28 + way] = p
        face_used[way] = 1
        at = (tail >> 1) * 32
        for k in range(LIST):
            there = lists[at + LIST + k]
            near = listed & (lists[at + k] == tail) & (there >= 0) & (there < 192)
            there = jnp.where(near, there, 0)
            towards = direction(code(there) - place, near)
            source[towards * 16 + p] = there
            used[towards] = 1
        return _

    lax.fori_loop(0, LIST, slot, 0)


def swap(low, high, is_low, width):
    first = jnp.where(is_low, low, pltpu.roll(high, width, 1))
    second = jnp.where(is_low, pltpu.roll(low, 128 - width, 1), high)
    return first, second


def collect_sites(chunks, source, used, near):
    group = iota((8, 128), 1) // 8
    bit = [(group >> k) % 2 == 0 for k in range(4)]

    def one_way(way, _):
        @pl.when(used[way] > 0)
        def _present():
            froms = [source[way * 16 + p] for p in range(LIST)]
            there = jnp.zeros((8, 128), jnp.int32)
            second = jnp.zeros((8, 128), jnp.int32)
            for p in range(LIST):
                mask = group == p
                there = jnp.where(mask, jnp.where(froms[p] >= 0, 1, 0), there)
                second = jnp.where(mask, froms[p] & 1, second)
            there, second = there > 0, second > 0
            at = [jnp.maximum(f, 0) >> 1 for f in froms]
            at += [at[0], at[1]]
            for t in range(5):
                v = [chunks[at[p], 8 * t : 8 * t + 8, :] for p in range(16)]
                for k in (0, 1, 3):
                    step = 1 << k
                    for p in range(16):
                        if not p & step:
                            v[p], v[p + step] = swap(v[p], v[p + step], bit[k], 8 * step)
                for n in range(8):
                    par, x = n // 4, n % 4
                    low, high = v[8 * par + x], v[8 * par + x + 4]
                    low = jnp.where(second, pltpu.roll(low, 96, 1), low)
                    high = jnp.where(second, high, pltpu.roll(high, 32, 1))
                    out = jnp.where(there, jnp.where(bit[2], low, high), 0.0)
                    if 2 * t + par == 8:
                        near[way, 9, x] = out
                        out = jnp.where(out > 0.0, 1.0, 0.0)
                    if 2 * t + par < 9:
                        near[way, 2 * t + par, x] = out

        @pl.when(used[way] == 0)
        def _absent():
            near[way] = jnp.zeros((10, 4, 8, 128), F32)

        return _

    lax.fori_loop(0, 27, one_way, 0)


def shifted(base, below, above, z, dz):
    if dz == 0:
        return base
    inside = pltpu.roll(base, (-dz) % 128, 1)
    if dz > 0:
        return jnp.where(z + dz < 8, inside, pltpu.roll(above, 8 - dz, 1))
    return jnp.where(z + dz >= 0, inside, pltpu.roll(below, 128 - 8 - dz, 1))


def shift_sites(near, halo):
    z = iota((8, 128), 1) % 8
    upper = iota((8, 128), 0) < 4

    def one_row(row, _):
        for xe in range(8):
            sx, x = (0, xe + 2) if xe < 2 else (1, xe - 2) if xe < 6 else (2, xe - 6)
            mid = [near[sx * 9 + 3 + sz, row, x] for sz in (1, 0, 2)]
            rim = [
                jnp.where(upper, near[sx * 9 + 6 + sz, row, x], near[sx * 9 + sz, row, x])
                for sz in (1, 0, 2)
            ]
            for dz in range(-2, 3):
                halo[dz + 2, row, xe, 8:16, :] = shifted(*mid, z, dz)
                edge = shifted(*rim, z, dz)
                halo[dz + 2, row, xe, 0:8, :] = edge
                halo[dz + 2, row, xe, 16:24, :] = edge
        return _

    lax.fori_loop(0, 9, one_row, 0)


def moments(near, halo, fields):
    def one_plane(x, _):
        xi, yi, zi = [near[SELF, k, x] for k in range(3)]
        qi = [near[SELF, 3 + k, x] for k in range(5)]
        alive, radius = near[SELF, 8, x], near[SELF, 9, x]
        radius = jnp.where(radius > 0.0, radius, 1.0)
        inverse_radius = 1.0 / radius

        def step(n, sums):
            dz = n // 5
            xe = n % 5 + x
            sums = list(sums)
            for dy in range(-2, 3):
                near_j = [halo[dz, k, xe, 8 + dy : 16 + dy, :] for k in range(9)]
                ox, oy, oz = near_j[0] - xi, near_j[1] - yi, near_j[2] - zi
                square = ox * ox + oy * oy + oz * oz
                scaled = square * lax.rsqrt(jnp.maximum(square, 1e-12)) * inverse_radius
                remain = jnp.maximum(1.0 - scaled, 0.0)
                remain = remain * remain
                w = remain * remain * (1.0 + 4.0 * scaled) * near_j[8]
                wx, wy, wz = w * ox, w * oy, w * oz
                terms = [w, wx * ox, wy * oy, wz * oz, wx * oy, wx * oz, wy * oz]
                for k in range(5):
                    change = near_j[3 + k] - qi[k]
                    terms += [wx * change, wy * change, wz * change]
                sums = [a + b for a, b in zip(sums, terms)]
            return tuple(sums)

        zero = jnp.zeros((8, 128), F32)
        sums = lax.fori_loop(0, 25, step, (zero,) * 22)
        omega = sums[0] + (1.0 - alive)
        per = 1.0 / omega
        shift = ridge_scale * radius * radius
        m = [sums[1 + k] * per for k in range(6)]
        m[0], m[1], m[2] = m[0] + shift, m[1] + shift, m[2] + shift
        c = [
            m[1] * m[2] - m[5] * m[5],
            m[0] * m[2] - m[4] * m[4],
            m[0] * m[1] - m[3] * m[3],
            m[4] * m[5] - m[3] * m[2],
            m[3] * m[5] - m[4] * m[1],
            m[3] * m[4] - m[0] * m[5],
        ]
        over = 1.0 / (m[0] * c[0] + m[3] * c[3] + m[4] * c[4])
        b = [v * over for v in c]
        rows = [xi, yi, zi] + qi + [near[SELF, 9, x]]
        square = per * per
        rows += [v * square for v in b]
        for k in range(5):
            f = [sums[7 + 3 * k + a] * per for a in range(3)]
            rows.append(b[0] * f[0] + b[3] * f[1] + b[4] * f[2])
            rows.append(b[3] * f[0] + b[1] * f[1] + b[5] * f[2])
            rows.append(b[4] * f[0] + b[5] * f[1] + b[2] * f[2])
        at = pl.ds(pl.multiple_of(x * 128, 128), 128)
        for k in range(15):
            pair = jnp.concatenate(rows[2 * k : 2 * k + 2], axis=0)
            for n, part in enumerate(split3(pair)):
                fields[240 * n + 16 * k : 240 * n + 16 * k + 16, at] = part
        return _

    lax.fori_loop(0, 4, one_plane, 0)


def gather_fields(fields, faces, face_used, around):
    lanes = iota((1, 128), 1)
    z = lanes % 8
    sources = iota((128, 128), 0)

    def one_way(n, _):
        sz = n // 3
        sy = n % 3
        any_used = face_used[sy * 3 + sz] + face_used[9 + sy * 3 + sz] + face_used[18 + sy * 3 + sz]

        @pl.when(any_used > 0)
        def _present():
            hot = []
            for x in range(4):
                wanted = jnp.full((1, 128), -1, jnp.int32)
                for sx, xe in ((1, x + 2), (2, x + 6) if x < 2 else (0, x - 2)):
                    for s in range(2):
                        p = faces[s * 28 + sx * 9 + sy * 3 + sz]
                        lane = jnp.where(p >= 0, p * 8 + z, -1)
                        wanted = jnp.where(lanes // 8 == xe * 2 + s, lane, wanted)
                hot.append(jnp.where(sources == wanted, 1.0, 0.0).astype(BF16))
            found = jnp.dot(
                fields[...], jnp.concatenate(hot, axis=0), preferred_element_type=F32
            )
            around[n] = found[0:240] + found[240:480] + found[480:720]

        @pl.when(any_used == 0)
        def _absent():
            around[n] = jnp.zeros((240, 128), F32)

        return _

    lax.fori_loop(0, 9, one_way, 0)


def shift_fields(around, wide, inner):
    lanes = iota((8, 128), 1)
    z = lanes % 8
    outer = (lanes < 16) | (lanes >= 112)
    middle = (lanes >= 32) & (lanes < 96)
    left = lanes < 64
    upper = iota((8, 128), 0) < 4

    def some_rows(n, _):
        for m in range(3):
            row = n * 3 + m
            at = pl.ds(pl.multiple_of(row * 8, 8), 8)
            mid = [around[sz * 3 + 1, at, :] for sz in (1, 0, 2)]
            rim = [
                jnp.where(upper, around[sz * 3 + 2, at, :], around[sz * 3, at, :])
                for sz in (1, 0, 2)
            ]
            for is_rim, parts in ((False, mid), (True, rim)):
                for dz in range(-2, 3):
                    far = shifted(*parts, z, dz)
                    half = pltpu.roll(far, 64, 1)
                    orders = far, jnp.where(outer, half, far), jnp.where(middle, far, half)
                    for k, value in enumerate(orders):
                        if is_rim:
                            wide[dz + 2, k, row, 0:8, :] = value
                            wide[dz + 2, k, row, 16:24, :] = value
                        else:
                            wide[dz + 2, k, row, 8:16, :] = value
                    if dz == 0 and not is_rim:
                        own = orders[2]
                        back, on = pltpu.roll(own, 112, 1), pltpu.roll(own, 16, 1)
                        inner[0, row] = pltpu.roll(own, 32, 1)
                        inner[1, row] = jnp.where(left, back, on)
                        inner[2, row] = own
        return _

    lax.fori_loop(0, 10, some_rows, 0)


def weight(scaled):
    remain = jnp.maximum(1.0 - scaled, 0.0)
    remain = remain * remain
    return remain * remain * (1.0 + 4.0 * scaled)


def side(state, n):
    density, pressure = jnp.exp(state[0]), jnp.exp(state[4])
    v = state[1:4]
    speed = v[0] * n[0] + v[1] * n[1] + v[2] * n[2]
    sound = jnp.exp(0.5 * (state[4] - state[0])) * (gamma**0.5)
    return density, pressure, v[0], v[1], v[2], speed, sound


def face(near, far):
    o = [far(k) - near(k) for k in range(3)]
    square = jnp.maximum(o[0] * o[0] + o[1] * o[1] + o[2] * o[2], 1e-12)
    inverse = lax.rsqrt(square)
    distance = square * inverse
    n = [v * inverse for v in o]
    hi, hj = near(8), far(8)
    live = jnp.minimum(hi, hj) > 0.0
    wi = weight(distance * (1.0 / jnp.where(hi > 0.0, hi, 1.0)))
    wj = weight(distance * (1.0 / jnp.where(hj > 0.0, hj, 1.0)))
    c = [wi * near(9 + k) + wj * far(9 + k) for k in range(6)]
    a = [
        c[0] * o[0] + c[3] * o[1] + c[4] * o[2],
        c[3] * o[0] + c[1] * o[1] + c[5] * o[2],
        c[4] * o[0] + c[5] * o[1] + c[2] * o[2],
    ]
    area = a[0] * a[0] + a[1] * a[1] + a[2] * a[2]
    area = jnp.where(live, jnp.sqrt(area), 0.0)
    left, right = [], []
    for k in range(5):
        gi = near(15 + 3 * k) * o[0] + near(16 + 3 * k) * o[1] + near(17 + 3 * k) * o[2]
        gj = far(15 + 3 * k) * o[0] + far(16 + 3 * k) * o[1] + far(17 + 3 * k) * o[2]
        left.append(near(3 + k) + 0.5 * jnp.tanh(gi))
        right.append(far(3 + k) - 0.5 * jnp.tanh(gj))
    sl, sr = side(left, n), side(right, n)
    slow = jnp.minimum(sl[5] - sl[6], sr[5] - sr[6])
    fast = jnp.maximum(sl[5] + sl[6], sr[5] + sr[6])
    ml, mr = sl[0] * (slow - sl[5]), sr[0] * (fast - sr[5])
    middle = (sr[1] - sl[1] + ml * sl[5] - mr * sr[5]) / (ml - mr)
    from_left = (slow >= 0.0) | (middle >= 0.0)
    density, pressure, v0, v1, v2, speed, _ = [
        jnp.where(from_left, p, q) for p, q in zip(sl, sr)
    ]
    mass, wave = jnp.where(from_left, ml, mr), jnp.where(from_left, slow, fast)
    star = jnp.where(from_left, -slow, fast) > 0.0
    kinetic = 0.5 * (v0 * v0 + v1 * v1 + v2 * v2)
    energy = pressure * (1.0 / (gamma - 1.0)) + density * kinetic
    push = jnp.where(star, wave * mass / (wave - middle), 0.0)
    rest = speed - jnp.where(star, wave, 0.0)
    lift = middle - speed
    flow = density * rest + push
    press = pressure + push * lift
    heat = energy * rest + pressure * speed
    heat = heat + push * (energy / density + lift * (middle + pressure / mass))
    terms = [flow, v0 * flow + press * n[0], v1 * flow + press * n[1], v2 * flow + press * n[2]]
    return [jnp.where(live, t * area, 0.0) for t in terms + [heat]]


def fluxes(wide, inner):
    left = iota((8, 128), 1) < 64

    def add(order, sums, far):
        return tuple(a + b for a, b in zip(sums, face(lambda row: inner[order, row], far)))

    def step(dz, sums):
        sums = list(sums)
        for k in range(2):
            for dy in range(-2, 3):
                sums[k] = add(k, sums[k], lambda row: wide[dz, k, row, 8 + dy : 16 + dy, :])
        for d in (-2, 1):
            sums[2] = add(
                2,
                sums[2],
                lambda row: jnp.where(
                    left, wide[dz, 2, row, 8 + d : 16 + d, :], wide[dz, 2, row, 9 + d : 17 + d, :]
                ),
            )
        return tuple(sums)

    zero = (jnp.zeros((8, 128), F32),) * 5
    two, one, same = lax.fori_loop(0, 5, step, (zero, zero, zero))
    for d in (0, 1):
        same = add(
            2,
            same,
            lambda row: jnp.where(left, wide[d, 2, row, 8:16, :], wide[4 - d, 2, row, 8:16, :]),
        )
    found = []
    for a, b, c in zip(two, one, same):
        total = c + pltpu.roll(a, 32, 1)
        total = total + pltpu.roll(jnp.where(left, b, 0.0), 16, 1)
        total = total + pltpu.roll(jnp.where(left, 0.0, b), 112, 1)
        found.append(-(total + pltpu.roll(total, 64, 1)))
    return found


def sweep(
    lists, chunks, place, gradients, rate, source, used, faces, face_used, near, halo, fields,
    around, wide, inner,
):
    fill_tables(lists, source, used, faces, face_used)
    collect_sites(chunks, source, used, near)
    shift_sites(near, halo)
    moments(near, halo, fields)
    gather_fields(fields, faces, face_used, around)
    shift_fields(around, wide, inner)
    rates = fluxes(wide, inner)
    rows = [wide[2, 0, 15 + k, 8:16, :] for k in range(15)] + rates
    found = jnp.concatenate(rows, axis=0)
    lane = place[1:2, :].astype(jnp.int32) + 32
    hot = jnp.where(iota((128, 512), 0) == lane, 1.0, 0.0).astype(BF16)
    total = jnp.zeros((160, 512), F32)
    for part in split3(found):
        total = total + jnp.dot(part, hot, preferred_element_type=F32)
    here = (iota((8, 512), 0) == place[0:1, :].astype(jnp.int32)) & (place[2:3, :] > 0.0)
    for k in range(20):
        row = jnp.sum(jnp.where(here, total[8 * k : 8 * k + 8], 0.0), axis=0, keepdims=True)
        if k < 15:
            gradients[k : k + 1, :] = row
        else:
            rate[k - 15 : k - 14, :] = row


def sweep_call(lists, chunks, place):
    vmem = pl.BlockSpec(memory_space=pltpu.VMEM)
    smem = pl.BlockSpec(memory_space=pltpu.SMEM)
    return pl.pallas_call(
        sweep,
        out_shape=(jax.ShapeDtypeStruct((15, 512), F32), jax.ShapeDtypeStruct((5, 512), F32)),
        in_specs=[smem, vmem, vmem],
        out_specs=(vmem, vmem),
        scratch_shapes=[
            pltpu.SMEM((28 * 16,), jnp.int32),
            pltpu.SMEM((28,), jnp.int32),
            pltpu.SMEM((56,), jnp.int32),
            pltpu.SMEM((28,), jnp.int32),
            pltpu.VMEM((27, 10, 4, 8, 128), F32),
            pltpu.VMEM((5, 9, 8, 24, 128), F32),
            pltpu.VMEM((720, 512), BF16),
            pltpu.VMEM((9, 240, 128), F32),
            pltpu.VMEM((5, 3, 30, 24, 128), F32),
            pltpu.VMEM((3, 30, 8, 128), F32),
        ],
        compiler_params=pltpu.CompilerParams(vmem_limit_bytes=48 * 1024 * 1024),
        name="sweep",
    )(lists.reshape(24 * 128), chunks, place)


def body(geom, density, velocity, pressure, block_live, pair_list):
    chunks, place, lists = exchange_call(geom, density, velocity, pressure, block_live, pair_list)
    return sweep_call(lists, chunks, place)


def solution(mesh):
    both = ("region", "group")
    return jax.shard_map(
        body,
        mesh=mesh,
        in_specs=(P(None, both), P(both), P(None, both), P(both), P(both), P(both, None)),
        out_specs=(P(None, both), P(None, both)),
        check_vma=False,
    )
```

```python
import functools

import jax
import jax.numpy as jnp
from jax import lax
from jax.experimental import pallas as pl
from jax.experimental.pallas import tpu as pltpu
from jax.sharding import PartitionSpec as P

BLOCK = 256
LIST = 14
LAYERS = 3
F32 = jnp.float32
BF16 = jnp.bfloat16
ridge_scale = 0.05
gamma = 5.0 / 3.0
HEAD, TAIL, CORNER = 64, 78, 92
MESH = pl.DeviceIdType.MESH
SELF = 13


def iota(shape, dim):
    return lax.broadcasted_iota(jnp.int32, shape, dim)


def split3(value):
    high = value.astype(BF16)
    rest = value - high.astype(F32)
    middle = rest.astype(BF16)
    low = (rest - middle.astype(F32)).astype(BF16)
    return high, middle, low


def prepare(values, line, place):
    lanes = iota((1, 128), 1)
    total = jnp.zeros((40, 128), F32)
    line[...] = jnp.zeros((8, 128), F32)
    line[0:1, HEAD : HEAD + LIST] = values[9:10, 0:LIST]
    line[0:1, TAIL : TAIL + LIST] = values[10:11, 0:LIST]
    listed = line[0:1, :]
    for s in range(2):
        at = slice(s * BLOCK, (s + 1) * BLOCK)
        corner = values[0:4, at]
        columns = jnp.concatenate([corner, corner], axis=0).T
        cells = []
        for k, count in ((0, 64), (1, 32), (2, 32)):
            smaller = columns[:, k : k + 1] < corner[k : k + 1, :]
            rank = jnp.sum(jnp.where(smaller, 1.0, 0.0), axis=0, keepdims=True)
            cells.append(jnp.floor(rank * (1.0 / count)).astype(jnp.int32))
            low = jnp.min(corner[k : k + 1, :], axis=1, keepdims=True)
            listed = listed + jnp.where(lanes == CORNER + 3 * s + k, low, 0.0)
        lane = cells[0] * 8 + cells[2]
        alive = iota((1, BLOCK), 1).astype(F32) < values[11:12, s : s + 1]
        rows = [corner[0:1], corner[1:2], corner[2:3], jnp.log(values[4:5, at])]
        rows += [values[5 + k : 6 + k, at] for k in range(3)]
        rows += [jnp.log(values[8:9, at]), jnp.where(alive, corner[3:4], 0.0)]
        here = iota((8, BLOCK), 0) == cells[1]
        spread = [jnp.where(here, row, 0.0) for row in rows] + [jnp.zeros((8, BLOCK), F32)]
        for par in range(2):
            target = jnp.where(iota((128, BLOCK), 0) == lane + (par * 64 + s * 32), 1.0, 0.0)
            target = target.astype(BF16)
            for part in split3(jnp.concatenate(spread[par::2], axis=0)):
                total = total + lax.dot_general(
                    part, target, (((1,), (1,)), ((), ())), preferred_element_type=F32
                )
        place[0:1, at] = cells[1].astype(F32)
        place[1:2, at] = (cells[0] * 16 + cells[2] + 8 * s).astype(F32)
        place[2:3, at] = jnp.where(alive, 1.0, 0.0)
    return total + jnp.where(iota((40, 128), 0) == 32, listed, 0.0)


def read_lists(chunks, lists, region, group):
    lanes = iota((24, 128), 1)
    kind = (lanes - CORNER) % 3
    scale = jnp.where(kind == 0, 0.25, 0.125)
    weight = jnp.where(kind == 0, 1024.0, jnp.where(kind == 1, 32.0, 1.0))
    own = chunks[1, group // 4, group % 4, 32:33, :]
    own = jnp.where(lanes[0:1] >= CORNER + 3, pltpu.roll(own, 3, 1), own)
    first = ((region - 1) * 64).astype(F32)
    whole = jnp.zeros((24, 128), jnp.int32)
    for m in range(4):
        rows = chunks[:, :, m, 32, :].reshape(24, 128)
        steps = jnp.floor((rows - own) * scale + 0.5) * weight
        steps = steps + pltpu.roll(steps, 127, 1) + pltpu.roll(steps, 126, 1)
        ids = jnp.where(rows < 0.0, -1.0, rows - first)
        rows = jnp.where(lanes < CORNER, ids, steps).astype(jnp.int32)
        rows = jnp.where(lanes == CORNER + 1, region, jnp.where(lanes == CORNER + 2, group, rows))
        whole = jnp.where(lanes // 32 == m, pltpu.roll(rows, (64 + 32 * m) % 128, 1), whole)
    lists[...] = whole


STEPS = (1, -1, 2, -2, 3, -3, 4)


def exchange(
    values, chunks, place, lists, line,
    z_send, z_recv, x_send, x_recv, r_send, r_recv,
):
    region, group = lax.axis_index("region"), lax.axis_index("group")
    z, x = group // 4, group % 4

    def column(step):
        return (region, z * 4 + (x + step) % 4)

    def plane(step):
        return (region, (z + 8 + step) % 8 * 4 + x)

    def slab(step):
        return ((region + 16 + step) % 16, group)

    partners = [column(k) for k in (1, 2, 3)] + [plane(k) for k in STEPS] + [slab(1), slab(-1)]
    barrier = pltpu.get_barrier_semaphore()
    for partner in partners:
        pl.semaphore_signal(barrier, inc=1, device_id=partner, device_id_type=MESH)
    chunks[1, z, x] = prepare(values, line, place)
    pl.semaphore_wait(barrier, len(partners))

    def copy(source, target, device, send, recv):
        return pltpu.make_async_remote_copy(
            src_ref=source,
            dst_ref=target,
            send_sem=send,
            recv_sem=recv,
            device_id=device,
            device_id_type=MESH,
        )

    def row(step):
        return (z + 16 + step) % 8

    def along_z(step, arrived=False):
        ref = chunks.at[1, row(-step) if arrived else z, x]
        return copy(ref, ref, plane(step), z_send.at[step % 8], z_recv.at[step % 8])

    def along_x(n, k, arrived=False):
        ref = chunks.at[1, row(n), (x + 4 - k) % 4 if arrived else x]
        return copy(ref, ref, column(k), x_send.at[n % 8, k - 1], x_recv.at[n % 8, k - 1])

    def along_r(step, n, arrived=False):
        side = 0 if step > 0 else 1
        target = chunks.at[2 * side, row(n)]
        source = target if arrived else chunks.at[1, row(n)]
        return copy(source, target, slab(step), r_send.at[side, n % 8], r_recv.at[side, n % 8])

    def spread(n):
        for k in (2, 1, 3):
            along_x(n, k).start()

    def give(n):
        for k in (1, 2, 3):
            along_x(n, k, True).wait_recv()
        for step in (1, -1):
            along_r(step, n).start()

    for step in STEPS:
        along_z(step).start()
    spread(0)
    for step in (-1, 1):
        along_z(-step, True).wait_recv()
        spread(step)
    give(0)
    for far in (2, 3, 4):
        for step in (-far, far) if far < 4 else (4,):
            along_z(-step if far < 4 else 4, True).wait_recv()
            spread(step)
        give(1 - far)
        give(far - 1)
    give(4)
    for n in range(8):
        for step in (1, -1):
            along_r(step, n, True).wait_recv()
    read_lists(chunks, lists, region, group)
    for step in STEPS:
        along_z(step).wait_send()
    for n in range(8):
        for k in (1, 2, 3):
            along_x(n, k).wait_send()
        for step in (1, -1):
            along_r(step, n).wait_send()


def exchange_call(geom, density, velocity, pressure, live, pair):
    vmem = pl.BlockSpec(memory_space=pltpu.VMEM)
    def rows(v, first):
        return jnp.pad(v, ((first, 12 - first - v.shape[0]), (0, 2 * BLOCK - v.shape[1])))

    values = rows(geom, 0) + rows(density[None], 4) + rows(velocity, 5) + rows(pressure[None], 8)
    values = values + rows(pair.T.astype(F32), 9) + rows(live[None].astype(F32), 11)
    dma = pltpu.SemaphoreType.DMA
    chunks, place, lists = pl.pallas_call(
        exchange,
        out_shape=(
            jax.ShapeDtypeStruct((LAYERS, 8, 4, 40, 128), F32),
            jax.ShapeDtypeStruct((8, 512), F32),
            jax.ShapeDtypeStruct((24, 128), jnp.int32),
        ),
        in_specs=[vmem],
        out_specs=(vmem, vmem, vmem),
        scratch_shapes=[
            pltpu.VMEM((8, 128), F32),
            dma((8,)),
            dma((8,)),
            dma((8, 3)),
            dma((8, 3)),
            dma((2, 8)),
            dma((2, 8)),
        ],
        compiler_params=pltpu.CompilerParams(
            collective_id=0, has_side_effects=True, vmem_limit_bytes=16 * 1024 * 1024
        ),
        name="gather_sites",
    )(values)
    return chunks.reshape(LAYERS * 32, 40, 128), place, lists


def direction(step, wanted):
    u = step + 1057
    a, b, c = u >> 10, (u >> 5) & 31, u & 31
    fits = wanted & (u >= 0) & (jnp.maximum(jnp.maximum(a, b), c) <= 2)
    return jnp.where(fits, a * 9 + b * 3 + c, 27)


def fill_tables(lists, source, used, faces, face_used):
    def clear(k, _):
        source[k] = -1
        return _

    lax.fori_loop(0, 27 * 16, clear, 0, unroll=16)

    def clear_way(k, _):
        used[k] = 0
        face_used[k] = 0
        faces[k] = -1
        faces[28 + k] = -1
        return _

    lax.fori_loop(0, 28, clear_way, 0, unroll=14)
    own = (32 + lists[30]) * 32

    def code(block):
        return lists[(block >> 1) * 32 + 28 + 3 * (block & 1)]

    def slot(p, _):
        head = lists[own + p]
        listed = head >= 0
        tail = jnp.where(listed, lists[own + LIST + p], 64)
        place = code(tail)
        way = direction(place - lists[own + 28 + 3 * (head & 1)], listed)
        faces[(head & 1) * 28 + way] = p
        face_used[way] = 1
        at = (tail >> 1) * 32
        for k in range(LIST):
            there = lists[at + LIST + k]
            near = listed & (lists[at + k] == tail) & (there >= 0) & (there < 192)
            there = jnp.where(near, there, 0)
            towards = direction(code(there) - place, near)
            source[towards * 16 + p] = there
            used[towards] = 1
        return _

    lax.fori_loop(0, LIST, slot, 0)


def swap(low, high, is_low, width):
    first = jnp.where(is_low, low, pltpu.roll(high, width, 1))
    second = jnp.where(is_low, pltpu.roll(low, 128 - width, 1), high)
    return first, second


def collect_sites(chunks, source, used, near):
    group = iota((8, 128), 1) // 8
    bit = [(group >> k) % 2 == 0 for k in range(4)]

    def one_way(way, _):
        @pl.when(used[way] > 0)
        def _present():
            froms = [source[way * 16 + p] for p in range(LIST)]
            there = jnp.zeros((8, 128), jnp.int32)
            second = jnp.zeros((8, 128), jnp.int32)
            for p in range(LIST):
                mask = group == p
                there = jnp.where(mask, jnp.where(froms[p] >= 0, 1, 0), there)
                second = jnp.where(mask, froms[p] & 1, second)
            there, second = there > 0, second > 0
            at = [jnp.maximum(f, 0) >> 1 for f in froms]
            at += [at[0], at[1]]
            for t in range(5):
                v = [chunks[at[p], 8 * t : 8 * t + 8, :] for p in range(16)]
                for k in (0, 1, 3):
                    step = 1 << k
                    for p in range(16):
                        if not p & step:
                            v[p], v[p + step] = swap(v[p], v[p + step], bit[k], 8 * step)
                for n in range(8):
                    par, x = n // 4, n % 4
                    low, high = v[8 * par + x], v[8 * par + x + 4]
                    low = jnp.where(second, pltpu.roll(low, 96, 1), low)
                    high = jnp.where(second, high, pltpu.roll(high, 32, 1))
                    out = jnp.where(there, jnp.where(bit[2], low, high), 0.0)
                    if 2 * t + par == 8:
                        near[way, 9, x] = out
                        out = jnp.where(out > 0.0, 1.0, 0.0)
                    if 2 * t + par < 9:
                        near[way, 2 * t + par, x] = out

        @pl.when(used[way] == 0)
        def _absent():
            near[way] = jnp.zeros((10, 4, 8, 128), F32)

        return _

    lax.fori_loop(0, 27, one_way, 0)


def shifted(base, below, above, z, dz):
    if dz == 0:
        return base
    inside = pltpu.roll(base, (-dz) % 128, 1)
    if dz > 0:
        return jnp.where(z + dz < 8, inside, pltpu.roll(above, 8 - dz, 1))
    return jnp.where(z + dz >= 0, inside, pltpu.roll(below, 128 - 8 - dz, 1))


def shift_sites(near, halo):
    z = iota((8, 128), 1) % 8
    upper = iota((8, 128), 0) < 4

    def one_row(row, _):
        for xe in range(8):
            sx, x = (0, xe + 2) if xe < 2 else (1, xe - 2) if xe < 6 else (2, xe - 6)
            mid = [near[sx * 9 + 3 + sz, row, x] for sz in (1, 0, 2)]
            rim = [
                jnp.where(upper, near[sx * 9 + 6 + sz, row, x], near[sx * 9 + sz, row, x])
                for sz in (1, 0, 2)
            ]
            for dz in range(-2, 3):
                halo[dz + 2, row, xe, 8:16, :] = shifted(*mid, z, dz)
                edge = shifted(*rim, z, dz)
                halo[dz + 2, row, xe, 0:8, :] = edge
                halo[dz + 2, row, xe, 16:24, :] = edge
        return _

    lax.fori_loop(0, 9, one_row, 0)


def moments(near, halo, fields):
    def one_plane(x, _):
        xi, yi, zi = [near[SELF, k, x] for k in range(3)]
        qi = [near[SELF, 3 + k, x] for k in range(5)]
        alive, radius = near[SELF, 8, x], near[SELF, 9, x]
        radius = jnp.where(radius > 0.0, radius, 1.0)
        inverse_radius = 1.0 / radius

        def step(n, sums):
            dz = n // 5
            xe = n % 5 + x
            sums = list(sums)
            for dy in range(-2, 3):
                near_j = [halo[dz, k, xe, 8 + dy : 16 + dy, :] for k in range(9)]
                ox, oy, oz = near_j[0] - xi, near_j[1] - yi, near_j[2] - zi
                square = ox * ox + oy * oy + oz * oz
                scaled = square * lax.rsqrt(jnp.maximum(square, 1e-12)) * inverse_radius
                remain = jnp.maximum(1.0 - scaled, 0.0)
                remain = remain * remain
                w = remain * remain * (1.0 + 4.0 * scaled) * near_j[8]
                wx, wy, wz = w * ox, w * oy, w * oz
                terms = [w, wx * ox, wy * oy, wz * oz, wx * oy, wx * oz, wy * oz]
                for k in range(5):
                    change = near_j[3 + k] - qi[k]
                    terms += [wx * change, wy * change, wz * change]
                sums = [a + b for a, b in zip(sums, terms)]
            return tuple(sums)

        zero = jnp.zeros((8, 128), F32)
        sums = lax.fori_loop(0, 25, step, (zero,) * 22)
        omega = sums[0] + (1.0 - alive)
        per = 1.0 / omega
        shift = ridge_scale * radius * radius
        m = [sums[1 + k] * per for k in range(6)]
        m[0], m[1], m[2] = m[0] + shift, m[1] + shift, m[2] + shift
        c = [
            m[1] * m[2] - m[5] * m[5],
            m[0] * m[2] - m[4] * m[4],
            m[0] * m[1] - m[3] * m[3],
            m[4] * m[5] - m[3] * m[2],
            m[3] * m[5] - m[4] * m[1],
            m[3] * m[4] - m[0] * m[5],
        ]
        over = 1.0 / (m[0] * c[0] + m[3] * c[3] + m[4] * c[4])
        b = [v * over for v in c]
        rows = [xi, yi, zi] + qi + [near[SELF, 9, x]]
        square = per * per
        rows += [v * square for v in b]
        for k in range(5):
            f = [sums[7 + 3 * k + a] * per for a in range(3)]
            rows.append(b[0] * f[0] + b[3] * f[1] + b[4] * f[2])
            rows.append(b[3] * f[0] + b[1] * f[1] + b[5] * f[2])
            rows.append(b[4] * f[0] + b[5] * f[1] + b[2] * f[2])
        at = pl.ds(pl.multiple_of(x * 128, 128), 128)
        for k in range(15):
            pair = jnp.concatenate(rows[2 * k : 2 * k + 2], axis=0)
            for n, part in enumerate(split3(pair)):
                fields[240 * n + 16 * k : 240 * n + 16 * k + 16, at] = part
        return _

    lax.fori_loop(0, 4, one_plane, 0)


def gather_fields(fields, faces, face_used, around):
    lanes = iota((1, 128), 1)
    z = lanes % 8
    sources = iota((128, 128), 0)

    def one_way(n, _):
        sz = n // 3
        sy = n % 3
        any_used = face_used[sy * 3 + sz] + face_used[9 + sy * 3 + sz] + face_used[18 + sy * 3 + sz]

        @pl.when(any_used > 0)
        def _present():
            hot = []
            for x in range(4):
                wanted = jnp.full((1, 128), -1, jnp.int32)
                for sx, xe in ((1, x + 2), (2, x + 6) if x < 2 else (0, x - 2)):
                    for s in range(2):
                        p = faces[s * 28 + sx * 9 + sy * 3 + sz]
                        lane = jnp.where(p >= 0, p * 8 + z, -1)
                        wanted = jnp.where(lanes // 8 == xe * 2 + s, lane, wanted)
                hot.append(jnp.where(sources == wanted, 1.0, 0.0).astype(BF16))
            found = jnp.dot(
                fields[...], jnp.concatenate(hot, axis=0), preferred_element_type=F32
            )
            around[n] = found[0:240] + found[240:480] + found[480:720]

        @pl.when(any_used == 0)
        def _absent():
            around[n] = jnp.zeros((240, 128), F32)

        return _

    lax.fori_loop(0, 9, one_way, 0)


def shift_fields(around, wide, inner):
    lanes = iota((8, 128), 1)
    z = lanes % 8
    outer = (lanes < 16) | (lanes >= 112)
    middle = (lanes >= 32) & (lanes < 96)
    left = lanes < 64
    upper = iota((8, 128), 0) < 4

    def some_rows(n, _):
        for m in range(3):
            row = n * 3 + m
            at = pl.ds(pl.multiple_of(row * 8, 8), 8)
            mid = [around[sz * 3 + 1, at, :] for sz in (1, 0, 2)]
            rim = [
                jnp.where(upper, around[sz * 3 + 2, at, :], around[sz * 3, at, :])
                for sz in (1, 0, 2)
            ]
            for is_rim, parts in ((False, mid), (True, rim)):
                for dz in range(-2, 3):
                    far = shifted(*parts, z, dz)
                    half = pltpu.roll(far, 64, 1)
                    orders = far, jnp.where(outer, half, far), jnp.where(middle, far, half)
                    for k, value in enumerate(orders):
                        if is_rim:
                            wide[dz + 2, k, row, 0:8, :] = value
                            wide[dz + 2, k, row, 16:24, :] = value
                        else:
                            wide[dz + 2, k, row, 8:16, :] = value
                    if dz == 0 and not is_rim:
                        own = orders[2]
                        back, on = pltpu.roll(own, 112, 1), pltpu.roll(own, 16, 1)
                        inner[0, row] = pltpu.roll(own, 32, 1)
                        inner[1, row] = jnp.where(left, back, on)
                        inner[2, row] = own
        return _

    lax.fori_loop(0, 10, some_rows, 0)


def weight(scaled):
    remain = jnp.maximum(1.0 - scaled, 0.0)
    remain = remain * remain
    return remain * remain * (1.0 + 4.0 * scaled)


def side(state, n):
    density, pressure = jnp.exp(state[0]), jnp.exp(state[4])
    v = state[1:4]
    speed = v[0] * n[0] + v[1] * n[1] + v[2] * n[2]
    sound = jnp.exp(0.5 * (state[4] - state[0])) * (gamma**0.5)
    return density, pressure, v[0], v[1], v[2], speed, sound


def face(near, far):
    o = [far(k) - near(k) for k in range(3)]
    square = jnp.maximum(o[0] * o[0] + o[1] * o[1] + o[2] * o[2], 1e-12)
    inverse = lax.rsqrt(square)
    distance = square * inverse
    n = [v * inverse for v in o]
    hi, hj = near(8), far(8)
    live = jnp.minimum(hi, hj) > 0.0
    wi = weight(distance * (1.0 / jnp.where(hi > 0.0, hi, 1.0)))
    wj = weight(distance * (1.0 / jnp.where(hj > 0.0, hj, 1.0)))
    c = [wi * near(9 + k) + wj * far(9 + k) for k in range(6)]
    a = [
        c[0] * o[0] + c[3] * o[1] + c[4] * o[2],
        c[3] * o[0] + c[1] * o[1] + c[5] * o[2],
        c[4] * o[0] + c[5] * o[1] + c[2] * o[2],
    ]
    area = a[0] * a[0] + a[1] * a[1] + a[2] * a[2]
    area = jnp.where(live, jnp.sqrt(area), 0.0)
    left, right = [], []
    for k in range(5):
        gi = near(15 + 3 * k) * o[0] + near(16 + 3 * k) * o[1] + near(17 + 3 * k) * o[2]
        gj = far(15 + 3 * k) * o[0] + far(16 + 3 * k) * o[1] + far(17 + 3 * k) * o[2]
        left.append(near(3 + k) + 0.5 * jnp.tanh(gi))
        right.append(far(3 + k) - 0.5 * jnp.tanh(gj))
    sl, sr = side(left, n), side(right, n)
    slow = jnp.minimum(sl[5] - sl[6], sr[5] - sr[6])
    fast = jnp.maximum(sl[5] + sl[6], sr[5] + sr[6])
    ml, mr = sl[0] * (slow - sl[5]), sr[0] * (fast - sr[5])
    middle = (sr[1] - sl[1] + ml * sl[5] - mr * sr[5]) / (ml - mr)
    from_left = (slow >= 0.0) | (middle >= 0.0)
    density, pressure, v0, v1, v2, speed, _ = [
        jnp.where(from_left, p, q) for p, q in zip(sl, sr)
    ]
    mass, wave = jnp.where(from_left, ml, mr), jnp.where(from_left, slow, fast)
    star = jnp.where(from_left, -slow, fast) > 0.0
    kinetic = 0.5 * (v0 * v0 + v1 * v1 + v2 * v2)
    energy = pressure * (1.0 / (gamma - 1.0)) + density * kinetic
    push = jnp.where(star, wave * mass / (wave - middle), 0.0)
    rest = speed - jnp.where(star, wave, 0.0)
    lift = middle - speed
    flow = density * rest + push
    press = pressure + push * lift
    heat = energy * rest + pressure * speed
    heat = heat + push * (energy / density + lift * (middle + pressure / mass))
    terms = [flow, v0 * flow + press * n[0], v1 * flow + press * n[1], v2 * flow + press * n[2]]
    return [jnp.where(live, t * area, 0.0) for t in terms + [heat]]


def fluxes(wide, inner):
    left = iota((8, 128), 1) < 64

    def add(order, sums, far):
        return tuple(a + b for a, b in zip(sums, face(lambda row: inner[order, row], far)))

    def step(dz, sums):
        sums = list(sums)
        for k in range(2):
            for dy in range(-2, 3):
                sums[k] = add(k, sums[k], lambda row: wide[dz, k, row, 8 + dy : 16 + dy, :])
        for d in (-2, 1):
            sums[2] = add(
                2,
                sums[2],
                lambda row: jnp.where(
                    left, wide[dz, 2, row, 8 + d : 16 + d, :], wide[dz, 2, row, 9 + d : 17 + d, :]
                ),
            )
        return tuple(sums)

    zero = (jnp.zeros((8, 128), F32),) * 5
    two, one, same = lax.fori_loop(0, 5, step, (zero, zero, zero))
    for d in (0, 1):
        same = add(
            2,
            same,
            lambda row: jnp.where(left, wide[d, 2, row, 8:16, :], wide[4 - d, 2, row, 8:16, :]),
        )
    found = []
    for a, b, c in zip(two, one, same):
        total = c + pltpu.roll(a, 32, 1)
        total = total + pltpu.roll(jnp.where(left, b, 0.0), 16, 1)
        total = total + pltpu.roll(jnp.where(left, 0.0, b), 112, 1)
        found.append(-(total + pltpu.roll(total, 64, 1)))
    return found


def sweep(
    lists, chunks, place, gradients, rate, source, used, faces, face_used, near, halo, fields,
    around, wide, inner,
):
    fill_tables(lists, source, used, faces, face_used)
    collect_sites(chunks, source, used, near)
    shift_sites(near, halo)
    moments(near, halo, fields)
    gather_fields(fields, faces, face_used, around)
    shift_fields(around, wide, inner)
    rates = fluxes(wide, inner)
    rows = [wide[2, 0, 15 + k, 8:16, :] for k in range(15)] + rates
    found = jnp.concatenate(rows, axis=0)
    lane = place[1:2, :].astype(jnp.int32) + 32
    hot = jnp.where(iota((128, 512), 0) == lane, 1.0, 0.0).astype(BF16)
    total = jnp.zeros((160, 512), F32)
    for part in split3(found):
        total = total + jnp.dot(part, hot, preferred_element_type=F32)
    here = (iota((8, 512), 0) == place[0:1, :].astype(jnp.int32)) & (place[2:3, :] > 0.0)
    for k in range(20):
        row = jnp.sum(jnp.where(here, total[8 * k : 8 * k + 8], 0.0), axis=0, keepdims=True)
        if k < 15:
            gradients[k : k + 1, :] = row
        else:
            rate[k - 15 : k - 14, :] = row


def sweep_call(lists, chunks, place):
    vmem = pl.BlockSpec(memory_space=pltpu.VMEM)
    smem = pl.BlockSpec(memory_space=pltpu.SMEM)
    return pl.pallas_call(
        sweep,
        out_shape=(jax.ShapeDtypeStruct((15, 512), F32), jax.ShapeDtypeStruct((5, 512), F32)),
        in_specs=[smem, vmem, vmem],
        out_specs=(vmem, vmem),
        scratch_shapes=[
            pltpu.SMEM((28 * 16,), jnp.int32),
            pltpu.SMEM((28,), jnp.int32),
            pltpu.SMEM((56,), jnp.int32),
            pltpu.SMEM((28,), jnp.int32),
            pltpu.VMEM((27, 10, 4, 8, 128), F32),
            pltpu.VMEM((5, 9, 8, 24, 128), F32),
            pltpu.VMEM((720, 512), BF16),
            pltpu.VMEM((9, 240, 128), F32),
            pltpu.VMEM((5, 3, 30, 24, 128), F32),
            pltpu.VMEM((3, 30, 8, 128), F32),
        ],
        compiler_params=pltpu.CompilerParams(vmem_limit_bytes=48 * 1024 * 1024),
        name="sweep",
    )(lists.reshape(24 * 128), chunks, place)


def body(geom, density, velocity, pressure, block_live, pair_list):
    chunks, place, lists = exchange_call(geom, density, velocity, pressure, block_live, pair_list)
    return sweep_call(lists, chunks, place)


def solution(mesh):
    both = ("region", "group")
    return jax.shard_map(
        body,
        mesh=mesh,
        in_specs=(P(None, both), P(both), P(None, both), P(both), P(both), P(both, None)),
        out_specs=(P(None, both), P(None, both)),
        check_vma=False,
    )
```

```python
import functools

import jax
import jax.numpy as jnp
from jax import lax
from jax.experimental import pallas as pl
from jax.experimental.pallas import tpu as pltpu
from jax.sharding import PartitionSpec as P

BLOCK = 256
LIST = 14
LAYERS = 3
F32 = jnp.float32
BF16 = jnp.bfloat16
ridge_scale = 0.05
gamma = 5.0 / 3.0
HEAD, TAIL, CORNER = 64, 78, 92
MESH = pl.DeviceIdType.MESH


def iota(shape, dim):
    return lax.broadcasted_iota(jnp.int32, shape, dim)


def split3(value):
    high = value.astype(BF16)
    rest = value - high.astype(F32)
    middle = rest.astype(BF16)
    low = (rest - middle.astype(F32)).astype(BF16)
    return high, middle, low


def prepare(values, line, place):
    lanes = iota((1, 128), 1)
    total = jnp.zeros((40, 128), F32)
    line[...] = jnp.zeros((8, 128), F32)
    line[0:1, HEAD : HEAD + LIST] = values[9:10, 0:LIST]
    line[0:1, TAIL : TAIL + LIST] = values[10:11, 0:LIST]
    listed = line[0:1, :]
    for s in range(2):
        at = slice(s * BLOCK, (s + 1) * BLOCK)
        corner = values[0:4, at]
        columns = jnp.concatenate([corner, corner], axis=0).T
        cells = []
        for k, count in ((0, 64), (1, 32), (2, 32)):
            smaller = columns[:, k : k + 1] < corner[k : k + 1, :]
            rank = jnp.sum(jnp.where(smaller, 1.0, 0.0), axis=0, keepdims=True)
            cells.append(jnp.floor(rank * (1.0 / count)).astype(jnp.int32))
            low = jnp.min(corner[k : k + 1, :], axis=1, keepdims=True)
            listed = listed + jnp.where(lanes == CORNER + 3 * s + k, low, 0.0)
        lane = cells[0] * 8 + cells[2]
        alive = iota((1, BLOCK), 1).astype(F32) < values[11:12, s : s + 1]
        rows = [corner[0:1], corner[1:2], corner[2:3], jnp.log(values[4:5, at])]
        rows += [values[5 + k : 6 + k, at] for k in range(3)]
        rows += [jnp.log(values[8:9, at]), jnp.where(alive, corner[3:4], 0.0)]
        here = iota((8, BLOCK), 0) == cells[1]
        spread = [jnp.where(here, row, 0.0) for row in rows] + [jnp.zeros((8, BLOCK), F32)]
        for par in range(2):
            target = jnp.where(iota((128, BLOCK), 0) == lane + (par * 64 + s * 32), 1.0, 0.0)
            target = target.astype(BF16)
            for part in split3(jnp.concatenate(spread[par::2], axis=0)):
                total = total + lax.dot_general(
                    part, target, (((1,), (1,)), ((), ())), preferred_element_type=F32
                )
        place[0:1, at] = cells[1].astype(F32)
        place[1:2, at] = (cells[0] * 16 + cells[2] + 8 * s).astype(F32)
        place[2:3, at] = jnp.where(alive, 1.0, 0.0)
    return total + jnp.where(iota((40, 128), 0) == 32, listed, 0.0)


def read_lists(chunks, lists, region, group):
    lanes = iota((24, 128), 1)
    kind = (lanes - CORNER) % 3
    scale = jnp.where(kind == 0, 0.25, 0.125)
    weight = jnp.where(kind == 0, 1024.0, jnp.where(kind == 1, 32.0, 1.0))
    own = chunks[1, group // 4, group % 4, 32:33, :]
    own = jnp.where(lanes[0:1] >= CORNER + 3, pltpu.roll(own, 3, 1), own)
    first = ((region - 1) * 64).astype(F32)
    whole = jnp.zeros((24, 128), jnp.int32)
    for m in range(4):
        rows = chunks[:, :, m, 32, :].reshape(24, 128)
        steps = jnp.floor((rows - own) * scale + 0.5) * weight
        steps = steps + pltpu.roll(steps, 127, 1) + pltpu.roll(steps, 126, 1)
        ids = jnp.where(rows < 0.0, -1.0, rows - first)
        rows = jnp.where(lanes < CORNER, ids, steps).astype(jnp.int32)
        rows = jnp.where(lanes == CORNER + 1, region, jnp.where(lanes == CORNER + 2, group, rows))
        whole = jnp.where(lanes // 32 == m, pltpu.roll(rows, (64 + 32 * m) % 128, 1), whole)
    lists[...] = whole


STEPS = (1, -1, 2, -2, 3, -3, 4)


def exchange(
    values, chunks, place, lists, line,
    z_send, z_recv, x_send, x_recv, r_send, r_recv,
):
    region, group = lax.axis_index("region"), lax.axis_index("group")
    z, x = group // 4, group % 4

    def column(step):
        return (region, z * 4 + (x + step) % 4)

    def plane(step):
        return (region, (z + 8 + step) % 8 * 4 + x)

    def slab(step):
        return ((region + 16 + step) % 16, group)

    partners = [column(k) for k in (1, 2, 3)] + [plane(k) for k in STEPS] + [slab(1), slab(-1)]
    barrier = pltpu.get_barrier_semaphore()
    for partner in partners:
        pl.semaphore_signal(barrier, inc=1, device_id=partner, device_id_type=MESH)
    chunks[1, z, x] = prepare(values, line, place)
    pl.semaphore_wait(barrier, len(partners))

    def copy(source, target, device, send, recv):
        return pltpu.make_async_remote_copy(
            src_ref=source,
            dst_ref=target,
            send_sem=send,
            recv_sem=recv,
            device_id=device,
            device_id_type=MESH,
        )

    def row(step):
        return (z + 16 + step) % 8

    def along_z(step, arrived=False):
        ref = chunks.at[1, row(-step) if arrived else z, x]
        return copy(ref, ref, plane(step), z_send.at[step % 8], z_recv.at[step % 8])

    def along_x(n, k, arrived=False):
        ref = chunks.at[1, row(n), (x + 4 - k) % 4 if arrived else x]
        return copy(ref, ref, column(k), x_send.at[n % 8, k - 1], x_recv.at[n % 8, k - 1])

    def along_r(step, n, arrived=False):
        side = 0 if step > 0 else 1
        target = chunks.at[2 * side, row(n)]
        source = target if arrived else chunks.at[1, row(n)]
        return copy(source, target, slab(step), r_send.at[side, n % 8], r_recv.at[side, n % 8])

    def spread(n):
        for k in (2, 1, 3):
            along_x(n, k).start()

    def give(n):
        for k in (1, 2, 3):
            along_x(n, k, True).wait_recv()
        for step in (1, -1):
            along_r(step, n).start()

    for step in STEPS:
        along_z(step).start()
    spread(0)
    for step in (-1, 1):
        along_z(-step, True).wait_recv()
        spread(step)
    give(0)
    for far in (2, 3, 4):
        for step in (-far, far) if far < 4 else (4,):
            along_z(-step if far < 4 else 4, True).wait_recv()
            spread(step)
        give(1 - far)
        give(far - 1)
    give(4)
    for n in range(8):
        for step in (1, -1):
            along_r(step, n, True).wait_recv()
    read_lists(chunks, lists, region, group)
    for step in STEPS:
        along_z(step).wait_send()
    for n in range(8):
        for k in (1, 2, 3):
            along_x(n, k).wait_send()
        for step in (1, -1):
            along_r(step, n).wait_send()


def exchange_call(geom, density, velocity, pressure, live, pair):
    vmem = pl.BlockSpec(memory_space=pltpu.VMEM)
    def rows(v, first):
        return jnp.pad(v, ((first, 12 - first - v.shape[0]), (0, 2 * BLOCK - v.shape[1])))

    values = rows(geom, 0) + rows(density[None], 4) + rows(velocity, 5) + rows(pressure[None], 8)
    values = values + rows(pair.T.astype(F32), 9) + rows(live[None].astype(F32), 11)
    dma = pltpu.SemaphoreType.DMA
    chunks, place, lists = pl.pallas_call(
        exchange,
        out_shape=(
            jax.ShapeDtypeStruct((LAYERS, 8, 4, 40, 128), F32),
            jax.ShapeDtypeStruct((8, 512), F32),
            jax.ShapeDtypeStruct((24, 128), jnp.int32),
        ),
        in_specs=[vmem],
        out_specs=(vmem, vmem, vmem),
        scratch_shapes=[
            pltpu.VMEM((8, 128), F32),
            dma((8,)),
            dma((8,)),
            dma((8, 3)),
            dma((8, 3)),
            dma((2, 8)),
            dma((2, 8)),
        ],
        compiler_params=pltpu.CompilerParams(
            collective_id=0, has_side_effects=True, vmem_limit_bytes=16 * 1024 * 1024
        ),
        name="gather_sites",
    )(values)
    return chunks.reshape(LAYERS * 32, 40, 128), place, lists


def direction(step, wanted):
    u = step + 1057
    a, b, c = u >> 10, (u >> 5) & 31, u & 31
    fits = wanted & (u >= 0) & (jnp.maximum(jnp.maximum(a, b), c) <= 2)
    return jnp.where(fits, a * 9 + b * 3 + c, 27)


def fill_tables(lists, source, used, faces, face_used):
    def clear(k, _):
        source[k] = -1
        return _

    lax.fori_loop(0, 27 * 16, clear, 0, unroll=16)

    def clear_way(k, _):
        used[k] = 0
        face_used[k] = 0
        faces[k] = -1
        faces[28 + k] = -1
        return _

    lax.fori_loop(0, 28, clear_way, 0, unroll=14)
    own = (32 + lists[30]) * 32

    def code(block):
        return lists[(block >> 1) * 32 + 28 + 3 * (block & 1)]

    def slot(p, _):
        head = lists[own + p]
        listed = head >= 0
        tail = jnp.where(listed, lists[own + LIST + p], 64)
        place = code(tail)
        way = direction(place - lists[own + 28 + 3 * (head & 1)], listed)
        faces[(head & 1) * 28 + way] = p
        face_used[way] = 1
        at = (tail >> 1) * 32
        for k in range(LIST):
            there = lists[at + LIST + k]
            near = listed & (lists[at + k] == tail) & (there >= 0) & (there < 192)
            there = jnp.where(near, there, 0)
            towards = direction(code(there) - place, near)
            source[towards * 16 + p] = there
            used[towards] = 1
        return _

    lax.fori_loop(0, LIST, slot, 0)


def swap(low, high, is_low, width):
    first = jnp.where(is_low, low, pltpu.roll(high, width, 1))
    second = jnp.where(is_low, pltpu.roll(low, 128 - width, 1), high)
    return first, second


def collect_sites(chunks, source, used, near):
    lanes = iota((8, 128), 1)
    group = lanes // 8
    bit = [(group >> k) % 2 == 0 for k in range(4)]
    low_y, low_z, low_x = iota((8, 128), 0) < 4, lanes % 8 < 4, (group % 4) < 2

    def choose(sides, mask, value):
        if len(sides) == 1:
            return value(sides[0])
        return jnp.where(mask, value(2), value(0))

    for kind in range(8):
        xs, ys, zs = [(2, 0) if kind & b else (1,) for b in (4, 2, 1)]
        ways = [(sx * 9 + sy * 3 + sz) for sx in xs for sy in ys for sz in zs]
        any_used = sum(used[way] for way in ways)

        @pl.when(any_used > 0)
        def _present():
            froms = {(way, p): source[way * 16 + p] for way in ways for p in range(LIST)}

            def code(way, p):
                f = froms[way, p]
                return jnp.where(f >= 0, 1 + 2 * (f & 1), 0)

            codes = {}
            for sx in xs:
                codes[sx] = jnp.zeros((8, 128), jnp.int32)
                for p in range(LIST):
                    value = choose(
                        ys,
                        low_y,
                        lambda sy: choose(zs, low_z, lambda sz: code(sx * 9 + sy * 3 + sz, p)),
                    )
                    codes[sx] = jnp.where(group == p, value, codes[sx])

            def tile(p, rows):
                def load(sx, sy, sz):
                    return chunks[jnp.maximum(froms[sx * 9 + sy * 3 + sz, p], 0) >> 1, rows, :]

                return choose(
                    xs,
                    low_x,
                    lambda sx: choose(
                        ys, low_y, lambda sy: choose(zs, low_z, lambda sz: load(sx, sy, sz))
                    ),
                )

            for t in range(5):
                v = [tile(p, slice(8 * t, 8 * t + 8)) for p in range(LIST)]
                v += v[:2]
                for k in (0, 1, 3):
                    step = 1 << k
                    for p in range(16):
                        if not p & step:
                            v[p], v[p + step] = swap(v[p], v[p + step], bit[k], 8 * step)
                for n in range(8 if t < 4 else 4):
                    par, x = n // 4, n % 4
                    info = codes[xs[0] if x < 2 else xs[-1]]
                    second = info >= 2
                    low, high = v[8 * par + x], v[8 * par + x + 4]
                    low = jnp.where(second, pltpu.roll(low, 96, 1), low)
                    high = jnp.where(second, high, pltpu.roll(high, 32, 1))
                    out = jnp.where(info > 0, jnp.where(bit[2], low, high), 0.0)
                    if t == 4:
                        if kind == 0:
                            near[0, 9, x] = out
                        out = jnp.where(out > 0.0, 1.0, 0.0)
                    near[kind, 2 * t + par, x] = out

        @pl.when(any_used == 0)
        def _absent():
            near[kind] = jnp.zeros((10, 4, 8, 128), F32)


def shifted(base, outer, z, dz):
    if dz == 0:
        return base
    inside = pltpu.roll(base, (-dz) % 128, 1)
    if dz > 0:
        return jnp.where(z + dz < 8, inside, pltpu.roll(outer, 8 - dz, 1))
    return jnp.where(z + dz >= 0, inside, pltpu.roll(outer, 128 - 8 - dz, 1))


def shift_sites(near, halo):
    z = iota((8, 128), 1) % 8

    def one_row(row, _):
        for xe in range(8):
            mx, x = (4, xe + 2) if xe < 2 else (0, xe - 2) if xe < 6 else (4, xe - 6)
            mid = near[mx, row, x], near[mx + 1, row, x]
            rim = near[mx + 2, row, x], near[mx + 3, row, x]
            for dz in range(-2, 3):
                halo[dz + 2, row, xe, 8:16, :] = shifted(*mid, z, dz)
                edge = shifted(*rim, z, dz)
                halo[dz + 2, row, xe, 0:8, :] = edge
                halo[dz + 2, row, xe, 16:24, :] = edge
        return _

    lax.fori_loop(0, 9, one_row, 0)


def moments(near, halo, fields):
    def one_plane(x, _):
        xi, yi, zi = [near[0, k, x] for k in range(3)]
        qi = [near[0, 3 + k, x] for k in range(5)]
        alive, radius = near[0, 8, x], near[0, 9, x]
        radius = jnp.where(radius > 0.0, radius, 1.0)
        inverse_radius = 1.0 / radius

        def step(dz, dx, steps, sums):
            xe = dx + x
            sums = list(sums)
            for dy in steps:
                near_j = [halo[dz, k, xe, 8 + dy : 16 + dy, :] for k in range(9)]
                ox, oy, oz = near_j[0] - xi, near_j[1] - yi, near_j[2] - zi
                square = ox * ox + oy * oy + oz * oz
                scaled = square * lax.rsqrt(jnp.maximum(square, 1e-12)) * inverse_radius
                remain = jnp.maximum(1.0 - scaled, 0.0)
                remain = remain * remain
                w = remain * remain * (1.0 + 4.0 * scaled) * near_j[8]
                wx, wy, wz = w * ox, w * oy, w * oz
                terms = [w, wx * ox, wy * oy, wz * oz, wx * oy, wx * oz, wy * oz]
                for k in range(5):
                    change = near_j[3 + k] - qi[k]
                    terms += [wx * change, wy * change, wz * change]
                sums = [a + b for a, b in zip(sums, terms)]
            return tuple(sums)

        zero = jnp.zeros((8, 128), F32)
        every, inner = range(-2, 3), range(-1, 2)
        sums = lax.fori_loop(
            0, 15, lambda n, v: step(1 + n // 5, n % 5, every, v), (zero,) * 22
        )
        sums = lax.fori_loop(0, 6, lambda n, v: step(n // 3 * 4, 1 + n % 3, every, v), sums)
        sums = lax.fori_loop(0, 4, lambda n, v: step(n // 2 * 4, n % 2 * 4, inner, v), sums)
        omega = sums[0] + (1.0 - alive)
        per = 1.0 / omega
        shift = ridge_scale * radius * radius
        m = [sums[1 + k] * per for k in range(6)]
        m[0], m[1], m[2] = m[0] + shift, m[1] + shift, m[2] + shift
        c = [
            m[1] * m[2] - m[5] * m[5],
            m[0] * m[2] - m[4] * m[4],
            m[0] * m[1] - m[3] * m[3],
            m[4] * m[5] - m[3] * m[2],
            m[3] * m[5] - m[4] * m[1],
            m[3] * m[4] - m[0] * m[5],
        ]
        over = 1.0 / (m[0] * c[0] + m[3] * c[3] + m[4] * c[4])
        b = [v * over for v in c]
        rows = [xi, yi, zi] + qi + [near[0, 9, x]]
        square = per * per
        rows += [v * square for v in b]
        for k in range(5):
            f = [sums[7 + 3 * k + a] * per for a in range(3)]
            rows.append(b[0] * f[0] + b[3] * f[1] + b[4] * f[2])
            rows.append(b[3] * f[0] + b[1] * f[1] + b[5] * f[2])
            rows.append(b[4] * f[0] + b[5] * f[1] + b[2] * f[2])
        at = pl.ds(pl.multiple_of(x * 128, 128), 128)
        for k in range(15):
            pair = jnp.concatenate(rows[2 * k : 2 * k + 2], axis=0)
            for n, part in enumerate(split3(pair)[: 3 if k < 2 else 2]):
                fields[240 * n + 16 * k : 240 * n + 16 * k + 16, at] = part
        return _

    lax.fori_loop(0, 4, one_plane, 0)


def gather_fields(fields, faces, face_used, around):
    lanes = iota((1, 128), 1)
    z = lanes % 8
    sources = iota((128, 128), 0)

    def hot(sy, zs):
        blocks = []
        for x in range(4):
            wanted = jnp.full((1, 128), -1, jnp.int32)
            for sx, xe in ((1, x + 2), (2, x + 6) if x < 2 else (0, x - 2)):
                for s in range(2):
                    p = [faces[s * 28 + sx * 9 + sy * 3 + sz] for sz in zs]
                    p = p[0] if len(p) == 1 else jnp.where(z < 4, p[0], p[1])
                    lane = jnp.where(p >= 0, p * 8 + z, -1)
                    wanted = jnp.where(lanes // 8 == xe * 2 + s, lane, wanted)
            blocks.append(jnp.where(sources == wanted, 1.0, 0.0).astype(BF16))
        return jnp.concatenate(blocks, axis=0)

    def pick(columns):
        found = jnp.dot(
            fields[...], jnp.concatenate(columns, axis=1), preferred_element_type=F32
        )
        first = found[0:32] + found[240:272] + found[480:512]
        return jnp.concatenate([first, found[32:240] + found[272:480]], axis=0)

    low_y = iota((240, 128), 0) % 8 < 4
    found = pick([hot(1, (1,)), hot(1, (2, 0)), hot(0, (1,)), hot(2, (1,))])
    around[0] = found[:, 0:128]
    around[1] = found[:, 128:256]
    around[2] = jnp.where(low_y, found[:, 384:512], found[:, 256:384])
    corner = [face_used[sx * 9 + sy * 3 + sz] for sx in range(3) for sy in (0, 2) for sz in (0, 2)]
    any_corner = sum(corner)

    @pl.when(any_corner > 0)
    def _present():
        found = pick([hot(0, (2, 0)), hot(2, (2, 0))])
        around[3] = jnp.where(low_y, found[:, 128:256], found[:, 0:128])

    @pl.when(any_corner == 0)
    def _absent():
        around[3] = jnp.zeros((240, 128), F32)


def shift_fields(around, wide, inner):
    lanes = iota((8, 128), 1)
    z = lanes % 8
    outer = (lanes < 16) | (lanes >= 112)
    middle = (lanes >= 32) & (lanes < 96)
    left = lanes < 64

    def some_rows(n, _):
        for m in range(3):
            row = n * 3 + m
            at = pl.ds(pl.multiple_of(row * 8, 8), 8)
            for is_rim in (False, True):
                parts = around[2 * is_rim, at, :], around[2 * is_rim + 1, at, :]
                for dz in range(-2, 3):
                    far = shifted(*parts, z, dz)
                    half = pltpu.roll(far, 64, 1)
                    orders = far, jnp.where(outer, half, far), jnp.where(middle, far, half)
                    for k, value in enumerate(orders):
                        if is_rim:
                            wide[dz + 2, k, row, 0:8, :] = value
                            wide[dz + 2, k, row, 16:24, :] = value
                        else:
                            wide[dz + 2, k, row, 8:16, :] = value
                    if dz == 0 and not is_rim:
                        own = orders[2]
                        back, on = pltpu.roll(own, 112, 1), pltpu.roll(own, 16, 1)
                        inner[0, row] = pltpu.roll(own, 32, 1)
                        inner[1, row] = jnp.where(left, back, on)
                        inner[2, row] = own
        return _

    lax.fori_loop(0, 10, some_rows, 0)


def weight(scaled):
    remain = jnp.maximum(1.0 - scaled, 0.0)
    remain = remain * remain
    return remain * remain * (1.0 + 4.0 * scaled)


def side(state, n):
    density, pressure = jnp.exp(state[0]), jnp.exp(state[4])
    v = state[1:4]
    speed = v[0] * n[0] + v[1] * n[1] + v[2] * n[2]
    sound = jnp.exp(0.5 * (state[4] - state[0])) * (gamma**0.5)
    return density, pressure, v[0], v[1], v[2], speed, sound


def face(near, far):
    o = [far(k) - near(k) for k in range(3)]
    square = jnp.maximum(o[0] * o[0] + o[1] * o[1] + o[2] * o[2], 1e-12)
    inverse = lax.rsqrt(square)
    distance = square * inverse
    n = [v * inverse for v in o]
    hi, hj = near(8), far(8)
    live = jnp.minimum(hi, hj) > 0.0
    wi = weight(distance * (1.0 / jnp.where(hi > 0.0, hi, 1.0)))
    wj = weight(distance * (1.0 / jnp.where(hj > 0.0, hj, 1.0)))
    c = [wi * near(9 + k) + wj * far(9 + k) for k in range(6)]
    a = [
        c[0] * o[0] + c[3] * o[1] + c[4] * o[2],
        c[3] * o[0] + c[1] * o[1] + c[5] * o[2],
        c[4] * o[0] + c[5] * o[1] + c[2] * o[2],
    ]
    area = a[0] * a[0] + a[1] * a[1] + a[2] * a[2]
    area = jnp.where(live, jnp.sqrt(area), 0.0)
    left, right = [], []
    for k in range(5):
        gi = near(15 + 3 * k) * o[0] + near(16 + 3 * k) * o[1] + near(17 + 3 * k) * o[2]
        gj = far(15 + 3 * k) * o[0] + far(16 + 3 * k) * o[1] + far(17 + 3 * k) * o[2]
        left.append(near(3 + k) + 0.5 * jnp.tanh(gi))
        right.append(far(3 + k) - 0.5 * jnp.tanh(gj))
    sl, sr = side(left, n), side(right, n)
    slow = jnp.minimum(sl[5] - sl[6], sr[5] - sr[6])
    fast = jnp.maximum(sl[5] + sl[6], sr[5] + sr[6])
    ml, mr = sl[0] * (slow - sl[5]), sr[0] * (fast - sr[5])
    middle = (sr[1] - sl[1] + ml * sl[5] - mr * sr[5]) / (ml - mr)
    from_left = (slow >= 0.0) | (middle >= 0.0)
    density, pressure, v0, v1, v2, speed, _ = [
        jnp.where(from_left, p, q) for p, q in zip(sl, sr)
    ]
    mass, wave = jnp.where(from_left, ml, mr), jnp.where(from_left, slow, fast)
    star = jnp.where(from_left, -slow, fast) > 0.0
    kinetic = 0.5 * (v0 * v0 + v1 * v1 + v2 * v2)
    energy = pressure * (1.0 / (gamma - 1.0)) + density * kinetic
    push = jnp.where(star, wave * mass / (wave - middle), 0.0)
    rest = speed - jnp.where(star, wave, 0.0)
    lift = middle - speed
    flow = density * rest + push
    press = pressure + push * lift
    heat = energy * rest + pressure * speed
    heat = heat + push * (energy / density + lift * (middle + pressure / mass))
    terms = [flow, v0 * flow + press * n[0], v1 * flow + press * n[1], v2 * flow + press * n[2]]
    return [jnp.where(live, t * area, 0.0) for t in terms + [heat]]


def fluxes(wide, inner):
    left = iota((8, 128), 1) < 64

    def add(order, sums, far):
        return tuple(a + b for a, b in zip(sums, face(lambda row: inner[order, row], far)))

    def step(dz, reach, sums):
        sums = list(sums)
        for k in range(2):
            for dy in range(-2, 3) if k else range(-reach, reach + 1):
                sums[k] = add(k, sums[k], lambda row: wide[dz, k, row, 8 + dy : 16 + dy, :])
        for d in (-2, 1):
            sums[2] = add(
                2,
                sums[2],
                lambda row: jnp.where(
                    left, wide[dz, 2, row, 8 + d : 16 + d, :], wide[dz, 2, row, 9 + d : 17 + d, :]
                ),
            )
        return tuple(sums)

    zero = (jnp.zeros((8, 128), F32),) * 5
    sums = lax.fori_loop(1, 4, lambda dz, v: step(dz, 2, v), (zero, zero, zero))
    two, one, same = lax.fori_loop(0, 2, lambda n, v: step(4 * n, 1, v), sums)
    for d in (0, 1):
        same = add(
            2,
            same,
            lambda row: jnp.where(left, wide[d, 2, row, 8:16, :], wide[4 - d, 2, row, 8:16, :]),
        )
    found = []
    for a, b, c in zip(two, one, same):
        total = c + pltpu.roll(a, 32, 1)
        total = total + pltpu.roll(jnp.where(left, b, 0.0), 16, 1)
        total = total + pltpu.roll(jnp.where(left, 0.0, b), 112, 1)
        found.append(-(total + pltpu.roll(total, 64, 1)))
    return found


def sweep(
    lists, chunks, place, gradients, rate, source, used, faces, face_used, near, halo, fields,
    around, wide, inner,
):
    fill_tables(lists, source, used, faces, face_used)
    collect_sites(chunks, source, used, near)
    shift_sites(near, halo)
    moments(near, halo, fields)
    gather_fields(fields, faces, face_used, around)
    shift_fields(around, wide, inner)
    rates = fluxes(wide, inner)
    rows = [wide[2, 0, 15 + k, 8:16, :] for k in range(15)] + rates
    found = jnp.concatenate(rows, axis=0)
    lane = place[1:2, :].astype(jnp.int32) + 32
    hot = jnp.where(iota((128, 512), 0) == lane, 1.0, 0.0).astype(BF16)
    total = jnp.zeros((160, 512), F32)
    for part in split3(found):
        total = total + jnp.dot(part, hot, preferred_element_type=F32)
    here = (iota((8, 512), 0) == place[0:1, :].astype(jnp.int32)) & (place[2:3, :] > 0.0)
    for k in range(20):
        row = jnp.sum(jnp.where(here, total[8 * k : 8 * k + 8], 0.0), axis=0, keepdims=True)
        if k < 15:
            gradients[k : k + 1, :] = row
        else:
            rate[k - 15 : k - 14, :] = row


def sweep_call(lists, chunks, place):
    vmem = pl.BlockSpec(memory_space=pltpu.VMEM)
    smem = pl.BlockSpec(memory_space=pltpu.SMEM)
    return pl.pallas_call(
        sweep,
        out_shape=(jax.ShapeDtypeStruct((15, 512), F32), jax.ShapeDtypeStruct((5, 512), F32)),
        in_specs=[smem, vmem, vmem],
        out_specs=(vmem, vmem),
        scratch_shapes=[
            pltpu.SMEM((28 * 16,), jnp.int32),
            pltpu.SMEM((28,), jnp.int32),
            pltpu.SMEM((56,), jnp.int32),
            pltpu.SMEM((28,), jnp.int32),
            pltpu.VMEM((8, 10, 4, 8, 128), F32),
            pltpu.VMEM((5, 9, 8, 24, 128), F32),
            pltpu.VMEM((512, 512), BF16),
            pltpu.VMEM((4, 240, 128), F32),
            pltpu.VMEM((5, 3, 30, 24, 128), F32),
            pltpu.VMEM((3, 30, 8, 128), F32),
        ],
        compiler_params=pltpu.CompilerParams(vmem_limit_bytes=48 * 1024 * 1024),
        name="sweep",
    )(lists.reshape(24 * 128), chunks, place)


def body(geom, density, velocity, pressure, block_live, pair_list):
    chunks, place, lists = exchange_call(geom, density, velocity, pressure, block_live, pair_list)
    return sweep_call(lists, chunks, place)


def solution(mesh):
    both = ("region", "group")
    return jax.shard_map(
        body,
        mesh=mesh,
        in_specs=(P(None, both), P(both), P(None, both), P(both), P(both), P(both, None)),
        out_specs=(P(None, both), P(None, both)),
        check_vma=False,
    )
```

```python
import functools

import jax
import jax.numpy as jnp
from jax import lax
from jax.experimental import pallas as pl
from jax.experimental.pallas import tpu as pltpu
from jax.sharding import PartitionSpec as P

BLOCK = 256
LIST = 14
LAYERS = 3
F32 = jnp.float32
BF16 = jnp.bfloat16
ridge_scale = 0.05
gamma = 5.0 / 3.0
HEAD, TAIL, CORNER = 64, 78, 92
MESH = pl.DeviceIdType.MESH


def iota(shape, dim):
    return lax.broadcasted_iota(jnp.int32, shape, dim)


def split3(value):
    high = value.astype(BF16)
    rest = value - high.astype(F32)
    middle = rest.astype(BF16)
    low = (rest - middle.astype(F32)).astype(BF16)
    return high, middle, low


def order_key(heads, index):
    parity = (heads - 2.0 * jnp.floor(heads * 0.5)).astype(jnp.int32)
    return jnp.where((heads >= 0.0) & (index < LIST), parity, 2)


def prepare(values, place):
    lanes = iota((1, 128), 1)
    total = jnp.zeros((40, 128), F32)
    both = jnp.concatenate([values[8:12, 0:128], values[8:12, 0:128]], axis=0).T[0:16]
    kinds = [order_key(values[9:10, 0:128], lanes), order_key(both[:, 1:2], iota((16, 1), 0))]
    here, there = iota((16, 128), 1), iota((16, 128), 0)
    ahead = (kinds[0] < kinds[1]) | ((kinds[0] == kinds[1]) & (here < there))
    ahead = jnp.where(ahead & (here < LIST), 1.0, 0.0)
    rank = jnp.sum(ahead, axis=1, keepdims=True).astype(jnp.int32)
    listed = jnp.where((here == TAIL + rank) & (there < LIST), both[:, 2:3], 0.0)
    listed = jnp.sum(listed, axis=0, keepdims=True)
    for s in range(2):
        count = jnp.sum(jnp.where(kinds[0] == s, 1.0, 0.0), axis=1, keepdims=True)
        listed = listed + jnp.where(lanes == HEAD + s, count, 0.0)
    for s in range(2):
        at = slice(s * BLOCK, (s + 1) * BLOCK)
        corner = values[0:4, at]
        columns = jnp.concatenate([corner, corner], axis=0).T
        cells = []
        for k, count in ((0, 64), (1, 32), (2, 32)):
            smaller = columns[:, k : k + 1] < corner[k : k + 1, :]
            rank = jnp.sum(jnp.where(smaller, 1.0, 0.0), axis=0, keepdims=True)
            cells.append(jnp.floor(rank * (1.0 / count)).astype(jnp.int32))
            low = jnp.min(corner[k : k + 1, :], axis=1, keepdims=True)
            listed = listed + jnp.where(lanes == CORNER + 3 * s + k, low, 0.0)
        lane = cells[0] * 8 + cells[2]
        alive = iota((1, BLOCK), 1).astype(F32) < values[11:12, s : s + 1]
        rows = [corner[0:1], corner[1:2], corner[2:3], jnp.log(values[4:5, at])]
        rows += [values[5 + k : 6 + k, at] for k in range(3)]
        rows += [jnp.log(values[8:9, at]), jnp.where(alive, corner[3:4], 0.0)]
        here = iota((8, BLOCK), 0) == cells[1]
        spread = [jnp.where(here, row, 0.0) for row in rows] + [jnp.zeros((8, BLOCK), F32)]
        for par in range(2):
            target = jnp.where(iota((128, BLOCK), 0) == lane + (par * 64 + s * 32), 1.0, 0.0)
            target = target.astype(BF16)
            for part in split3(jnp.concatenate(spread[par::2], axis=0)):
                total = total + lax.dot_general(
                    part, target, (((1,), (1,)), ((), ())), preferred_element_type=F32
                )
        place[0:1, at] = cells[1].astype(F32)
        place[1:2, at] = (cells[0] * 16 + cells[2] + 8 * s).astype(F32)
        place[2:3, at] = jnp.where(alive, 1.0, 0.0)
    return total + jnp.where(iota((40, 128), 0) == 32, listed, 0.0)


def read_lists(chunks, lists, region, group):
    lanes = iota((24, 128), 1)
    kind = (lanes - CORNER) % 3
    scale = jnp.where(kind == 0, 0.25, 0.125)
    weight = jnp.where(kind == 0, 1024.0, jnp.where(kind == 1, 32.0, 1.0))
    own = chunks[1, group // 4, group % 4, 32:33, :]
    own = jnp.where(lanes[0:1] >= CORNER + 3, pltpu.roll(own, 3, 1), own)
    first = ((region - 1) * 64).astype(F32)
    whole = jnp.zeros((24, 128), jnp.int32)
    for m in range(4):
        rows = chunks[:, :, m, 32, :].reshape(24, 128)
        steps = jnp.floor((rows - own) * scale + 0.5) * weight
        steps = steps + pltpu.roll(steps, 127, 1) + pltpu.roll(steps, 126, 1)
        ids = jnp.where(lanes < TAIL, rows, rows - first)
        rows = jnp.where(lanes < CORNER, ids, steps).astype(jnp.int32)
        rows = jnp.where(lanes == CORNER + 1, region, jnp.where(lanes == CORNER + 2, group, rows))
        whole = jnp.where(lanes // 32 == m, pltpu.roll(rows, (64 + 32 * m) % 128, 1), whole)
    lists[...] = whole


STEPS = (1, -1, 2, -2, 3, -3, 4)


def exchange(
    values, chunks, place, lists,
    z_send, z_recv, x_send, x_recv, r_send, r_recv,
):
    region, group = lax.axis_index("region"), lax.axis_index("group")
    z, x = group // 4, group % 4

    def column(step):
        return (region, z * 4 + (x + step) % 4)

    def plane(step):
        return (region, (z + 8 + step) % 8 * 4 + x)

    def slab(step):
        return ((region + 16 + step) % 16, group)

    partners = [column(k) for k in (1, 2, 3)] + [plane(k) for k in STEPS] + [slab(1), slab(-1)]
    barrier = pltpu.get_barrier_semaphore()
    for partner in partners:
        pl.semaphore_signal(barrier, inc=1, device_id=partner, device_id_type=MESH)
    chunks[1, z, x] = prepare(values, place)
    pl.semaphore_wait(barrier, len(partners))

    def copy(source, target, device, send, recv):
        return pltpu.make_async_remote_copy(
            src_ref=source,
            dst_ref=target,
            send_sem=send,
            recv_sem=recv,
            device_id=device,
            device_id_type=MESH,
        )

    def row(step):
        return (z + 16 + step) % 8

    def along_z(step, arrived=False):
        ref = chunks.at[1, row(-step) if arrived else z, x]
        return copy(ref, ref, plane(step), z_send.at[step % 8], z_recv.at[step % 8])

    def along_x(n, k, arrived=False):
        ref = chunks.at[1, row(n), (x + 4 - k) % 4 if arrived else x]
        return copy(ref, ref, column(k), x_send.at[n % 8, k - 1], x_recv.at[n % 8, k - 1])

    def along_r(step, n, arrived=False):
        side = 0 if step > 0 else 1
        target = chunks.at[2 * side, row(n)]
        source = target if arrived else chunks.at[1, row(n)]
        return copy(source, target, slab(step), r_send.at[side, n % 8], r_recv.at[side, n % 8])

    def spread(n):
        for k in (2, 1, 3):
            along_x(n, k).start()

    def give(n):
        for k in (1, 2, 3):
            along_x(n, k, True).wait_recv()
        for step in (1, -1):
            along_r(step, n).start()

    for step in STEPS:
        along_z(step).start()
    spread(0)
    for step in (-1, 1):
        along_z(-step, True).wait_recv()
        spread(step)
    give(0)
    for far in (2, 3, 4):
        for step in (-far, far) if far < 4 else (4,):
            along_z(-step if far < 4 else 4, True).wait_recv()
            spread(step)
        give(1 - far)
        give(far - 1)
    give(4)
    for n in range(8):
        for step in (1, -1):
            along_r(step, n, True).wait_recv()
    read_lists(chunks, lists, region, group)
    for step in STEPS:
        along_z(step).wait_send()
    for n in range(8):
        for k in (1, 2, 3):
            along_x(n, k).wait_send()
        for step in (1, -1):
            along_r(step, n).wait_send()


def exchange_call(geom, density, velocity, pressure, live, pair):
    vmem = pl.BlockSpec(memory_space=pltpu.VMEM)
    def rows(v, first):
        return jnp.pad(v, ((first, 12 - first - v.shape[0]), (0, 2 * BLOCK - v.shape[1])))

    values = rows(geom, 0) + rows(density[None], 4) + rows(velocity, 5) + rows(pressure[None], 8)
    values = values + rows(pair.T.astype(F32), 9) + rows(live[None].astype(F32), 11)
    dma = pltpu.SemaphoreType.DMA
    chunks, place, lists = pl.pallas_call(
        exchange,
        out_shape=(
            jax.ShapeDtypeStruct((LAYERS, 8, 4, 40, 128), F32),
            jax.ShapeDtypeStruct((8, 512), F32),
            jax.ShapeDtypeStruct((24, 128), jnp.int32),
        ),
        in_specs=[vmem],
        out_specs=(vmem, vmem, vmem),
        scratch_shapes=[
            dma((8,)),
            dma((8,)),
            dma((8, 3)),
            dma((8, 3)),
            dma((2, 8)),
            dma((2, 8)),
        ],
        compiler_params=pltpu.CompilerParams(
            collective_id=0, has_side_effects=True, vmem_limit_bytes=16 * 1024 * 1024
        ),
        name="gather_sites",
    )(values)
    return chunks.reshape(LAYERS * 32, 40, 128), place, lists


def direction(step, wanted):
    u = step + 1057
    a, b, c = u >> 10, (u >> 5) & 31, u & 31
    fits = wanted & (u >= 0) & (jnp.maximum(jnp.maximum(a, b), c) <= 2)
    return jnp.where(fits, a * 9 + b * 3 + c, 27)


def fill_tables(lists, source, used, faces, face_used):
    def clear(k, _):
        source[k] = -1
        return _

    lax.fori_loop(0, 27 * 16, clear, 0, unroll=16)

    def clear_way(k, _):
        used[k] = 0
        face_used[k] = 0
        faces[k] = -1
        faces[28 + k] = -1
        return _

    lax.fori_loop(0, 28, clear_way, 0, unroll=14)
    own = (32 + lists[30]) * 32

    def code(block):
        return lists[(block >> 1) * 32 + 28 + 3 * (block & 1)]

    def slot(p, _):
        first, second = lists[own], lists[own + 1]
        listed = p < first + second
        odd = jnp.where(p < first, 0, 1)
        tail = jnp.where(listed, lists[own + LIST + p], 64)
        place = code(tail)
        way = direction(place - lists[own + 28 + 3 * odd], listed)
        faces[odd * 28 + way] = p
        face_used[way] = 1
        at = (tail >> 1) * 32
        other = tail & 1
        count = jnp.where(listed, jnp.where(other == 0, lists[at], lists[at + 1]), 0)
        start = at + LIST + jnp.where(other == 0, 0, lists[at])

        def entry(k):
            near = k < count
            there = lists[jnp.where(near, start + k, at)]
            near = near & (there >= 0) & (there < 192)
            there = jnp.where(near, there, 0)
            towards = direction(code(there) - place, near)
            source[towards * 16 + p] = there
            used[towards] = 1

        for k in range(LIST // 2):
            entry(k)

        @pl.when(count > LIST // 2)
        def _more():
            for k in range(LIST // 2, LIST):
                entry(k)

        return _

    lax.fori_loop(0, LIST, slot, 0)


def swap(low, high, is_low, width):
    first = jnp.where(is_low, low, pltpu.roll(high, width, 1))
    second = jnp.where(is_low, pltpu.roll(low, 128 - width, 1), high)
    return first, second


def collect_sites(chunks, source, used, near):
    lanes = iota((8, 128), 1)
    group = lanes // 8
    bit = [(group >> k) % 2 == 0 for k in range(4)]
    low_y, low_z, low_x = iota((8, 128), 0) < 4, lanes % 8 < 4, (group % 4) < 2

    def choose(sides, mask, value):
        if len(sides) == 1:
            return value(sides[0])
        return jnp.where(mask, value(2), value(0))

    for kind in range(8):
        xs, ys, zs = [(2, 0) if kind & b else (1,) for b in (4, 2, 1)]
        ways = [(sx * 9 + sy * 3 + sz) for sx in xs for sy in ys for sz in zs]
        any_used = sum(used[way] for way in ways)

        @pl.when(any_used > 0)
        def _present():
            froms = {(way, p): source[way * 16 + p] for way in ways for p in range(LIST)}

            def code(way, p):
                f = froms[way, p]
                return jnp.where(f >= 0, 1 + 2 * (f & 1), 0)

            codes = {}
            for sx in xs:
                codes[sx] = jnp.zeros((8, 128), jnp.int32)
                for p in range(LIST):
                    value = choose(
                        ys,
                        low_y,
                        lambda sy: choose(zs, low_z, lambda sz: code(sx * 9 + sy * 3 + sz, p)),
                    )
                    codes[sx] = jnp.where(group == p, value, codes[sx])

            def tile(p, rows):
                def load(sx, sy, sz):
                    return chunks[jnp.maximum(froms[sx * 9 + sy * 3 + sz, p], 0) >> 1, rows, :]

                return choose(
                    xs,
                    low_x,
                    lambda sx: choose(
                        ys, low_y, lambda sy: choose(zs, low_z, lambda sz: load(sx, sy, sz))
                    ),
                )

            def one_tile(t, _):
                v = [tile(p, pl.ds(t * 8, 8)) for p in range(LIST)]
                v += v[:2]
                for k in (0, 1, 3):
                    step = 1 << k
                    for p in range(16):
                        if not p & step:
                            v[p], v[p + step] = swap(v[p], v[p + step], bit[k], 8 * step)
                for n in range(8):
                    par, x = n // 4, n % 4
                    info = codes[xs[0] if x < 2 else xs[-1]]
                    second = info >= 2
                    low, high = v[8 * par + x], v[8 * par + x + 4]
                    low = jnp.where(second, pltpu.roll(low, 96, 1), low)
                    high = jnp.where(second, high, pltpu.roll(high, 32, 1))
                    out = jnp.where(info > 0, jnp.where(bit[2], low, high), 0.0)
                    near[kind, 2 * t + par, x] = out
                return _

            if kind in (0, 1, 2, 4):
                for t in range(5):
                    one_tile(t, 0)
            else:
                lax.fori_loop(0, 5, one_tile, 0)
            for x in range(4):
                radius = near[kind, 8, x]
                near[kind, 9, x] = radius
                near[kind, 8, x] = jnp.where(radius > 0.0, 1.0, 0.0)

        @pl.when(any_used == 0)
        def _absent():
            near[kind] = jnp.zeros((10, 4, 8, 128), F32)


def shifted(base, outer, z, dz):
    if dz == 0:
        return base
    inside = pltpu.roll(base, (-dz) % 128, 1)
    if dz > 0:
        return jnp.where(z + dz < 8, inside, pltpu.roll(outer, 8 - dz, 1))
    return jnp.where(z + dz >= 0, inside, pltpu.roll(outer, 128 - 8 - dz, 1))


def rim_rows(dy):
    row = iota((8, 128), 0)
    return row < dy if dy > 0 else row >= 8 + dy


def across(dy, edge, middle):
    return middle if dy == 0 else jnp.where(rim_rows(dy), edge, middle)


def shift_sites(near, halo):
    z = iota((8, 128), 1) % 8

    def one_row(row, _):
        for xe in range(8):
            mx, x = (4, xe + 2) if xe < 2 else (0, xe - 2) if xe < 6 else (4, xe - 6)
            mid = near[mx, row, x], near[mx + 1, row, x]
            rim = near[mx + 2, row, x], near[mx + 3, row, x]
            for dz in range(-2, 3):
                middle, edge = shifted(*mid, z, dz), shifted(*rim, z, dz)
                for dy in range(-2, 3):
                    halo[dz + 2, dy + 2, row, xe] = across(dy, edge, middle)
        return _

    lax.fori_loop(0, 9, one_row, 0, unroll=3)


def moments(near, halo, fields, spin, turn):
    def one_plane(x, _):
        xi, yi, zi = [near[0, k, x] for k in range(3)]
        qi = [near[0, 3 + k, x] for k in range(5)]
        alive, radius = near[0, 8, x], near[0, 9, x]
        radius = jnp.where(radius > 0.0, radius, 1.0)
        for k, value in enumerate([xi, yi, zi] + qi + [1.0 / radius]):
            spin[k, 0:8, :] = value
            spin[k, 8:16, :] = value
        sums = [jnp.zeros((8, 128), F32)] * 22
        for dy in range(-2, 3):
            own = [spin[k, -dy % 8 : -dy % 8 + 8, :] for k in range(9)]

            def step(dz, steps, total):
                total = list(total)
                for dx in steps:
                    part = [halo[dz, dy + 2, k, x + dx] for k in range(9)]
                    ox, oy, oz = [part[k] - own[k] for k in range(3)]
                    square = ox * ox + oy * oy + oz * oz
                    scaled = square * lax.rsqrt(jnp.maximum(square, 1e-12)) * own[8]
                    remain = jnp.maximum(1.0 - scaled, 0.0)
                    remain = remain * remain
                    w = remain * remain * (1.0 + 4.0 * scaled) * part[8]
                    wx, wy, wz = w * ox, w * oy, w * oz
                    total[0] = total[0] + w
                    total[1] = total[1] + wx * ox
                    total[2] = total[2] + wy * oy
                    total[3] = total[3] + wz * oz
                    total[4] = total[4] + wx * oy
                    total[5] = total[5] + wx * oz
                    total[6] = total[6] + wy * oz
                    for k in range(5):
                        change = part[3 + k] - own[3 + k]
                        for c, v in enumerate((wx, wy, wz)):
                            total[7 + 3 * k + c] = total[7 + 3 * k + c] + v * change
                return tuple(total)

            total = (jnp.zeros((8, 128), F32),) * 22
            wide = range(5) if abs(dy) < 2 else range(1, 4)
            for dz in range(5):
                total = step(dz, range(5) if dz in (1, 2, 3) else wide, total)
            if dy != 0:
                for k in range(22):
                    turn[k, 0:8, :] = total[k]
                    turn[k, 8:16, :] = total[k]
                total = [turn[k, dy % 8 : dy % 8 + 8, :] for k in range(22)]
            sums = [a + b for a, b in zip(sums, total)]
        omega = sums[0] + (1.0 - alive)
        per = 1.0 / omega
        shift = ridge_scale * radius * radius
        m = [sums[1 + k] * per for k in range(6)]
        m[0], m[1], m[2] = m[0] + shift, m[1] + shift, m[2] + shift
        c = [
            m[1] * m[2] - m[5] * m[5],
            m[0] * m[2] - m[4] * m[4],
            m[0] * m[1] - m[3] * m[3],
            m[4] * m[5] - m[3] * m[2],
            m[3] * m[5] - m[4] * m[1],
            m[3] * m[4] - m[0] * m[5],
        ]
        over = 1.0 / (m[0] * c[0] + m[3] * c[3] + m[4] * c[4])
        b = [v * over for v in c]
        rows = [xi, yi, zi] + qi + [near[0, 9, x]]
        square = per * per
        rows += [v * square for v in b]
        for k in range(5):
            f = [sums[7 + 3 * k + a] * per for a in range(3)]
            rows.append(b[0] * f[0] + b[3] * f[1] + b[4] * f[2])
            rows.append(b[3] * f[0] + b[1] * f[1] + b[5] * f[2])
            rows.append(b[4] * f[0] + b[5] * f[1] + b[2] * f[2])
        at = pl.ds(pl.multiple_of(x * 128, 128), 128)
        for k in range(15):
            pair = jnp.concatenate(rows[2 * k : 2 * k + 2], axis=0)
            for n, part in enumerate(split3(pair)[: 3 if k < 2 else 2]):
                fields[240 * n + 16 * k : 240 * n + 16 * k + 16, at] = part
        return _

    lax.fori_loop(0, 4, one_plane, 0)


def gather_fields(fields, faces, face_used, around):
    lanes = iota((1, 128), 1)
    z = lanes % 8
    sources = iota((128, 128), 0)

    def hot(sy, zs):
        blocks = []
        for x in range(4):
            wanted = jnp.full((1, 128), -1, jnp.int32)
            for sx, xe in ((1, x + 2), (2, x + 6) if x < 2 else (0, x - 2)):
                for s in range(2):
                    p = [faces[s * 28 + sx * 9 + sy * 3 + sz] for sz in zs]
                    p = p[0] if len(p) == 1 else jnp.where(z < 4, p[0], p[1])
                    lane = jnp.where(p >= 0, p * 8 + z, -1)
                    wanted = jnp.where(lanes // 8 == xe * 2 + s, lane, wanted)
            blocks.append(jnp.where(sources == wanted, 1.0, 0.0).astype(BF16))
        return jnp.concatenate(blocks, axis=0)

    def pick(columns):
        found = jnp.dot(
            fields[...], jnp.concatenate(columns, axis=1), preferred_element_type=F32
        )
        first = found[0:32] + found[240:272] + found[480:512]
        return jnp.concatenate([first, found[32:240] + found[272:480]], axis=0)

    low_y = iota((240, 128), 0) % 8 < 4
    found = pick([hot(1, (1,)), hot(1, (2, 0)), hot(0, (1,)), hot(2, (1,))])
    around[0] = found[:, 0:128]
    around[1] = found[:, 128:256]
    around[2] = jnp.where(low_y, found[:, 384:512], found[:, 256:384])
    corner = [face_used[sx * 9 + sy * 3 + sz] for sx in range(3) for sy in (0, 2) for sz in (0, 2)]
    any_corner = sum(corner)

    @pl.when(any_corner > 0)
    def _present():
        found = pick([hot(0, (2, 0)), hot(2, (2, 0))])
        around[3] = jnp.where(low_y, found[:, 128:256], found[:, 0:128])

    @pl.when(any_corner == 0)
    def _absent():
        around[3] = jnp.zeros((240, 128), F32)


HALF = 6
TILES = [(0, -2, -2), (0, -1, -1), (0, 0, 0), (1, -2, -2), (1, -1, -1), (2, -2, -1)]
TILES += [(0, 2, 2), (0, 1, 1), (1, 0, 0), (1, 2, 2), (1, 1, 1), (2, 1, 2), (2, 0, 0)]


def shift_fields(around, wide, inner):
    lanes = iota((8, 128), 1)
    z = lanes % 8
    outer = (lanes < 16) | (lanes >= 112)
    middle = (lanes >= 32) & (lanes < 96)
    left = lanes < 64

    def some_rows(n, _):
        for m in range(3):
            row = n * 3 + m
            at = pl.ds(pl.multiple_of(row * 8, 8), 8)
            parts = [(around[n, at, :], around[n + 1, at, :]) for n in (0, 2)]
            for dz in range(-2, 3):
                orders = []
                for base, beyond in parts:
                    far = shifted(base, beyond, z, dz)
                    half = pltpu.roll(far, 64, 1)
                    orders.append(
                        (far, jnp.where(outer, half, far), jnp.where(middle, far, half))
                    )
                for tile, (k, first, second) in enumerate(TILES):
                    value = across(first, orders[1][k], orders[0][k])
                    if first != second:
                        value = jnp.where(left, value, across(second, orders[1][k], orders[0][k]))
                    wide[dz + 2, tile, row] = value
                if dz == 0:
                    own = orders[0][2]
                    back, on = pltpu.roll(own, 112, 1), pltpu.roll(own, 16, 1)
                    values = pltpu.roll(own, 32, 1), jnp.where(left, back, on), own
                    for k, value in enumerate(values):
                        inner[k, row, 0:8, :] = value
                        inner[k, row, 8:16, :] = value
        return _

    lax.fori_loop(0, 10, some_rows, 0)


def weight(scaled):
    remain = jnp.maximum(1.0 - scaled, 0.0)
    remain = remain * remain
    return remain * remain * (1.0 + 4.0 * scaled)


def side(state, n):
    density, pressure = jnp.exp(state[0]), jnp.exp(state[4])
    v = state[1:4]
    speed = v[0] * n[0] + v[1] * n[1] + v[2] * n[2]
    sound = jnp.exp(0.5 * (state[4] - state[0])) * (gamma**0.5)
    return density, pressure, v[0], v[1], v[2], speed, sound


def face(near, far):
    o = [far(k) - near(k) for k in range(3)]
    square = jnp.maximum(o[0] * o[0] + o[1] * o[1] + o[2] * o[2], 1e-12)
    inverse = lax.rsqrt(square)
    distance = square * inverse
    n = [v * inverse for v in o]
    hi, hj = near(8), far(8)
    live = jnp.minimum(hi, hj) > 0.0
    wi = weight(distance * (1.0 / jnp.where(hi > 0.0, hi, 1.0)))
    wj = weight(distance * (1.0 / jnp.where(hj > 0.0, hj, 1.0)))
    c = [wi * near(9 + k) + wj * far(9 + k) for k in range(6)]
    a = [
        c[0] * o[0] + c[3] * o[1] + c[4] * o[2],
        c[3] * o[0] + c[1] * o[1] + c[5] * o[2],
        c[4] * o[0] + c[5] * o[1] + c[2] * o[2],
    ]
    area = a[0] * a[0] + a[1] * a[1] + a[2] * a[2]
    area = jnp.where(live, jnp.sqrt(area), 0.0)
    left, right = [], []
    for k in range(5):
        gi = near(15 + 3 * k) * o[0] + near(16 + 3 * k) * o[1] + near(17 + 3 * k) * o[2]
        gj = far(15 + 3 * k) * o[0] + far(16 + 3 * k) * o[1] + far(17 + 3 * k) * o[2]
        left.append(near(3 + k) + 0.5 * jnp.tanh(gi))
        right.append(far(3 + k) - 0.5 * jnp.tanh(gj))
    sl, sr = side(left, n), side(right, n)
    slow = jnp.minimum(sl[5] - sl[6], sr[5] - sr[6])
    fast = jnp.maximum(sl[5] + sl[6], sr[5] + sr[6])
    ml, mr = sl[0] * (slow - sl[5]), sr[0] * (fast - sr[5])
    middle = (sr[1] - sl[1] + ml * sl[5] - mr * sr[5]) / (ml - mr)
    from_left = (slow >= 0.0) | (middle >= 0.0)
    density, pressure, v0, v1, v2, speed, _ = [
        jnp.where(from_left, p, q) for p, q in zip(sl, sr)
    ]
    mass, wave = jnp.where(from_left, ml, mr), jnp.where(from_left, slow, fast)
    star = jnp.where(from_left, -slow, fast) > 0.0
    kinetic = 0.5 * (v0 * v0 + v1 * v1 + v2 * v2)
    energy = pressure * (1.0 / (gamma - 1.0)) + density * kinetic
    push = jnp.where(star, wave * mass / (wave - middle), 0.0)
    rest = speed - jnp.where(star, wave, 0.0)
    lift = middle - speed
    flow = density * rest + push
    press = pressure + push * lift
    heat = energy * rest + pressure * speed
    heat = heat + push * (energy / density + lift * (middle + pressure / mass))
    terms = [flow, v0 * flow + press * n[0], v1 * flow + press * n[1], v2 * flow + press * n[2]]
    return [jnp.where(live, t * area, 0.0) for t in terms + [heat]]


def fluxes(wide, inner, turned, gains):
    left = iota((8, 128), 1) < 64
    zero = jnp.zeros((8, 128), F32)

    def halves(first, second, load):
        return load(first) if first == second else jnp.where(left, load(first), load(second))

    def turn(row, _):
        for n, (k, first, second) in enumerate(TILES):
            turned[n, row] = halves(
                first, second, lambda dy: inner[k, row, -dy % 8 : -dy % 8 + 8, :]
            )
        return _

    lax.fori_loop(0, 30, turn, 0, unroll=10)
    def add(sums, n, far):
        return [a + b for a, b in zip(sums, face(lambda row: turned[n, row], far))]

    def keep(sums, n):
        for c, value in enumerate(sums):
            gains[n, c, 0:8, :] = value

    def some_tiles(part, _):
        for m in range(HALF):
            n = part * HALF + m
            sums = [zero] * 5
            for dz in range(1, 4) if m == 0 else range(5):
                sums = add(sums, n, lambda row: wide[dz, n, row])
            keep(sums, n)
        return _

    lax.fori_loop(0, 2, some_tiles, 0)
    last = len(TILES) - 1
    sums = [zero] * 5
    for d in (0, 1):
        sums = add(
            sums, last, lambda row: jnp.where(left, wide[d, last, row], wide[4 - d, last, row])
        )
    keep(sums, last)
    found = []
    for c in range(5):
        orders = [zero, zero, zero]
        for n, (k, first, second) in enumerate(TILES):
            gains[n, c, 8:16, :] = gains[n, c, 0:8, :]
            part = halves(first, second, lambda dy: gains[n, c, dy % 8 : dy % 8 + 8, :])
            orders[k] = orders[k] + part
        two, one, same = orders
        total = same + pltpu.roll(two, 32, 1)
        total = total + pltpu.roll(jnp.where(left, one, 0.0), 16, 1)
        total = total + pltpu.roll(jnp.where(left, 0.0, one), 112, 1)
        found.append(-(total + pltpu.roll(total, 64, 1)))
    return found


def sweep(
    lists, chunks, place, gradients, rate, source, used, faces, face_used, near, halo, fields,
    around, wide, inner, spin, turn, turned, gains,
):
    fill_tables(lists, source, used, faces, face_used)
    collect_sites(chunks, source, used, near)
    shift_sites(near, halo)
    moments(near, halo, fields, spin, turn)
    gather_fields(fields, faces, face_used, around)
    shift_fields(around, wide, inner)
    rates = fluxes(wide, inner, turned, gains)
    rows = [wide[2, 2, 15 + k] for k in range(15)] + rates
    found = jnp.concatenate(rows, axis=0)
    lane = place[1:2, :].astype(jnp.int32) + 32
    hot = jnp.where(iota((128, 512), 0) == lane, 1.0, 0.0).astype(BF16)
    total = jnp.zeros((160, 512), F32)
    for part in split3(found):
        total = total + jnp.dot(part, hot, preferred_element_type=F32)
    here = (iota((8, 512), 0) == place[0:1, :].astype(jnp.int32)) & (place[2:3, :] > 0.0)
    for k in range(20):
        row = jnp.sum(jnp.where(here, total[8 * k : 8 * k + 8], 0.0), axis=0, keepdims=True)
        if k < 15:
            gradients[k : k + 1, :] = row
        else:
            rate[k - 15 : k - 14, :] = row


def sweep_call(lists, chunks, place):
    vmem = pl.BlockSpec(memory_space=pltpu.VMEM)
    smem = pl.BlockSpec(memory_space=pltpu.SMEM)
    return pl.pallas_call(
        sweep,
        out_shape=(jax.ShapeDtypeStruct((15, 512), F32), jax.ShapeDtypeStruct((5, 512), F32)),
        in_specs=[smem, vmem, vmem],
        out_specs=(vmem, vmem),
        scratch_shapes=[
            pltpu.SMEM((28 * 16,), jnp.int32),
            pltpu.SMEM((28,), jnp.int32),
            pltpu.SMEM((56,), jnp.int32),
            pltpu.SMEM((28,), jnp.int32),
            pltpu.VMEM((8, 10, 4, 8, 128), F32),
            pltpu.VMEM((5, 5, 9, 8, 8, 128), F32),
            pltpu.VMEM((512, 512), BF16),
            pltpu.VMEM((4, 240, 128), F32),
            pltpu.VMEM((5, len(TILES), 30, 8, 128), F32),
            pltpu.VMEM((3, 30, 16, 128), F32),
            pltpu.VMEM((9, 16, 128), F32),
            pltpu.VMEM((22, 16, 128), F32),
            pltpu.VMEM((len(TILES), 30, 8, 128), F32),
            pltpu.VMEM((len(TILES), 5, 16, 128), F32),
        ],
        compiler_params=pltpu.CompilerParams(vmem_limit_bytes=48 * 1024 * 1024),
        name="sweep",
    )(lists.reshape(24 * 128), chunks, place)


def body(geom, density, velocity, pressure, block_live, pair_list):
    chunks, place, lists = exchange_call(geom, density, velocity, pressure, block_live, pair_list)
    return sweep_call(lists, chunks, place)


def solution(mesh):
    both = ("region", "group")
    return jax.shard_map(
        body,
        mesh=mesh,
        in_specs=(P(None, both), P(both), P(None, both), P(both), P(both), P(both, None)),
        out_specs=(P(None, both), P(None, both)),
        check_vma=False,
    )
```

```python
import functools

import jax
import jax.numpy as jnp
from jax import lax
from jax.experimental import pallas as pl
from jax.experimental.pallas import tpu as pltpu
from jax.sharding import PartitionSpec as P

BLOCK = 256
LIST = 14
LAYERS = 3
F32 = jnp.float32
BF16 = jnp.bfloat16
ridge_scale = 0.05
gamma = 5.0 / 3.0
HEAD, TAIL, CORNER = 64, 78, 92
MESH = pl.DeviceIdType.MESH


def iota(shape, dim):
    return lax.broadcasted_iota(jnp.int32, shape, dim)


def split3(value):
    high = value.astype(BF16)
    rest = value - high.astype(F32)
    middle = rest.astype(BF16)
    low = (rest - middle.astype(F32)).astype(BF16)
    return high, middle, low


def order_key(heads, index):
    parity = (heads - 2.0 * jnp.floor(heads * 0.5)).astype(jnp.int32)
    return jnp.where((heads >= 0.0) & (index < LIST), parity, 2)


def prepare(values, place):
    lanes = iota((1, 128), 1)
    total = jnp.zeros((40, 128), F32)
    both = jnp.concatenate([values[8:12, 0:128], values[8:12, 0:128]], axis=0).T[0:16]
    kinds = [order_key(values[9:10, 0:128], lanes), order_key(both[:, 1:2], iota((16, 1), 0))]
    here, there = iota((16, 128), 1), iota((16, 128), 0)
    ahead = (kinds[0] < kinds[1]) | ((kinds[0] == kinds[1]) & (here < there))
    ahead = jnp.where(ahead & (here < LIST), 1.0, 0.0)
    rank = jnp.sum(ahead, axis=1, keepdims=True).astype(jnp.int32)
    listed = jnp.where((here == TAIL + rank) & (there < LIST), both[:, 2:3], 0.0)
    listed = jnp.sum(listed, axis=0, keepdims=True)
    for s in range(2):
        count = jnp.sum(jnp.where(kinds[0] == s, 1.0, 0.0), axis=1, keepdims=True)
        listed = listed + jnp.where(lanes == HEAD + s, count, 0.0)
    for s in range(2):
        at = slice(s * BLOCK, (s + 1) * BLOCK)
        corner = values[0:4, at]
        columns = jnp.concatenate([corner, corner], axis=0).T
        cells = []
        for k, count in ((0, 64), (1, 32), (2, 32)):
            smaller = columns[:, k : k + 1] < corner[k : k + 1, :]
            rank = jnp.sum(jnp.where(smaller, 1.0, 0.0), axis=0, keepdims=True)
            cells.append(jnp.floor(rank * (1.0 / count)).astype(jnp.int32))
            low = jnp.min(corner[k : k + 1, :], axis=1, keepdims=True)
            listed = listed + jnp.where(lanes == CORNER + 3 * s + k, low, 0.0)
        lane = cells[0] * 8 + cells[2]
        alive = iota((1, BLOCK), 1).astype(F32) < values[11:12, s : s + 1]
        rows = [corner[0:1], corner[1:2], corner[2:3], jnp.log(values[4:5, at])]
        rows += [values[5 + k : 6 + k, at] for k in range(3)]
        rows += [jnp.log(values[8:9, at]), jnp.where(alive, corner[3:4], 0.0)]
        here = iota((8, BLOCK), 0) == cells[1]
        spread = [jnp.where(here, row, 0.0) for row in rows] + [jnp.zeros((8, BLOCK), F32)]
        for par in range(2):
            target = jnp.where(iota((128, BLOCK), 0) == lane + (par * 64 + s * 32), 1.0, 0.0)
            target = target.astype(BF16)
            for part in split3(jnp.concatenate(spread[par::2], axis=0)):
                total = total + lax.dot_general(
                    part, target, (((1,), (1,)), ((), ())), preferred_element_type=F32
                )
        place[0:1, at] = cells[1].astype(F32)
        place[1:2, at] = (cells[0] * 16 + cells[2] + 8 * s).astype(F32)
        place[2:3, at] = jnp.where(alive, 1.0, 0.0)
    return total + jnp.where(iota((40, 128), 0) == 32, listed, 0.0)


def read_lists(chunks, lists, region, group):
    lanes = iota((24, 128), 1)
    kind = (lanes - CORNER) % 3
    scale = jnp.where(kind == 0, 0.25, 0.125)
    weight = jnp.where(kind == 0, 1024.0, jnp.where(kind == 1, 32.0, 1.0))
    own = chunks[1, group // 4, group % 4, 32:33, :]
    own = jnp.where(lanes[0:1] >= CORNER + 3, pltpu.roll(own, 3, 1), own)
    first = ((region - 1) * 64).astype(F32)
    whole = jnp.zeros((24, 128), jnp.int32)
    for m in range(4):
        rows = chunks[:, :, m, 32, :].reshape(24, 128)
        steps = jnp.floor((rows - own) * scale + 0.5) * weight
        steps = steps + pltpu.roll(steps, 127, 1) + pltpu.roll(steps, 126, 1)
        ids = jnp.where(lanes < TAIL, rows, rows - first)
        rows = jnp.where(lanes < CORNER, ids, steps).astype(jnp.int32)
        rows = jnp.where(lanes == CORNER + 1, region, jnp.where(lanes == CORNER + 2, group, rows))
        whole = jnp.where(lanes // 32 == m, pltpu.roll(rows, (64 + 32 * m) % 128, 1), whole)
    lists[...] = whole


STEPS = (1, -1, 2, -2, 3, -3, 4)


def exchange(
    values, chunks, place, lists,
    z_send, z_recv, x_send, x_recv, r_send, r_recv,
):
    region, group = lax.axis_index("region"), lax.axis_index("group")
    z, x = group // 4, group % 4

    def column(step):
        return (region, z * 4 + (x + step) % 4)

    def plane(step):
        return (region, (z + 8 + step) % 8 * 4 + x)

    def slab(step):
        return ((region + 16 + step) % 16, group)

    partners = [column(k) for k in (1, 2, 3)] + [plane(k) for k in STEPS] + [slab(1), slab(-1)]
    barrier = pltpu.get_barrier_semaphore()
    for partner in partners:
        pl.semaphore_signal(barrier, inc=1, device_id=partner, device_id_type=MESH)
    chunks[1, z, x] = prepare(values, place)
    pl.semaphore_wait(barrier, len(partners))

    def copy(source, target, device, send, recv):
        return pltpu.make_async_remote_copy(
            src_ref=source,
            dst_ref=target,
            send_sem=send,
            recv_sem=recv,
            device_id=device,
            device_id_type=MESH,
        )

    def row(step):
        return (z + 16 + step) % 8

    def along_z(step, arrived=False):
        ref = chunks.at[1, row(-step) if arrived else z, x]
        return copy(ref, ref, plane(step), z_send.at[step % 8], z_recv.at[step % 8])

    def along_x(n, k, arrived=False):
        ref = chunks.at[1, row(n), (x + 4 - k) % 4 if arrived else x]
        return copy(ref, ref, column(k), x_send.at[n % 8, k - 1], x_recv.at[n % 8, k - 1])

    def along_r(step, n, arrived=False):
        side = 0 if step > 0 else 1
        target = chunks.at[2 * side, row(n)]
        source = target if arrived else chunks.at[1, row(n)]
        return copy(source, target, slab(step), r_send.at[side, n % 8], r_recv.at[side, n % 8])

    def spread(n):
        for k in (2, 1, 3):
            along_x(n, k).start()

    def give(n):
        for k in (1, 2, 3):
            along_x(n, k, True).wait_recv()
        for step in (1, -1):
            along_r(step, n).start()

    for step in STEPS:
        along_z(step).start()
    spread(0)
    for step in (-1, 1):
        along_z(-step, True).wait_recv()
        spread(step)
    give(0)
    for far in (2, 3, 4):
        for step in (-far, far) if far < 4 else (4,):
            along_z(-step if far < 4 else 4, True).wait_recv()
            spread(step)
        if far > 2:
            give(2 - far)
            give(far - 2)
    give(-3)
    give(3)
    give(4)
    for n in range(8):
        for step in (1, -1):
            along_r(step, n, True).wait_recv()
    read_lists(chunks, lists, region, group)
    for step in STEPS:
        along_z(step).wait_send()
    for n in range(8):
        for k in (1, 2, 3):
            along_x(n, k).wait_send()
        for step in (1, -1):
            along_r(step, n).wait_send()


def exchange_call(geom, density, velocity, pressure, live, pair):
    vmem = pl.BlockSpec(memory_space=pltpu.VMEM)
    def rows(v, first):
        return jnp.pad(v, ((first, 12 - first - v.shape[0]), (0, 2 * BLOCK - v.shape[1])))

    values = rows(geom, 0) + rows(density[None], 4) + rows(velocity, 5) + rows(pressure[None], 8)
    values = values + (rows(pair.T, 9) + rows(live[None], 11)).astype(F32)
    dma = pltpu.SemaphoreType.DMA
    chunks, place, lists = pl.pallas_call(
        exchange,
        out_shape=(
            jax.ShapeDtypeStruct((LAYERS, 8, 4, 40, 128), F32),
            jax.ShapeDtypeStruct((8, 512), F32),
            jax.ShapeDtypeStruct((24, 128), jnp.int32),
        ),
        in_specs=[vmem],
        out_specs=(vmem, vmem, vmem),
        scratch_shapes=[
            dma((8,)),
            dma((8,)),
            dma((8, 3)),
            dma((8, 3)),
            dma((2, 8)),
            dma((2, 8)),
        ],
        compiler_params=pltpu.CompilerParams(
            collective_id=0, has_side_effects=True, vmem_limit_bytes=16 * 1024 * 1024
        ),
        name="gather_sites",
    )(values)
    return chunks.reshape(LAYERS * 32, 40, 128), place, lists


def direction(step, wanted):
    u = step + 1057
    a, b, c = u >> 10, (u >> 5) & 31, u & 31
    fits = wanted & (u >= 0) & (jnp.maximum(jnp.maximum(a, b), c) <= 2)
    return jnp.where(fits, a * 9 + b * 3 + c, 27)


def fill_tables(lists, source, used, faces, face_used):
    def clear(k, _):
        source[k] = -1
        return _

    lax.fori_loop(0, 27 * 16, clear, 0, unroll=16)

    def clear_way(k, _):
        used[k] = 0
        face_used[k] = 0
        faces[k] = -1
        faces[28 + k] = -1
        return _

    lax.fori_loop(0, 28, clear_way, 0, unroll=14)
    own = (32 + lists[30]) * 32

    def code(block):
        return lists[(block >> 1) * 32 + 28 + 3 * (block & 1)]

    def slot(p, _):
        first, second = lists[own], lists[own + 1]
        listed = p < first + second
        odd = jnp.where(p < first, 0, 1)
        tail = jnp.where(listed, lists[own + LIST + p], 64)
        place = code(tail)
        way = direction(place - lists[own + 28 + 3 * odd], listed)
        faces[odd * 28 + way] = p
        face_used[way] = 1
        at = (tail >> 1) * 32
        other = tail & 1
        count = jnp.where(listed, jnp.where(other == 0, lists[at], lists[at + 1]), 0)
        start = at + LIST + jnp.where(other == 0, 0, lists[at])

        def entry(k):
            near = k < count
            there = lists[jnp.where(near, start + k, at)]
            near = near & (there >= 0) & (there < 192)
            there = jnp.where(near, there, 0)
            towards = direction(code(there) - place, near)
            source[towards * 16 + p] = there
            used[towards] = 1

        for k in range(LIST // 2):
            entry(k)

        @pl.when(count > LIST // 2)
        def _more():
            for k in range(LIST // 2, LIST):
                entry(k)

        return _

    lax.fori_loop(0, LIST, slot, 0)


def swap(low, high, is_low, width):
    first = jnp.where(is_low, low, pltpu.roll(high, width, 1))
    second = jnp.where(is_low, pltpu.roll(low, 128 - width, 1), high)
    return first, second


def collect_sites(chunks, source, used, near):
    lanes = iota((8, 128), 1)
    group = lanes // 8
    bit = [(group >> k) % 2 == 0 for k in range(4)]
    low_y, low_z, low_x = iota((8, 128), 0) < 4, lanes % 8 < 4, (group % 4) < 2

    def choose(sides, mask, value):
        if len(sides) == 1:
            return value(sides[0])
        return jnp.where(mask, value(2), value(0))

    for kind in range(8):
        xs, ys, zs = [(2, 0) if kind & b else (1,) for b in (4, 2, 1)]
        ways = [(sx * 9 + sy * 3 + sz) for sx in xs for sy in ys for sz in zs]
        any_used = sum(used[way] for way in ways)

        @pl.when(any_used > 0)
        def _present():
            froms = {(way, p): source[way * 16 + p] for way in ways for p in range(LIST)}

            def code(way, p):
                f = froms[way, p]
                return jnp.where(f >= 0, 1 + 2 * (f & 1), 0)

            codes = {}
            for sx in xs:
                codes[sx] = jnp.zeros((8, 128), jnp.int32)
                for p in range(LIST):
                    value = choose(
                        ys,
                        low_y,
                        lambda sy: choose(zs, low_z, lambda sz: code(sx * 9 + sy * 3 + sz, p)),
                    )
                    codes[sx] = jnp.where(group == p, value, codes[sx])

            def tile(p, rows):
                def load(sx, sy, sz):
                    return chunks[jnp.maximum(froms[sx * 9 + sy * 3 + sz, p], 0) >> 1, rows, :]

                return choose(
                    xs,
                    low_x,
                    lambda sx: choose(
                        ys, low_y, lambda sy: choose(zs, low_z, lambda sz: load(sx, sy, sz))
                    ),
                )

            def one_tile(t, _):
                v = [tile(p, pl.ds(t * 8, 8)) for p in range(LIST)]
                v += v[:2]
                for k in (0, 1, 3):
                    step = 1 << k
                    for p in range(16):
                        if not p & step:
                            v[p], v[p + step] = swap(v[p], v[p + step], bit[k], 8 * step)
                for n in range(8):
                    par, x = n // 4, n % 4
                    info = codes[xs[0] if x < 2 else xs[-1]]
                    second = info >= 2
                    low, high = v[8 * par + x], v[8 * par + x + 4]
                    low = jnp.where(second, pltpu.roll(low, 96, 1), low)
                    high = jnp.where(second, high, pltpu.roll(high, 32, 1))
                    out = jnp.where(info > 0, jnp.where(bit[2], low, high), 0.0)
                    near[kind, 2 * t + par, x] = out
                return _

            if kind in (0, 1, 2, 4):
                for t in range(5):
                    one_tile(t, 0)
            else:
                lax.fori_loop(0, 5, one_tile, 0)
            for x in range(4):
                radius = near[kind, 8, x]
                near[kind, 9, x] = radius
                near[kind, 8, x] = jnp.where(radius > 0.0, 1.0, 0.0)

        @pl.when(any_used == 0)
        def _absent():
            near[kind] = jnp.zeros((10, 4, 8, 128), F32)


def shifted(base, outer, z, dz):
    if dz == 0:
        return base
    inside = pltpu.roll(base, (-dz) % 128, 1)
    if dz > 0:
        return jnp.where(z + dz < 8, inside, pltpu.roll(outer, 8 - dz, 1))
    return jnp.where(z + dz >= 0, inside, pltpu.roll(outer, 128 - 8 - dz, 1))


def rim_rows(dy):
    row = iota((8, 128), 0)
    return row < dy if dy > 0 else row >= 8 + dy


def across(dy, edge, middle):
    return middle if dy == 0 else jnp.where(rim_rows(dy), edge, middle)


def shift_sites(near, halo):
    z = iota((8, 128), 1) % 8

    def one_row(row, _):
        for xe in range(8):
            mx, x = (4, xe + 2) if xe < 2 else (0, xe - 2) if xe < 6 else (4, xe - 6)
            mid = near[mx, row, x], near[mx + 1, row, x]
            rim = near[mx + 2, row, x], near[mx + 3, row, x]
            for dz in range(-2, 3):
                middle, edge = shifted(*mid, z, dz), shifted(*rim, z, dz)
                for dy in range(-2, 3):
                    halo[dz + 2, dy + 2, row, xe] = across(dy, edge, middle)
        return _

    lax.fori_loop(0, 9, one_row, 0, unroll=3)


def moments(near, halo, fields, spin, turn):
    def one_plane(x, _):
        xi, yi, zi = [near[0, k, x] for k in range(3)]
        qi = [near[0, 3 + k, x] for k in range(5)]
        alive, radius = near[0, 8, x], near[0, 9, x]
        radius = jnp.where(radius > 0.0, radius, 1.0)
        for k, value in enumerate([xi, yi, zi] + qi + [1.0 / radius]):
            spin[k, 0:8, :] = value
            spin[k, 8:16, :] = value
        sums = [jnp.zeros((8, 128), F32)] * 22
        for dy in range(-2, 3):
            own = [spin[k, -dy % 8 : -dy % 8 + 8, :] for k in range(9)]

            def step(dz, steps, total):
                total = list(total)
                for dx in steps:
                    part = [halo[dz, dy + 2, k, x + dx] for k in range(9)]
                    ox, oy, oz = [part[k] - own[k] for k in range(3)]
                    square = ox * ox + oy * oy + oz * oz
                    scaled = square * lax.rsqrt(jnp.maximum(square, 1e-12)) * own[8]
                    remain = jnp.maximum(1.0 - scaled, 0.0)
                    remain = remain * remain
                    w = remain * remain * (1.0 + 4.0 * scaled) * part[8]
                    wx, wy, wz = w * ox, w * oy, w * oz
                    total[0] = total[0] + w
                    total[1] = total[1] + wx * ox
                    total[2] = total[2] + wy * oy
                    total[3] = total[3] + wz * oz
                    total[4] = total[4] + wx * oy
                    total[5] = total[5] + wx * oz
                    total[6] = total[6] + wy * oz
                    for k in range(5):
                        change = part[3 + k] - own[3 + k]
                        for c, v in enumerate((wx, wy, wz)):
                            total[7 + 3 * k + c] = total[7 + 3 * k + c] + v * change
                return tuple(total)

            total = (jnp.zeros((8, 128), F32),) * 22
            wide = range(5) if abs(dy) < 2 else range(1, 4)
            for dz in range(5):
                total = step(dz, range(5) if dz in (1, 2, 3) else wide, total)
            if dy != 0:
                for k in range(22):
                    turn[k, 0:8, :] = total[k]
                    turn[k, 8:16, :] = total[k]
                total = [turn[k, dy % 8 : dy % 8 + 8, :] for k in range(22)]
            sums = [a + b for a, b in zip(sums, total)]
        omega = sums[0] + (1.0 - alive)
        per = 1.0 / omega
        shift = ridge_scale * radius * radius
        m = [sums[1 + k] * per for k in range(6)]
        m[0], m[1], m[2] = m[0] + shift, m[1] + shift, m[2] + shift
        c = [
            m[1] * m[2] - m[5] * m[5],
            m[0] * m[2] - m[4] * m[4],
            m[0] * m[1] - m[3] * m[3],
            m[4] * m[5] - m[3] * m[2],
            m[3] * m[5] - m[4] * m[1],
            m[3] * m[4] - m[0] * m[5],
        ]
        over = 1.0 / (m[0] * c[0] + m[3] * c[3] + m[4] * c[4])
        b = [v * over for v in c]
        rows = [xi, yi, zi] + qi + [near[0, 9, x]]
        square = per * per
        rows += [v * square for v in b]
        for k in range(5):
            f = [sums[7 + 3 * k + a] * per for a in range(3)]
            rows.append(b[0] * f[0] + b[3] * f[1] + b[4] * f[2])
            rows.append(b[3] * f[0] + b[1] * f[1] + b[5] * f[2])
            rows.append(b[4] * f[0] + b[5] * f[1] + b[2] * f[2])
        at = pl.ds(pl.multiple_of(x * 128, 128), 128)
        for k in range(15):
            pair = jnp.concatenate(rows[2 * k : 2 * k + 2], axis=0)
            for n, part in enumerate(split3(pair)[: 3 if k < 2 else 2]):
                fields[240 * n + 16 * k : 240 * n + 16 * k + 16, at] = part
        return _

    lax.fori_loop(0, 4, one_plane, 0)


def gather_fields(fields, faces, face_used, around):
    lanes = iota((1, 128), 1)
    z = lanes % 8
    sources = iota((128, 128), 0)

    def hot(sy, zs):
        blocks = []
        for x in range(4):
            wanted = jnp.full((1, 128), -1, jnp.int32)
            for sx, xe in ((1, x + 2), (2, x + 6) if x < 2 else (0, x - 2)):
                for s in range(2):
                    p = [faces[s * 28 + sx * 9 + sy * 3 + sz] for sz in zs]
                    p = p[0] if len(p) == 1 else jnp.where(z < 4, p[0], p[1])
                    lane = jnp.where(p >= 0, p * 8 + z, -1)
                    wanted = jnp.where(lanes // 8 == xe * 2 + s, lane, wanted)
            blocks.append(jnp.where(sources == wanted, 1.0, 0.0).astype(BF16))
        return jnp.concatenate(blocks, axis=0)

    def pick(columns):
        found = jnp.dot(
            fields[...], jnp.concatenate(columns, axis=1), preferred_element_type=F32
        )
        first = found[0:32] + found[240:272] + found[480:512]
        return jnp.concatenate([first, found[32:240] + found[272:480]], axis=0)

    low_y = iota((240, 128), 0) % 8 < 4
    found = pick([hot(1, (1,)), hot(1, (2, 0)), hot(0, (1,)), hot(2, (1,))])
    around[0] = found[:, 0:128]
    around[1] = found[:, 128:256]
    around[2] = jnp.where(low_y, found[:, 384:512], found[:, 256:384])
    corner = [face_used[sx * 9 + sy * 3 + sz] for sx in range(3) for sy in (0, 2) for sz in (0, 2)]
    any_corner = sum(corner)

    @pl.when(any_corner > 0)
    def _present():
        found = pick([hot(0, (2, 0)), hot(2, (2, 0))])
        around[3] = jnp.where(low_y, found[:, 128:256], found[:, 0:128])

    @pl.when(any_corner == 0)
    def _absent():
        around[3] = jnp.zeros((240, 128), F32)


HALF = 6
TILES = [(0, -2, -2), (0, -1, -1), (0, 0, 0), (1, -2, -2), (1, -1, -1), (2, -2, -1)]
TILES += [(0, 2, 2), (0, 1, 1), (1, 0, 0), (1, 2, 2), (1, 1, 1), (2, 1, 2), (2, 0, 0)]


def shift_fields(around, wide, inner):
    lanes = iota((8, 128), 1)
    z = lanes % 8
    outer = (lanes < 16) | (lanes >= 112)
    middle = (lanes >= 32) & (lanes < 96)
    left = lanes < 64

    def some_rows(n, _):
        for m in range(3):
            row = n * 3 + m
            at = pl.ds(pl.multiple_of(row * 8, 8), 8)
            parts = [(around[n, at, :], around[n + 1, at, :]) for n in (0, 2)]
            for dz in range(-2, 3):
                orders = []
                for base, beyond in parts:
                    far = shifted(base, beyond, z, dz)
                    half = pltpu.roll(far, 64, 1)
                    orders.append(
                        (far, jnp.where(outer, half, far), jnp.where(middle, far, half))
                    )
                for tile, (k, first, second) in enumerate(TILES):
                    value = across(first, orders[1][k], orders[0][k])
                    if first != second:
                        value = jnp.where(left, value, across(second, orders[1][k], orders[0][k]))
                    wide[dz + 2, tile, row] = value
                if dz == 0:
                    own = orders[0][2]
                    back, on = pltpu.roll(own, 112, 1), pltpu.roll(own, 16, 1)
                    values = pltpu.roll(own, 32, 1), jnp.where(left, back, on), own
                    for k, value in enumerate(values):
                        inner[k, row, 0:8, :] = value
                        inner[k, row, 8:16, :] = value
        return _

    lax.fori_loop(0, 10, some_rows, 0)


def weight(scaled):
    remain = jnp.maximum(1.0 - scaled, 0.0)
    remain = remain * remain
    return remain * remain * (1.0 + 4.0 * scaled)


def side(state, n):
    density, pressure = jnp.exp(state[0]), jnp.exp(state[4])
    v = state[1:4]
    speed = v[0] * n[0] + v[1] * n[1] + v[2] * n[2]
    sound = jnp.exp(0.5 * (state[4] - state[0])) * (gamma**0.5)
    return density, pressure, v[0], v[1], v[2], speed, sound


def face(near, far):
    o = [far(k) - near(k) for k in range(3)]
    square = jnp.maximum(o[0] * o[0] + o[1] * o[1] + o[2] * o[2], 1e-12)
    inverse = lax.rsqrt(square)
    distance = square * inverse
    n = [v * inverse for v in o]
    hi, hj = near(8), far(8)
    live = jnp.minimum(hi, hj) > 0.0
    wi = weight(distance * (1.0 / jnp.where(hi > 0.0, hi, 1.0)))
    wj = weight(distance * (1.0 / jnp.where(hj > 0.0, hj, 1.0)))
    c = [wi * near(9 + k) + wj * far(9 + k) for k in range(6)]
    a = [
        c[0] * o[0] + c[3] * o[1] + c[4] * o[2],
        c[3] * o[0] + c[1] * o[1] + c[5] * o[2],
        c[4] * o[0] + c[5] * o[1] + c[2] * o[2],
    ]
    area = a[0] * a[0] + a[1] * a[1] + a[2] * a[2]
    area = jnp.where(live, jnp.sqrt(area), 0.0)
    left, right = [], []
    for k in range(5):
        gi = near(15 + 3 * k) * o[0] + near(16 + 3 * k) * o[1] + near(17 + 3 * k) * o[2]
        gj = far(15 + 3 * k) * o[0] + far(16 + 3 * k) * o[1] + far(17 + 3 * k) * o[2]
        left.append(near(3 + k) + 0.5 * jnp.tanh(gi))
        right.append(far(3 + k) - 0.5 * jnp.tanh(gj))
    sl, sr = side(left, n), side(right, n)
    slow = jnp.minimum(sl[5] - sl[6], sr[5] - sr[6])
    fast = jnp.maximum(sl[5] + sl[6], sr[5] + sr[6])
    ml, mr = sl[0] * (slow - sl[5]), sr[0] * (fast - sr[5])
    middle = (sr[1] - sl[1] + ml * sl[5] - mr * sr[5]) / (ml - mr)
    from_left = (slow >= 0.0) | (middle >= 0.0)
    density, pressure, v0, v1, v2, speed, _ = [
        jnp.where(from_left, p, q) for p, q in zip(sl, sr)
    ]
    mass, wave = jnp.where(from_left, ml, mr), jnp.where(from_left, slow, fast)
    star = jnp.where(from_left, -slow, fast) > 0.0
    kinetic = 0.5 * (v0 * v0 + v1 * v1 + v2 * v2)
    energy = pressure * (1.0 / (gamma - 1.0)) + density * kinetic
    push = jnp.where(star, wave * mass / (wave - middle), 0.0)
    rest = speed - jnp.where(star, wave, 0.0)
    lift = middle - speed
    flow = density * rest + push
    press = pressure + push * lift
    heat = energy * rest + pressure * speed
    heat = heat + push * (energy / density + lift * (middle + pressure / mass))
    terms = [flow, v0 * flow + press * n[0], v1 * flow + press * n[1], v2 * flow + press * n[2]]
    return [jnp.where(live, t * area, 0.0) for t in terms + [heat]]


def fluxes(wide, inner, turned, gains):
    left = iota((8, 128), 1) < 64
    zero = jnp.zeros((8, 128), F32)

    def halves(first, second, load):
        return load(first) if first == second else jnp.where(left, load(first), load(second))

    def turn(row, _):
        for n, (k, first, second) in enumerate(TILES):
            turned[n, row] = halves(
                first, second, lambda dy: inner[k, row, -dy % 8 : -dy % 8 + 8, :]
            )
        return _

    lax.fori_loop(0, 30, turn, 0, unroll=10)
    def add(sums, n, far):
        return [a + b for a, b in zip(sums, face(lambda row: turned[n, row], far))]

    def keep(sums, n):
        for c, value in enumerate(sums):
            gains[n, c, 0:8, :] = value

    def some_tiles(part, _):
        for m in range(HALF):
            n = part * HALF + m
            sums = [zero] * 5
            for dz in range(1, 4) if m == 0 else range(5):
                sums = add(sums, n, lambda row: wide[dz, n, row])
            keep(sums, n)
        return _

    lax.fori_loop(0, 2, some_tiles, 0)
    last = len(TILES) - 1
    sums = [zero] * 5
    for d in (0, 1):
        sums = add(
            sums, last, lambda row: jnp.where(left, wide[d, last, row], wide[4 - d, last, row])
        )
    keep(sums, last)
    found = []
    for c in range(5):
        orders = [zero, zero, zero]
        for n, (k, first, second) in enumerate(TILES):
            gains[n, c, 8:16, :] = gains[n, c, 0:8, :]
            part = halves(first, second, lambda dy: gains[n, c, dy % 8 : dy % 8 + 8, :])
            orders[k] = orders[k] + part
        two, one, same = orders
        total = same + pltpu.roll(two, 32, 1)
        total = total + pltpu.roll(jnp.where(left, one, 0.0), 16, 1)
        total = total + pltpu.roll(jnp.where(left, 0.0, one), 112, 1)
        found.append(-(total + pltpu.roll(total, 64, 1)))
    return found


def sweep(
    lists, chunks, place, gradients, rate, source, used, faces, face_used, near, halo, fields,
    around, wide, inner, spin, turn, turned, gains,
):
    fill_tables(lists, source, used, faces, face_used)
    collect_sites(chunks, source, used, near)
    shift_sites(near, halo)
    moments(near, halo, fields, spin, turn)
    gather_fields(fields, faces, face_used, around)
    shift_fields(around, wide, inner)
    rates = fluxes(wide, inner, turned, gains)
    rows = [wide[2, 2, 15 + k] for k in range(15)] + rates
    found = jnp.concatenate(rows, axis=0)
    lane = place[1:2, :].astype(jnp.int32) + 32
    hot = jnp.where(iota((128, 512), 0) == lane, 1.0, 0.0).astype(BF16)
    total = jnp.zeros((160, 512), F32)
    for part in split3(found):
        total = total + jnp.dot(part, hot, preferred_element_type=F32)
    here = (iota((8, 512), 0) == place[0:1, :].astype(jnp.int32)) & (place[2:3, :] > 0.0)
    for k in range(20):
        row = jnp.sum(jnp.where(here, total[8 * k : 8 * k + 8], 0.0), axis=0, keepdims=True)
        if k < 15:
            gradients[k : k + 1, :] = row
        else:
            rate[k - 15 : k - 14, :] = row


def sweep_call(lists, chunks, place):
    vmem = pl.BlockSpec(memory_space=pltpu.VMEM)
    smem = pl.BlockSpec(memory_space=pltpu.SMEM)
    return pl.pallas_call(
        sweep,
        out_shape=(jax.ShapeDtypeStruct((15, 512), F32), jax.ShapeDtypeStruct((5, 512), F32)),
        in_specs=[smem, vmem, vmem],
        out_specs=(vmem, vmem),
        scratch_shapes=[
            pltpu.SMEM((28 * 16,), jnp.int32),
            pltpu.SMEM((28,), jnp.int32),
            pltpu.SMEM((56,), jnp.int32),
            pltpu.SMEM((28,), jnp.int32),
            pltpu.VMEM((8, 10, 4, 8, 128), F32),
            pltpu.VMEM((5, 5, 9, 8, 8, 128), F32),
            pltpu.VMEM((512, 512), BF16),
            pltpu.VMEM((4, 240, 128), F32),
            pltpu.VMEM((5, len(TILES), 30, 8, 128), F32),
            pltpu.VMEM((3, 30, 16, 128), F32),
            pltpu.VMEM((9, 16, 128), F32),
            pltpu.VMEM((22, 16, 128), F32),
            pltpu.VMEM((len(TILES), 30, 8, 128), F32),
            pltpu.VMEM((len(TILES), 5, 16, 128), F32),
        ],
        compiler_params=pltpu.CompilerParams(vmem_limit_bytes=48 * 1024 * 1024),
        name="sweep",
    )(lists.reshape(24 * 128), chunks, place)


def body(geom, density, velocity, pressure, block_live, pair_list):
    chunks, place, lists = exchange_call(geom, density, velocity, pressure, block_live, pair_list)
    return sweep_call(lists, chunks, place)


def solution(mesh):
    both = ("region", "group")
    return jax.shard_map(
        body,
        mesh=mesh,
        in_specs=(P(None, both), P(both), P(None, both), P(both), P(both), P(both, None)),
        out_specs=(P(None, both), P(None, both)),
        check_vma=False,
    )
```

```python
import functools

import jax
import jax.numpy as jnp
from jax import lax
from jax.experimental import pallas as pl
from jax.experimental.pallas import tpu as pltpu
from jax.sharding import PartitionSpec as P

BLOCK = 256
LIST = 14
LAYERS = 3
F32 = jnp.float32
BF16 = jnp.bfloat16
ridge_scale = 0.05
gamma = 5.0 / 3.0
HEAD, TAIL, CORNER = 64, 78, 92
MESH = pl.DeviceIdType.MESH


def iota(shape, dim):
    return lax.broadcasted_iota(jnp.int32, shape, dim)


def split3(value):
    high = value.astype(BF16)
    rest = value - high.astype(F32)
    middle = rest.astype(BF16)
    low = (rest - middle.astype(F32)).astype(BF16)
    return high, middle, low


def order_key(heads, index):
    parity = (heads - 2.0 * jnp.floor(heads * 0.5)).astype(jnp.int32)
    return jnp.where((heads >= 0.0) & (index < LIST), parity, 2)


def prepare(values, place):
    lanes = iota((1, 128), 1)
    total = jnp.zeros((40, 128), F32)
    both = jnp.concatenate([values[8:12, 0:128], values[8:12, 0:128]], axis=0).T[0:16]
    kinds = [order_key(values[9:10, 0:128], lanes), order_key(both[:, 1:2], iota((16, 1), 0))]
    here, there = iota((16, 128), 1), iota((16, 128), 0)
    ahead = (kinds[0] < kinds[1]) | ((kinds[0] == kinds[1]) & (here < there))
    ahead = jnp.where(ahead & (here < LIST), 1.0, 0.0)
    rank = jnp.sum(ahead, axis=1, keepdims=True).astype(jnp.int32)
    listed = jnp.where((here == TAIL + rank) & (there < LIST), both[:, 2:3], 0.0)
    listed = jnp.sum(listed, axis=0, keepdims=True)
    for s in range(2):
        count = jnp.sum(jnp.where(kinds[0] == s, 1.0, 0.0), axis=1, keepdims=True)
        listed = listed + jnp.where(lanes == HEAD + s, count, 0.0)
    for s in range(2):
        at = slice(s * BLOCK, (s + 1) * BLOCK)
        corner = values[0:4, at]
        columns = jnp.concatenate([corner, corner], axis=0).T
        cells = []
        for k, count in ((0, 64), (1, 32), (2, 32)):
            smaller = columns[:, k : k + 1] < corner[k : k + 1, :]
            rank = jnp.sum(jnp.where(smaller, 1.0, 0.0), axis=0, keepdims=True)
            cells.append(jnp.floor(rank * (1.0 / count)).astype(jnp.int32))
            low = jnp.min(corner[k : k + 1, :], axis=1, keepdims=True)
            listed = listed + jnp.where(lanes == CORNER + 3 * s + k, low, 0.0)
        lane = cells[0] * 8 + cells[2]
        alive = iota((1, BLOCK), 1).astype(F32) < values[11:12, s : s + 1]
        rows = [corner[0:1], corner[1:2], corner[2:3], jnp.log(values[4:5, at])]
        rows += [values[5 + k : 6 + k, at] for k in range(3)]
        rows += [jnp.log(values[8:9, at]), jnp.where(alive, corner[3:4], 0.0)]
        here = iota((8, BLOCK), 0) == cells[1]
        spread = [jnp.where(here, row, 0.0) for row in rows] + [jnp.zeros((8, BLOCK), F32)]
        for par in range(2):
            target = jnp.where(iota((128, BLOCK), 0) == lane + (par * 64 + s * 32), 1.0, 0.0)
            target = target.astype(BF16)
            for part in split3(jnp.concatenate(spread[par::2], axis=0)):
                total = total + lax.dot_general(
                    part, target, (((1,), (1,)), ((), ())), preferred_element_type=F32
                )
        place[0:1, at] = cells[1].astype(F32)
        place[1:2, at] = (cells[0] * 16 + cells[2] + 8 * s).astype(F32)
        place[2:3, at] = jnp.where(alive, 1.0, 0.0)
    return total + jnp.where(iota((40, 128), 0) == 32, listed, 0.0)


def read_lists(chunks, lists, region, group):
    lanes = iota((24, 128), 1)
    kind = (lanes - CORNER) % 3
    scale = jnp.where(kind == 0, 0.25, 0.125)
    weight = jnp.where(kind == 0, 1024.0, jnp.where(kind == 1, 32.0, 1.0))
    own = chunks[1, group // 4, group % 4, 32:33, :]
    own = jnp.where(lanes[0:1] >= CORNER + 3, pltpu.roll(own, 3, 1), own)
    first = ((region - 1) * 64).astype(F32)
    whole = jnp.zeros((24, 128), jnp.int32)
    for m in range(4):
        rows = chunks[:, :, m, 32, :].reshape(24, 128)
        steps = jnp.floor((rows - own) * scale + 0.5) * weight
        steps = steps + pltpu.roll(steps, 127, 1) + pltpu.roll(steps, 126, 1)
        ids = jnp.where(lanes < TAIL, rows, rows - first)
        rows = jnp.where(lanes < CORNER, ids, steps).astype(jnp.int32)
        rows = jnp.where(lanes == CORNER + 1, region, jnp.where(lanes == CORNER + 2, group, rows))
        whole = jnp.where(lanes // 32 == m, pltpu.roll(rows, (64 + 32 * m) % 128, 1), whole)
    lists[...] = whole


STEPS = (1, -1, 2, -2, 3, -3, 4)


def exchange(
    values, chunks, place, lists,
    z_send, z_recv, x_send, x_recv, r_send, r_recv,
):
    region, group = lax.axis_index("region"), lax.axis_index("group")
    z, x = group // 4, group % 4

    def column(step):
        return (region, z * 4 + (x + step) % 4)

    def plane(step):
        return (region, (z + 8 + step) % 8 * 4 + x)

    def slab(step):
        return ((region + 16 + step) % 16, group)

    partners = [column(k) for k in (1, 2, 3)] + [plane(k) for k in STEPS] + [slab(1), slab(-1)]
    barrier = pltpu.get_barrier_semaphore()
    for partner in partners:
        pl.semaphore_signal(barrier, inc=1, device_id=partner, device_id_type=MESH)
    chunks[1, z, x] = prepare(values, place)
    pl.semaphore_wait(barrier, len(partners))

    def copy(source, target, device, send, recv):
        return pltpu.make_async_remote_copy(
            src_ref=source,
            dst_ref=target,
            send_sem=send,
            recv_sem=recv,
            device_id=device,
            device_id_type=MESH,
        )

    def row(step):
        return (z + 16 + step) % 8

    def along_z(step, arrived=False):
        ref = chunks.at[1, row(-step) if arrived else z, x]
        return copy(ref, ref, plane(step), z_send.at[step % 8], z_recv.at[step % 8])

    def along_x(n, k, arrived=False):
        ref = chunks.at[1, row(n), (x + 4 - k) % 4 if arrived else x]
        return copy(ref, ref, column(k), x_send.at[n % 8, k - 1], x_recv.at[n % 8, k - 1])

    def along_r(step, n, arrived=False):
        side = 0 if step > 0 else 1
        target = chunks.at[2 * side, row(n)]
        source = target if arrived else chunks.at[1, row(n)]
        return copy(source, target, slab(step), r_send.at[side, n % 8], r_recv.at[side, n % 8])

    def spread(n):
        for k in (2, 1, 3):
            along_x(n, k).start()

    def give(n):
        for k in (1, 2, 3):
            along_x(n, k, True).wait_recv()
        for step in (1, -1):
            along_r(step, n).start()

    for step in STEPS:
        along_z(step).start()
    spread(0)
    for step in (-1, 1):
        along_z(-step, True).wait_recv()
        spread(step)
    give(0)
    for far in (2, 3, 4):
        for step in (-far, far) if far < 4 else (4,):
            along_z(-step if far < 4 else 4, True).wait_recv()
            spread(step)
        if far > 2:
            give(2 - far)
            give(far - 2)
    give(-3)
    give(3)
    give(4)
    for n in range(8):
        for step in (1, -1):
            along_r(step, n, True).wait_recv()
    read_lists(chunks, lists, region, group)
    for step in STEPS:
        along_z(step).wait_send()
    for n in range(8):
        for k in (1, 2, 3):
            along_x(n, k).wait_send()
        for step in (1, -1):
            along_r(step, n).wait_send()


def exchange_call(geom, density, velocity, pressure, live, pair):
    vmem = pl.BlockSpec(memory_space=pltpu.VMEM)
    def rows(v, first):
        return jnp.pad(v, ((first, 12 - first - v.shape[0]), (0, 2 * BLOCK - v.shape[1])))

    values = rows(geom, 0) + rows(density[None], 4) + rows(velocity, 5) + rows(pressure[None], 8)
    values = values + (rows(pair.T, 9) + rows(live[None], 11)).astype(F32)
    dma = pltpu.SemaphoreType.DMA
    chunks, place, lists = pl.pallas_call(
        exchange,
        out_shape=(
            jax.ShapeDtypeStruct((LAYERS, 8, 4, 40, 128), F32),
            jax.ShapeDtypeStruct((8, 512), F32),
            jax.ShapeDtypeStruct((24, 128), jnp.int32),
        ),
        in_specs=[vmem],
        out_specs=(vmem, vmem, vmem),
        scratch_shapes=[
            dma((8,)),
            dma((8,)),
            dma((8, 3)),
            dma((8, 3)),
            dma((2, 8)),
            dma((2, 8)),
        ],
        compiler_params=pltpu.CompilerParams(
            collective_id=0, has_side_effects=True, vmem_limit_bytes=16 * 1024 * 1024
        ),
        name="gather_sites",
    )(values)
    return chunks.reshape(LAYERS * 32, 40, 128), place, lists


def direction(step, wanted):
    u = step + 1057
    a, b, c = u >> 10, (u >> 5) & 31, u & 31
    fits = wanted & (u >= 0) & (jnp.maximum(jnp.maximum(a, b), c) <= 2)
    return jnp.where(fits, a * 9 + b * 3 + c, 27)


def fill_tables(lists, source, used, faces, face_used):
    def clear(k, _):
        source[k] = -1
        return _

    lax.fori_loop(0, 27 * 16, clear, 0, unroll=16)

    def clear_way(k, _):
        used[k] = 0
        face_used[k] = 0
        faces[k] = -1
        faces[28 + k] = -1
        return _

    lax.fori_loop(0, 28, clear_way, 0, unroll=14)
    own = (32 + lists[30]) * 32

    def code(block):
        return lists[(block >> 1) * 32 + 28 + 3 * (block & 1)]

    first = lists[own]
    listed_rows = first + lists[own + 1]

    def origin(p):
        listed = p < listed_rows
        odd = jnp.where(p < first, 0, 1)
        tail = jnp.where(listed, lists[own + LIST + p], 64)
        at = (tail >> 1) * 32
        other = tail & 1
        count = jnp.where(listed, jnp.where(other == 0, lists[at], lists[at + 1]), 0)
        start = at + LIST + jnp.where(other == 0, 0, lists[at])
        return listed, odd, at, count, start, code(tail)

    def enter(p, k, at, count, start, place):
        near = k < count
        there = lists[jnp.where(near, start + k, at)]
        near = near & (there >= 0) & (there < 192)
        there = jnp.where(near, there, 0)
        towards = direction(code(there) - place, near)
        source[towards * 16 + p] = there
        used[towards] = 1

    def slot(p, most):
        listed, odd, at, count, start, place = origin(p)
        way = direction(place - lists[own + 28 + 3 * odd], listed)
        faces[odd * 28 + way] = p
        face_used[way] = 1
        for k in range(LIST // 2):
            enter(p, k, at, count, start, place)
        return jnp.maximum(most, count)

    most = lax.fori_loop(0, LIST, slot, 0, unroll=7)

    @pl.when(most > LIST // 2)
    def _more():
        def rest(p, _):
            listed, odd, at, count, start, place = origin(p)
            for k in range(LIST // 2, LIST):
                enter(p, k, at, count, start, place)
            return _

        lax.fori_loop(0, LIST, rest, 0)


def swap(low, high, is_low, width):
    first = jnp.where(is_low, low, pltpu.roll(high, width, 1))
    second = jnp.where(is_low, pltpu.roll(low, 128 - width, 1), high)
    return first, second


def collect_sites(chunks, source, used, near):
    lanes = iota((8, 128), 1)
    group = lanes // 8
    bit = [(group >> k) % 2 == 0 for k in range(4)]
    low_y, low_z, low_x = iota((8, 128), 0) < 4, lanes % 8 < 4, (group % 4) < 2

    def choose(sides, mask, value):
        if len(sides) == 1:
            return value(sides[0])
        return jnp.where(mask, value(2), value(0))

    for kind in range(8):
        xs, ys, zs = [(2, 0) if kind & b else (1,) for b in (4, 2, 1)]
        ways = [(sx * 9 + sy * 3 + sz) for sx in xs for sy in ys for sz in zs]
        any_used = sum(used[way] for way in ways)

        @pl.when(any_used > 0)
        def _present():
            froms = {(way, p): source[way * 16 + p] for way in ways for p in range(LIST)}

            def code(way, p):
                f = froms[way, p]
                return jnp.where(f >= 0, 1 + 2 * (f & 1), 0)

            codes = {}
            for sx in xs:
                codes[sx] = jnp.zeros((8, 128), jnp.int32)
                for p in range(LIST):
                    value = choose(
                        ys,
                        low_y,
                        lambda sy: choose(zs, low_z, lambda sz: code(sx * 9 + sy * 3 + sz, p)),
                    )
                    codes[sx] = jnp.where(group == p, value, codes[sx])

            def tile(p, rows):
                def load(sx, sy, sz):
                    return chunks[jnp.maximum(froms[sx * 9 + sy * 3 + sz, p], 0) >> 1, rows, :]

                return choose(
                    xs,
                    low_x,
                    lambda sx: choose(
                        ys, low_y, lambda sy: choose(zs, low_z, lambda sz: load(sx, sy, sz))
                    ),
                )

            def one_tile(t, _):
                v = [tile(p, pl.ds(t * 8, 8)) for p in range(LIST)]
                v += v[:2]
                for k in (0, 1, 3):
                    step = 1 << k
                    for p in range(16):
                        if not p & step:
                            v[p], v[p + step] = swap(v[p], v[p + step], bit[k], 8 * step)
                for n in range(8):
                    par, x = n // 4, n % 4
                    info = codes[xs[0] if x < 2 else xs[-1]]
                    second = info >= 2
                    low, high = v[8 * par + x], v[8 * par + x + 4]
                    low = jnp.where(second, pltpu.roll(low, 96, 1), low)
                    high = jnp.where(second, high, pltpu.roll(high, 32, 1))
                    out = jnp.where(info > 0, jnp.where(bit[2], low, high), 0.0)
                    near[kind, 2 * t + par, x] = out
                return _

            if kind in (0, 1, 2, 4):
                for t in range(5):
                    one_tile(t, 0)
            else:
                lax.fori_loop(0, 5, one_tile, 0)
            for x in range(4):
                radius = near[kind, 8, x]
                near[kind, 9, x] = radius
                near[kind, 8, x] = jnp.where(radius > 0.0, 1.0, 0.0)

        @pl.when(any_used == 0)
        def _absent():
            near[kind] = jnp.zeros((10, 4, 8, 128), F32)


def shifted(base, outer, z, dz):
    if dz == 0:
        return base
    inside = pltpu.roll(base, (-dz) % 128, 1)
    if dz > 0:
        return jnp.where(z + dz < 8, inside, pltpu.roll(outer, 8 - dz, 1))
    return jnp.where(z + dz >= 0, inside, pltpu.roll(outer, 128 - 8 - dz, 1))


def rim_rows(dy):
    row = iota((8, 128), 0)
    return row < dy if dy > 0 else row >= 8 + dy


def across(dy, edge, middle):
    return middle if dy == 0 else jnp.where(rim_rows(dy), edge, middle)


def shift_sites(near, halo):
    z = iota((8, 128), 1) % 8

    def one_row(row, _):
        for xe in range(8):
            mx, x = (4, xe + 2) if xe < 2 else (0, xe - 2) if xe < 6 else (4, xe - 6)
            mid = near[mx, row, x], near[mx + 1, row, x]
            rim = near[mx + 2, row, x], near[mx + 3, row, x]
            for dz in range(-2, 3):
                middle, edge = shifted(*mid, z, dz), shifted(*rim, z, dz)
                for dy in range(-2, 3):
                    halo[dz + 2, dy + 2, row, xe] = across(dy, edge, middle)
        return _

    lax.fori_loop(0, 9, one_row, 0, unroll=3)


def moments(near, halo, fields, spin, turn):
    def one_plane(x, _):
        xi, yi, zi = [near[0, k, x] for k in range(3)]
        qi = [near[0, 3 + k, x] for k in range(5)]
        alive, radius = near[0, 8, x], near[0, 9, x]
        radius = jnp.where(radius > 0.0, radius, 1.0)
        for k, value in enumerate([xi, yi, zi] + qi + [1.0 / radius]):
            spin[k, 0:8, :] = value
            spin[k, 8:16, :] = value
        sums = [jnp.zeros((8, 128), F32)] * 22
        for dy in range(-2, 3):
            own = [spin[k, -dy % 8 : -dy % 8 + 8, :] for k in range(9)]

            def step(dz, steps, total):
                total = list(total)
                for dx in steps:
                    part = [halo[dz, dy + 2, k, x + dx] for k in range(9)]
                    ox, oy, oz = [part[k] - own[k] for k in range(3)]
                    square = ox * ox + oy * oy + oz * oz
                    scaled = square * lax.rsqrt(jnp.maximum(square, 1e-12)) * own[8]
                    remain = jnp.maximum(1.0 - scaled, 0.0)
                    remain = remain * remain
                    w = remain * remain * (1.0 + 4.0 * scaled) * part[8]
                    wx, wy, wz = w * ox, w * oy, w * oz
                    total[0] = total[0] + w
                    total[1] = total[1] + wx * ox
                    total[2] = total[2] + wy * oy
                    total[3] = total[3] + wz * oz
                    total[4] = total[4] + wx * oy
                    total[5] = total[5] + wx * oz
                    total[6] = total[6] + wy * oz
                    for k in range(5):
                        change = part[3 + k] - own[3 + k]
                        for c, v in enumerate((wx, wy, wz)):
                            total[7 + 3 * k + c] = total[7 + 3 * k + c] + v * change
                return tuple(total)

            total = (jnp.zeros((8, 128), F32),) * 22
            wide = range(5) if abs(dy) < 2 else range(1, 4)
            for dz in range(5):
                total = step(dz, range(5) if dz in (1, 2, 3) else wide, total)
            if dy != 0:
                for k in range(22):
                    turn[k, 0:8, :] = total[k]
                    turn[k, 8:16, :] = total[k]
                total = [turn[k, dy % 8 : dy % 8 + 8, :] for k in range(22)]
            sums = [a + b for a, b in zip(sums, total)]
        omega = sums[0] + (1.0 - alive)
        per = 1.0 / omega
        shift = ridge_scale * radius * radius
        m = [sums[1 + k] * per for k in range(6)]
        m[0], m[1], m[2] = m[0] + shift, m[1] + shift, m[2] + shift
        c = [
            m[1] * m[2] - m[5] * m[5],
            m[0] * m[2] - m[4] * m[4],
            m[0] * m[1] - m[3] * m[3],
            m[4] * m[5] - m[3] * m[2],
            m[3] * m[5] - m[4] * m[1],
            m[3] * m[4] - m[0] * m[5],
        ]
        over = 1.0 / (m[0] * c[0] + m[3] * c[3] + m[4] * c[4])
        b = [v * over for v in c]
        rows = [xi, yi, zi] + qi + [near[0, 9, x]]
        square = per * per
        rows += [v * square for v in b]
        for k in range(5):
            f = [sums[7 + 3 * k + a] * per for a in range(3)]
            rows.append(b[0] * f[0] + b[3] * f[1] + b[4] * f[2])
            rows.append(b[3] * f[0] + b[1] * f[1] + b[5] * f[2])
            rows.append(b[4] * f[0] + b[5] * f[1] + b[2] * f[2])
        at = pl.ds(pl.multiple_of(x * 128, 128), 128)
        for k in range(15):
            pair = jnp.concatenate(rows[2 * k : 2 * k + 2], axis=0)
            for n, part in enumerate(split3(pair)[: 3 if k < 2 else 2]):
                fields[240 * n + 16 * k : 240 * n + 16 * k + 16, at] = part
        return _

    lax.fori_loop(0, 4, one_plane, 0)


def gather_fields(fields, faces, face_used, around):
    lanes = iota((1, 128), 1)
    z = lanes % 8
    sources = iota((128, 128), 0)

    def hot(sy, zs):
        blocks = []
        for x in range(4):
            wanted = jnp.full((1, 128), -1, jnp.int32)
            for sx, xe in ((1, x + 2), (2, x + 6) if x < 2 else (0, x - 2)):
                for s in range(2):
                    p = [faces[s * 28 + sx * 9 + sy * 3 + sz] for sz in zs]
                    p = p[0] if len(p) == 1 else jnp.where(z < 4, p[0], p[1])
                    lane = jnp.where(p >= 0, p * 8 + z, -1)
                    wanted = jnp.where(lanes // 8 == xe * 2 + s, lane, wanted)
            blocks.append(jnp.where(sources == wanted, 1.0, 0.0).astype(BF16))
        return jnp.concatenate(blocks, axis=0)

    def pick(columns):
        found = jnp.dot(
            fields[...], jnp.concatenate(columns, axis=1), preferred_element_type=F32
        )
        first = found[0:32] + found[240:272] + found[480:512]
        return jnp.concatenate([first, found[32:240] + found[272:480]], axis=0)

    low_y = iota((240, 128), 0) % 8 < 4
    found = pick([hot(1, (1,)), hot(1, (2, 0)), hot(0, (1,)), hot(2, (1,))])
    around[0] = found[:, 0:128]
    around[1] = found[:, 128:256]
    around[2] = jnp.where(low_y, found[:, 384:512], found[:, 256:384])
    corner = [face_used[sx * 9 + sy * 3 + sz] for sx in range(3) for sy in (0, 2) for sz in (0, 2)]
    any_corner = sum(corner)

    @pl.when(any_corner > 0)
    def _present():
        found = pick([hot(0, (2, 0)), hot(2, (2, 0))])
        around[3] = jnp.where(low_y, found[:, 128:256], found[:, 0:128])

    @pl.when(any_corner == 0)
    def _absent():
        around[3] = jnp.zeros((240, 128), F32)


HALF = 6
TILES = [(0, -2, -2), (0, -1, -1), (0, 0, 0), (1, -2, -2), (1, -1, -1), (2, -2, -1)]
TILES += [(0, 2, 2), (0, 1, 1), (1, 0, 0), (1, 2, 2), (1, 1, 1), (2, 1, 2), (2, 0, 0)]


def shift_fields(around, wide, inner):
    lanes = iota((8, 128), 1)
    z = lanes % 8
    outer = (lanes < 16) | (lanes >= 112)
    middle = (lanes >= 32) & (lanes < 96)
    left = lanes < 64

    def some_rows(n, _):
        for m in range(3):
            row = n * 3 + m
            at = pl.ds(pl.multiple_of(row * 8, 8), 8)
            parts = [(around[n, at, :], around[n + 1, at, :]) for n in (0, 2)]
            for dz in range(-2, 3):
                orders = []
                for base, beyond in parts:
                    far = shifted(base, beyond, z, dz)
                    half = pltpu.roll(far, 64, 1)
                    orders.append(
                        (far, jnp.where(outer, half, far), jnp.where(middle, far, half))
                    )
                for tile, (k, first, second) in enumerate(TILES):
                    value = across(first, orders[1][k], orders[0][k])
                    if first != second:
                        value = jnp.where(left, value, across(second, orders[1][k], orders[0][k]))
                    wide[dz + 2, tile, row] = value
                if dz == 0:
                    own = orders[0][2]
                    back, on = pltpu.roll(own, 112, 1), pltpu.roll(own, 16, 1)
                    values = pltpu.roll(own, 32, 1), jnp.where(left, back, on), own
                    for k, value in enumerate(values):
                        inner[k, row, 0:8, :] = value
                        inner[k, row, 8:16, :] = value
        return _

    lax.fori_loop(0, 10, some_rows, 0)


def weight(scaled):
    remain = jnp.maximum(1.0 - scaled, 0.0)
    remain = remain * remain
    return remain * remain * (1.0 + 4.0 * scaled)


def side(state, n):
    density, pressure = jnp.exp(state[0]), jnp.exp(state[4])
    v = state[1:4]
    speed = v[0] * n[0] + v[1] * n[1] + v[2] * n[2]
    sound = jnp.exp(0.5 * (state[4] - state[0])) * (gamma**0.5)
    return density, pressure, v[0], v[1], v[2], speed, sound


def face(near, far):
    o = [far(k) - near(k) for k in range(3)]
    square = jnp.maximum(o[0] * o[0] + o[1] * o[1] + o[2] * o[2], 1e-12)
    inverse = lax.rsqrt(square)
    distance = square * inverse
    n = [v * inverse for v in o]
    hi, hj = near(8), far(8)
    live = jnp.minimum(hi, hj) > 0.0
    wi = weight(distance * (1.0 / jnp.where(hi > 0.0, hi, 1.0)))
    wj = weight(distance * (1.0 / jnp.where(hj > 0.0, hj, 1.0)))
    c = [wi * near(9 + k) + wj * far(9 + k) for k in range(6)]
    a = [
        c[0] * o[0] + c[3] * o[1] + c[4] * o[2],
        c[3] * o[0] + c[1] * o[1] + c[5] * o[2],
        c[4] * o[0] + c[5] * o[1] + c[2] * o[2],
    ]
    area = a[0] * a[0] + a[1] * a[1] + a[2] * a[2]
    area = jnp.where(live, jnp.sqrt(area), 0.0)
    left, right = [], []
    for k in range(5):
        gi = near(15 + 3 * k) * o[0] + near(16 + 3 * k) * o[1] + near(17 + 3 * k) * o[2]
        gj = far(15 + 3 * k) * o[0] + far(16 + 3 * k) * o[1] + far(17 + 3 * k) * o[2]
        left.append(near(3 + k) + 0.5 * jnp.tanh(gi))
        right.append(far(3 + k) - 0.5 * jnp.tanh(gj))
    sl, sr = side(left, n), side(right, n)
    slow = jnp.minimum(sl[5] - sl[6], sr[5] - sr[6])
    fast = jnp.maximum(sl[5] + sl[6], sr[5] + sr[6])
    ml, mr = sl[0] * (slow - sl[5]), sr[0] * (fast - sr[5])
    middle = (sr[1] - sl[1] + ml * sl[5] - mr * sr[5]) / (ml - mr)
    from_left = (slow >= 0.0) | (middle >= 0.0)
    density, pressure, v0, v1, v2, speed, _ = [
        jnp.where(from_left, p, q) for p, q in zip(sl, sr)
    ]
    mass, wave = jnp.where(from_left, ml, mr), jnp.where(from_left, slow, fast)
    star = jnp.where(from_left, -slow, fast) > 0.0
    kinetic = 0.5 * (v0 * v0 + v1 * v1 + v2 * v2)
    energy = pressure * (1.0 / (gamma - 1.0)) + density * kinetic
    push = jnp.where(star, wave * mass / (wave - middle), 0.0)
    rest = speed - jnp.where(star, wave, 0.0)
    lift = middle - speed
    flow = density * rest + push
    press = pressure + push * lift
    heat = energy * rest + pressure * speed
    heat = heat + push * (energy / density + lift * (middle + pressure / mass))
    terms = [flow, v0 * flow + press * n[0], v1 * flow + press * n[1], v2 * flow + press * n[2]]
    return [jnp.where(live, t * area, 0.0) for t in terms + [heat]]


def fluxes(wide, inner, turned, gains):
    left = iota((8, 128), 1) < 64
    zero = jnp.zeros((8, 128), F32)

    def halves(first, second, load):
        return load(first) if first == second else jnp.where(left, load(first), load(second))

    def turn(row, _):
        for n, (k, first, second) in enumerate(TILES):
            turned[n, row] = halves(
                first, second, lambda dy: inner[k, row, -dy % 8 : -dy % 8 + 8, :]
            )
        return _

    lax.fori_loop(0, 30, turn, 0, unroll=10)
    def add(sums, n, far):
        return [a + b for a, b in zip(sums, face(lambda row: turned[n, row], far))]

    def keep(sums, n):
        for c, value in enumerate(sums):
            gains[n, c, 0:8, :] = value

    def some_tiles(part, _):
        for m in range(HALF):
            n = part * HALF + m
            sums = [zero] * 5
            for dz in range(1, 4) if m == 0 else range(5):
                sums = add(sums, n, lambda row: wide[dz, n, row])
            keep(sums, n)
        return _

    lax.fori_loop(0, 2, some_tiles, 0)
    last = len(TILES) - 1
    sums = [zero] * 5
    for d in (0, 1):
        sums = add(
            sums, last, lambda row: jnp.where(left, wide[d, last, row], wide[4 - d, last, row])
        )
    keep(sums, last)
    found = []
    for c in range(5):
        orders = [zero, zero, zero]
        for n, (k, first, second) in enumerate(TILES):
            gains[n, c, 8:16, :] = gains[n, c, 0:8, :]
            part = halves(first, second, lambda dy: gains[n, c, dy % 8 : dy % 8 + 8, :])
            orders[k] = orders[k] + part
        two, one, same = orders
        total = same + pltpu.roll(two, 32, 1)
        total = total + pltpu.roll(jnp.where(left, one, 0.0), 16, 1)
        total = total + pltpu.roll(jnp.where(left, 0.0, one), 112, 1)
        found.append(-(total + pltpu.roll(total, 64, 1)))
    return found


def sweep(
    lists, chunks, place, gradients, rate, source, used, faces, face_used, near, halo, fields,
    around, wide, inner, spin, turn, turned, gains,
):
    fill_tables(lists, source, used, faces, face_used)
    collect_sites(chunks, source, used, near)
    shift_sites(near, halo)
    moments(near, halo, fields, spin, turn)
    gather_fields(fields, faces, face_used, around)
    shift_fields(around, wide, inner)
    rates = fluxes(wide, inner, turned, gains)
    rows = [wide[2, 2, 15 + k] for k in range(15)] + rates
    found = jnp.concatenate(rows, axis=0)
    lane = place[1:2, :].astype(jnp.int32) + 32
    hot = jnp.where(iota((128, 512), 0) == lane, 1.0, 0.0).astype(BF16)
    total = jnp.zeros((160, 512), F32)
    for part in split3(found)[:2]:
        total = total + jnp.dot(part, hot, preferred_element_type=F32)
    here = (iota((8, 512), 0) == place[0:1, :].astype(jnp.int32)) & (place[2:3, :] > 0.0)
    for k in range(20):
        row = jnp.sum(jnp.where(here, total[8 * k : 8 * k + 8], 0.0), axis=0, keepdims=True)
        if k < 15:
            gradients[k : k + 1, :] = row
        else:
            rate[k - 15 : k - 14, :] = row


def sweep_call(lists, chunks, place):
    vmem = pl.BlockSpec(memory_space=pltpu.VMEM)
    smem = pl.BlockSpec(memory_space=pltpu.SMEM)
    return pl.pallas_call(
        sweep,
        out_shape=(jax.ShapeDtypeStruct((15, 512), F32), jax.ShapeDtypeStruct((5, 512), F32)),
        in_specs=[smem, vmem, vmem],
        out_specs=(vmem, vmem),
        scratch_shapes=[
            pltpu.SMEM((28 * 16,), jnp.int32),
            pltpu.SMEM((28,), jnp.int32),
            pltpu.SMEM((56,), jnp.int32),
            pltpu.SMEM((28,), jnp.int32),
            pltpu.VMEM((8, 10, 4, 8, 128), F32),
            pltpu.VMEM((5, 5, 9, 8, 8, 128), F32),
            pltpu.VMEM((512, 512), BF16),
            pltpu.VMEM((4, 240, 128), F32),
            pltpu.VMEM((5, len(TILES), 30, 8, 128), F32),
            pltpu.VMEM((3, 30, 16, 128), F32),
            pltpu.VMEM((9, 16, 128), F32),
            pltpu.VMEM((22, 16, 128), F32),
            pltpu.VMEM((len(TILES), 30, 8, 128), F32),
            pltpu.VMEM((len(TILES), 5, 16, 128), F32),
        ],
        compiler_params=pltpu.CompilerParams(vmem_limit_bytes=48 * 1024 * 1024),
        name="sweep",
    )(lists.reshape(24 * 128), chunks, place)


def body(geom, density, velocity, pressure, block_live, pair_list):
    chunks, place, lists = exchange_call(geom, density, velocity, pressure, block_live, pair_list)
    return sweep_call(lists, chunks, place)


def solution(mesh):
    both = ("region", "group")
    return jax.shard_map(
        body,
        mesh=mesh,
        in_specs=(P(None, both), P(both), P(None, both), P(both), P(both), P(both, None)),
        out_specs=(P(None, both), P(None, both)),
        check_vma=False,
    )
```
